32 devices in a mesh: band: 8 (over y, x, core), spec: 4 (over z).
Axes of the slice: x: 2, y: 2, z: 4, core: 2. Of those that a mesh axis runs over, the one named last changes fastest.
Arguments:
- spectra: float32 [1296, 16, 512], P(None, 'band', 'spec'), may hold values from 0.05 to 2
- sea_mask: int32 [16, 512], P('band', 'spec'), may hold values 0 or 1
- wind: float32 [2, 16, 512], P(None, None, ('spec', 'band')), may hold values from -30 to 30
- current: float32 [2, 16, 512], P(None, None, ('spec', 'band')), may hold values from -0.2 to 0.2
Outputs:
- spectra_next: float32 [1296, 16, 512], P(None, 'band', 'spec')
The draws below stay inside these ranges and needn't reach their ends.
All inputs are finite; a program needn't handle non-finite values. No bound on the sum of `sea_mask` on one device may be relied on, other than what follows from the above.
Results may differ from the reference program's by a relative error of at most 0.0003.
Values sent between devices are 32-bit elements; how exact they have to be, the bound alone decides.
No kernel may reach another device: no remote copies, remote signals or barrier semaphores. Data moves between devices by JAX's collectives and lax.ppermute only.
A program may use at most 128 MiB of HBM per device.

```python
import math
import jax
import jax.numpy as jnp
from jax import lax

NF = 36
ND = 36
K = 1296
RY = 2
NY = 16
NX = 512


def place_ends(entries, stream_key, least, high):
    place = [jax.random.randint(jax.random.fold_in(stream_key, axis), (), 0, length) for axis, length in enumerate(entries.shape)]
    widest = entries.shape.index(max(entries.shape))
    neighbour = place[:widest] + [(place[widest] + 1) % entries.shape[widest]] + place[widest + 1:]
    return entries.at[tuple(place)].set(least).at[tuple(neighbour)].set(high)


def shard_levels(rng, shape, pieces, smallest, high):
    loudness, own = 1.0, jax.random.fold_in(rng, 6)
    for dim, parts in pieces:
        heights = jnp.exp(jax.random.uniform(jax.random.fold_in(own, dim), (parts,), jnp.float32, smallest / len(pieces), high / len(pieces)))
        loudness = loudness * jnp.repeat(heights, shape[dim] // parts).reshape([-1 if axis == dim else 1 for axis in range(len(shape))])
    return loudness


def centred(key, dims, spread, most, shards=(), held_as=jnp.bfloat16):
    array = spread * jax.random.normal(key, dims, jnp.float32)
    if shards:
        array = array * shard_levels(key, dims, shards, -0.22, 0.18)
    return jnp.clip(array, -most, most).astype(held_as)


def setup_inputs(seed: int = 0) -> dict:
    streams_of = jax.random.split(jax.random.key(seed), 5)
    spectra = jnp.clip(jnp.exp(math.log(2.0) - 3.6888794 * jax.random.uniform(streams_of[0], (K, NY, NX), jnp.float32) ** shard_levels(streams_of[0], (K, NY, NX), ((1, 8), (2, 4)), -0.2, 0.2)), 0.05, 2.0)
    sea_mask = place_ends((jax.random.randint(streams_of[1], (NY, NX), 0, 10) < 7).astype(jnp.int32), jax.random.fold_in(streams_of[1], 1), 0, 1)
    wind = centred(streams_of[2], (2, NY, NX), 8.0, 30.0, ((2, 32),), jnp.float32)
    current = jnp.clip(jax.random.uniform(streams_of[3], (2, NY, NX), jnp.float32, -0.2, 0.2) * shard_levels(streams_of[3], (2, NY, NX), ((2, 32),), -0.4, 0.0), -0.2, 0.2)
    return dict(spectra=spectra, sea_mask=sea_mask, wind=wind, current=current)


LAT_SOUTH = 30.0
LAT_NORTH = 55.0
SPEED_TOP = 0.35
FREQ_STEP = 1.1
TURNING = 1.5
GROWTH = 0.05
WIND_COUPLING = 0.04


def latitude(position, total_rows):
    return (LAT_SOUTH + (LAT_NORTH - LAT_SOUTH) * position / total_rows) * (math.pi / 180.0)


def wrap_columns(values):
    return jnp.concatenate([values[..., -2:], values, values[..., :2]], axis=-1)


def face_flux(behind, center, ahead, beyond, courant):
    forward = courant >= 0.0
    upwind = jnp.where(forward, behind, beyond)
    source_cell = jnp.where(forward, center, ahead)
    target_cell = jnp.where(forward, ahead, center)
    magnitude = jnp.abs(courant)
    face_value = 0.5 * (source_cell + target_cell) - 0.5 * magnitude * (target_cell - source_cell) - (1.0 - courant * courant) / 6.0 * (target_cell - 2.0 * source_cell + upwind)
    return courant * face_value


def axis_fluxes(extended, cell_courant, along_axis):
    cell_count = extended.shape[along_axis] - 4

    def take_slice(values, offset):
        return lax.slice_in_dim(values, offset, offset + cell_count + 1, axis=along_axis)

    face_courant = 0.5 * (take_slice(cell_courant, 1) + take_slice(cell_courant, 2))
    return face_flux(take_slice(extended, 0), take_slice(extended, 1), take_slice(extended, 2), take_slice(extended, 3), face_courant)


def component_tables(comp_index):
    freq_index = (comp_index // ND).astype(jnp.float32)
    direction = (comp_index % ND).astype(jnp.float32) * (2.0 * math.pi / ND)
    group_speed = SPEED_TOP * jnp.power(jnp.float32(FREQ_STEP), -freq_index)
    return group_speed, jnp.cos(direction), jnp.sin(direction)


def propagate(spec_wide, spec_tall, current_wide, current_tall, comp_index, row_start, total_rows):
    group_speed, cos_dir, sin_dir = component_tables(comp_index)
    row_count = spec_wide.shape[1]
    cell_rows = (row_start + jnp.arange(row_count, dtype=jnp.int32)).astype(jnp.float32) + 0.5
    face_rows = (row_start + jnp.arange(row_count + 1, dtype=jnp.int32)).astype(jnp.float32)
    cell_cos = jnp.cos(latitude(cell_rows, total_rows))
    face_cos = jnp.cos(latitude(face_rows, total_rows))
    east_speed = (group_speed * cos_dir)[:, None, None] / cell_cos[None, :, None] + current_wide[0][None]
    north_speed = (group_speed * sin_dir)[:, None, None] + current_tall[1][None]
    east_flux = axis_fluxes(spec_wide, east_speed, 2)
    north_flux = axis_fluxes(spec_tall, north_speed, 1) * face_cos[None, :, None]
    center_cells = spec_tall[:, 2:-2, :]
    return center_cells - (east_flux[:, :, 1:] - east_flux[:, :, :-1]) - (north_flux[:, 1:, :] - north_flux[:, :-1, :]) / cell_cos[None, :, None]


def point_step(propagated, wind_rows, sea_rows, row_start, total_rows):
    row_count = propagated.shape[2]
    freq_index = jnp.arange(NF, dtype=jnp.int32).astype(jnp.float32)
    direction = jnp.arange(ND, dtype=jnp.int32).astype(jnp.float32) * (2.0 * math.pi / ND)
    group_speed = SPEED_TOP * jnp.power(jnp.float32(FREQ_STEP), -freq_index)
    cell_rows = (row_start + jnp.arange(row_count, dtype=jnp.int32)).astype(jnp.float32) + 0.5
    tangent = jnp.tan(latitude(cell_rows, total_rows))
    turn_rate = -TURNING * group_speed[:, None, None] * jnp.cos(direction)[None, :, None] * tangent[None, None, :]
    turn_wide = jnp.concatenate([turn_rate[:, -2:], turn_rate, turn_rate[:, :2]], axis=1)[..., None]
    spec_wide = jnp.concatenate([propagated[:, -2:], propagated, propagated[:, :2]], axis=1)
    turn_flux = axis_fluxes(spec_wide, turn_wide, 1)
    turned = propagated - (turn_flux[:, 1:] - turn_flux[:, :-1])
    wind_along = wind_rows[0][None] * jnp.cos(direction)[:, None, None] + wind_rows[1][None] * jnp.sin(direction)[:, None, None]
    coupling = WIND_COUPLING * jnp.power(jnp.float32(FREQ_STEP), freq_index)
    growth = GROWTH * jnp.maximum(wind_along[None] * coupling[:, None, None, None] - 1.0, 0.0)
    freq_weight = (freq_index + 1.0) / NF
    steepness = jnp.sum(freq_weight[:, None, None, None] * turned * turned, axis=(0, 1)) * (2.0 / (NF * ND))
    damping = 1.0 + freq_weight[:, None, None, None] * steepness[None, None]
    return sea_rows[None, None] * turned * (1.0 + growth) / damping


def reference(spectra, sea_mask, wind, current):
    comp_count, total_rows, total_cols = spectra.shape
    sea_float = sea_mask.astype(jnp.float32)
    current_wide = wrap_columns(current)
    current_tall = jnp.pad(current, ((0, 0), (2, 2), (0, 0)))

    def prop_block(freq_step, done):
        start_comp = (freq_step * ND).astype(jnp.int32)
        block_spec = lax.dynamic_slice_in_dim(spectra, start_comp, ND, 0) * sea_float[None]
        comp_index = start_comp + jnp.arange(ND, dtype=jnp.int32)
        spec_wide = wrap_columns(block_spec)
        spec_tall = jnp.pad(block_spec, ((0, 0), (2, 2), (0, 0)))
        result = propagate(spec_wide, spec_tall, current_wide, current_tall, comp_index, 0, total_rows)
        return lax.dynamic_update_slice_in_dim(done, result, start_comp, 0)

    propagated = lax.fori_loop(0, NF, prop_block, jnp.zeros_like(spectra))

    def point_block(row_step, done):
        start_row = (row_step * RY).astype(jnp.int32)
        piece_spec = lax.dynamic_slice_in_dim(propagated, start_row, RY, 1).reshape(NF, ND, RY, total_cols)
        wind_rows = lax.dynamic_slice_in_dim(wind, start_row, RY, 1)
        sea_rows = lax.dynamic_slice_in_dim(sea_float, start_row, RY, 0)
        result = point_step(piece_spec, wind_rows, sea_rows, start_row, total_rows).reshape(comp_count, RY, total_cols)
        return lax.dynamic_update_slice_in_dim(done, result, start_row, 1)

    return lax.fori_loop(0, total_rows // RY, point_block, jnp.zeros_like(spectra))
```

```python
import functools
import math

import jax
import jax.numpy as jnp
import numpy as np
from jax import lax
from jax.experimental import pallas as pl
from jax.experimental.pallas import tpu as pltpu
from jax.sharding import PartitionSpec as P

NF = 36
ND = 36
HALF = ND // 2
LAT_SOUTH = 30.0
LAT_NORTH = 55.0
SPEED_TOP = 0.35
FREQ_STEP = 1.1
TURNING = 1.5
GROWTH = 0.05
WIND_COUPLING = 0.04

GF = 4
GROUPS = NF // GF
GROUP_ROWS = GF * ND * 2
DIRECT_GROUPS = 5
LANES = 128
ROWS = NF * ND * 2
WIDE = -(-(ROWS + 2) // LANES) * LANES

COS = [math.cos(2.0 * math.pi * d / ND) for d in range(HALF + 1)]
SIN = [math.sin(2.0 * math.pi * d / ND) for d in range(HALF + 1)]

(
    CUR_A,
    CUR_M,
    CUR_B,
    CX_A,
    CX_B,
    W0_A,
    W0_B,
    W1_A,
    W1_B,
    SEA_A,
    SEA_B,
    SEA_A1,
    SEA_A2,
    SEA_B1,
    SEA_B2,
    TAU,
    ICOS_A,
    ICOS_B,
    KAP_A,
    MU_A,
    MU_B,
    KAP_B,
    TAN_A,
    TAN_B,
    ICOS_0,
    ICOS_1,
) = range(26)
PAR_ROWS = 32


def flux(lo2, lo1, hi1, hi2, c):
    forward = c >= 0.0
    source = jnp.where(forward, lo1, hi1)
    upwind = jnp.where(forward, lo2, hi2)
    both = lo1 + hi1
    bend = both - 3.0 * source + upwind
    w = (1.0 / 6.0) - (c * c) * (1.0 / 6.0)
    return c * (0.5 * (both - c * (hi1 - lo1)) - w * bend)


def group_speed():
    k = lax.broadcasted_iota(jnp.int32, (8, LANES), 0)
    speed = jnp.zeros((8, LANES), jnp.float32)
    for i in range(GF):
        for h in range(2):
            value = SPEED_TOP * FREQ_STEP**-i * (1.0 - 2.0 * h)
            speed = jnp.where(k == 2 * i + h, value, speed)
    return speed


def freq_weight():
    k = lax.broadcasted_iota(jnp.int32, (8, LANES), 0)
    weight = jnp.zeros((8, LANES), jnp.float32)
    for i in range(GF):
        weight = jnp.where(lax.div(k, 2) == i, (i + 1.0) / NF, weight)
    return weight


def swap_halves(v):
    k = lax.broadcasted_iota(jnp.int32, (8, LANES), 0)
    return jnp.where(lax.rem(k, 2) == 0, pltpu.roll(v, 7, 0), pltpu.roll(v, 1, 0))


def wide_row(par, index):
    return jnp.broadcast_to(par[index : index + 1, :], (8, LANES))


def pack_kernel(bands, wind, current, sea, out, line):
    me = lax.axis_index("band")
    rows, strip = wind.shape[1], wind.shape[2]

    def placed(ref, part):
        empty = jnp.zeros((rows, LANES - strip), jnp.float32)
        return pltpu.roll(jnp.concatenate([ref[part], empty], axis=1), me * strip, 1)

    empty = jnp.zeros((8, LANES), jnp.float32)
    line[0, 0:8, :] = empty
    line[0, 8 + rows : 16 + rows, :] = empty
    line[0, 8 : 8 + rows, :] = placed(current, 1)
    line[1, 8 : 8 + rows, :] = placed(current, 0)
    line[2, 8 : 8 + rows, :] = placed(wind, 0)
    line[3, 8 : 8 + rows, :] = placed(wind, 1)
    seas = sea[...].astype(jnp.float32)
    for t in range(bands):
        at = 8 + 2 * t
        out[t, 0:4, :] = line[0, at - 1 : at + 3, :]
        for part in range(1, 4):
            out[t, 2 + 2 * part : 4 + 2 * part, :] = line[part, at : at + 2, :]
        out[t, 10:12, :] = seas
        out[t, 12:16, :] = jnp.zeros((4, LANES), jnp.float32)


def edge_kernel(bands, geometry, relaid, spectra, sea, par, west, east, line):
    me = lax.axis_index("band")
    odd = lax.rem(me, 2)
    is_even = odd == 0
    forcing = relaid[0]
    for source in range(1, bands):
        forcing = forcing + relaid[source]
    has_south = jnp.where(me > 0, 1.0, 0.0)
    has_north = jnp.where(me < bands - 1, 1.0, 0.0)
    sea_south = relaid[jnp.maximum(me - 1, 0)][10:12] * has_south
    sea_north = relaid[jnp.minimum(me + 1, bands - 1)][10:12] * has_north
    seas = sea[...].astype(jnp.float32)

    def pick(low, high):
        return jnp.where(is_even, low, high)

    def put(index, value):
        par[index : index + 1, :] = jnp.broadcast_to(value, (1, LANES))

    tau = jnp.where(is_even, 1.0, -1.0)
    north = [forcing[i : i + 1] for i in range(4)]
    face = [0.5 * (north[i] + north[i + 1]) for i in range(3)]
    put(CUR_A, tau * pick(face[0], face[2]))
    put(CUR_M, tau * face[1])
    put(CUR_B, tau * pick(face[2], face[0]))
    lane = lax.broadcasted_iota(jnp.int32, (1, LANES), 1)
    inside = jnp.where(lane == 0, 0.0, 1.0)
    east_speed = [forcing[4:5], forcing[5:6]]
    shifted = [0.5 * inside * (v + pltpu.roll(v, 1, 1)) for v in east_speed]
    put(CX_A, pick(shifted[0], shifted[1]))
    put(CX_B, pick(shifted[1], shifted[0]))
    put(W0_A, pick(forcing[6:7], forcing[7:8]))
    put(W0_B, pick(forcing[7:8], forcing[6:7]))
    put(W1_A, pick(forcing[8:9], forcing[9:10]))
    put(W1_B, pick(forcing[9:10], forcing[8:9]))
    put(SEA_A, pick(seas[0:1], seas[1:2]))
    put(SEA_B, pick(seas[1:2], seas[0:1]))
    put(SEA_A1, pick(sea_south[1:2], sea_north[0:1]))
    put(SEA_A2, pick(sea_south[0:1], sea_north[1:2]))
    put(SEA_B1, pick(sea_north[0:1], sea_south[1:2]))
    put(SEA_B2, pick(sea_north[1:2], sea_south[0:1]))
    put(TAU, tau)
    icos = [geometry[me, 0], geometry[me, 1]]
    put(ICOS_A, inside * pick(icos[0], icos[1]))
    put(ICOS_B, inside * pick(icos[1], icos[0]))
    put(KAP_A, geometry[me, 2])
    put(MU_A, geometry[me, 3])
    put(MU_B, geometry[me, 4])
    put(KAP_B, geometry[me, 5])
    put(TAN_A, geometry[me, 6])
    put(TAN_B, geometry[me, 7])
    put(ICOS_0, icos[0])
    put(ICOS_1, icos[1])
    par[26:32, :] = jnp.zeros((6, LANES), jnp.float32)

    sub = lax.broadcasted_iota(jnp.int32, (LANES, LANES), 0)
    both = jnp.where(
        lax.rem(sub, 2) == 0,
        jnp.broadcast_to(seas[0:1], (LANES, LANES)),
        jnp.broadcast_to(seas[1:2], (LANES, LANES)),
    )
    full = ROWS // LANES
    for block in range(WIDE // LANES):
        at = block * LANES
        if block < full:
            cells = spectra[at : at + LANES, :] * both
        else:
            left = ROWS - at
            line[...] = jnp.zeros((LANES, LANES), jnp.float32)
            line[0:left, :] = spectra[at : at + left, :] * both[0:left]
            line[left : left + 2, :] = forcing[4:6]
            cells = line[...]
        turned = cells.T
        west[:, at : at + LANES] = turned[0:2]
        east[:, at : at + LANES] = turned[LANES - 2 : LANES]


def base_kernel(table, par, spectra, beyond, west, east, from_west, from_east, base, tall, fix):
    odd = lax.rem(lax.axis_index("band"), 2)
    lane = lax.broadcasted_iota(jnp.int32, (1, WIDE), 1)
    even_row = lax.rem(lane, 2) == 0
    speed = table[0:1] * par[ICOS_0 : ICOS_0 + 1, 0:1] + table[1:2] * par[ICOS_1 : ICOS_1 + 1, 0:1]

    def column(ref, row):
        cells = ref[row : row + 1, :]
        drift = jnp.where(even_row, cells[:, ROWS : ROWS + 1], cells[:, ROWS + 1 : ROWS + 2])
        return cells, drift

    xm2, _ = column(from_west, 0)
    xm1, dm1 = column(from_west, 1)
    x0, d0 = column(west, 0)
    x1, d1 = column(west, 1)
    y2, d2 = column(east, 0)
    y1, dy1 = column(east, 1)
    z0, dz0 = column(from_east, 0)
    z1, _ = column(from_east, 1)
    first = flux(xm2, xm1, x0, x1, speed + 0.5 * (dm1 + d0))
    last = flux(y2, y1, z0, z1, speed + 0.5 * (dy1 + dz0))
    c = speed + 0.5 * (d0 + d1)
    second = jnp.where(c >= 0.0, -c * (1.0 - c * c) * (1.0 / 6.0), 0.0) * (xm1 - y1)
    c = speed + 0.5 * (d2 + dy1)
    before = jnp.where(c >= 0.0, 0.0, -c * (1.0 - c * c) * (1.0 / 6.0)) * (z0 - x0)
    tall[...] = jnp.zeros((LANES, WIDE), jnp.float32)
    tall[0:1, :] = first - second
    tall[1:2, :] = second
    tall[LANES - 2 : LANES - 1, :] = -before
    tall[LANES - 1 : LANES, :] = before - last
    for block in range(WIDE // LANES):
        at = block * LANES
        fix[at : at + LANES, :] = tall[:, at : at + LANES].T

    sea_a, sea_b = wide_row(par, SEA_A), wide_row(par, SEA_B)
    sea_b1, sea_b2 = wide_row(par, SEA_B1), wide_row(par, SEA_B2)
    cur_a, cur_m, cur_b = wide_row(par, CUR_A), wide_row(par, CUR_M), wide_row(par, CUR_B)
    cx_a, cx_b = wide_row(par, CX_A), wide_row(par, CX_B)
    kap_a, mu_a = wide_row(par, KAP_A), wide_row(par, MU_A)
    mu_b, kap_b = wide_row(par, MU_B), wide_row(par, KAP_B)
    tau = wide_row(par, TAU)
    icos_a, icos_b = wide_row(par, ICOS_A), wide_row(par, ICOS_B)

    def along_east(x, speed_x, current_x, cosine):
        crossing = flux(
            pltpu.roll(x, 2, 1),
            pltpu.roll(x, 1, 1),
            x,
            pltpu.roll(x, LANES - 1, 1),
            speed_x * cosine + current_x,
        )
        return crossing - pltpu.roll(crossing, LANES - 1, 1)

    def one_group(g, speeds):
        start = g * GROUP_ROWS
        north = speeds * tau
        east_a, east_b = speeds * icos_a, speeds * icos_b
        for d in range(HALF):
            row_a = pl.ds(start + 2 * d + odd, 8, stride=ND)
            row_b = pl.ds(start + 2 * d + 1 - odd, 8, stride=ND)
            a = spectra[row_a, :] * sea_a
            b = spectra[row_b, :] * sea_b
            b1 = beyond[row_a, :] * sea_b1
            b2 = beyond[row_b, :] * sea_b2
            c = north * SIN[d] + cur_a
            w = (1.0 / 6.0) - (c * c) * (1.0 / 6.0)
            flux_a = c * (0.5 * (a - c * a) - w * jnp.where(c >= 0.0, a, b - 2.0 * a))
            flux_m = flux(0.0, a, b, b1, north * SIN[d] + cur_m)
            flux_b = flux(a, b, b1, b2, north * SIN[d] + cur_b)
            to_a = along_east(a, east_a, cx_a, COS[d]) + fix[row_a, :]
            to_b = along_east(b, east_b, cx_b, COS[d]) + fix[row_b, :]
            at = pl.multiple_of(g * (HALF * 16) + d * 16, 8)
            base[pl.ds(at, 8), :] = a + to_a + kap_a * flux_a - mu_a * flux_m
            base[pl.ds(at + 8, 8), :] = b + to_b + mu_b * flux_m - kap_b * flux_b
        return speeds * FREQ_STEP**-GF

    lax.fori_loop(0, GROUPS, one_group, group_speed())


def turn(cells, rate):
    after = [swap_halves(cells[0]), swap_halves(cells[1])]
    lower = swap_halves(cells[HALF - 1])
    ring = [lower] + cells + after
    fluxes = []
    for d in range(HALF):
        mean = 0.5 * (COS[d] + COS[d + 1])
        fluxes.append(flux(ring[d], ring[d + 1], ring[d + 2], ring[d + 3], rate * mean))
    last = swap_halves(fluxes[HALF - 1])
    return [cells[d] - (fluxes[d] - (fluxes[d - 1] if d else last)) for d in range(HALF)]


def finish_groups(first, count, par, base, ahead, turned, odd, total):
    sea_a1, sea_a2 = wide_row(par, SEA_A1), wide_row(par, SEA_A2)
    cur_a, cur_m = wide_row(par, CUR_A), wide_row(par, CUR_M)
    kap_a, mu_a, mu_b = wide_row(par, KAP_A), wide_row(par, MU_A), wide_row(par, MU_B)
    tau = wide_row(par, TAU)
    tan_a, tan_b = wide_row(par, TAN_A), wide_row(par, TAN_B)

    def one_group(g, carry):
        speeds, weight, sum_a, sum_b = carry
        start = g * GROUP_ROWS
        north = speeds * tau
        cells_a, cells_b = [], []
        for d in range(HALF):
            n1 = ahead[pl.ds(start + 2 * d + 1 - odd, 8, stride=ND), :] * sea_a1
            n2 = ahead[pl.ds(start + 2 * d + odd, 8, stride=ND), :] * sea_a2
            c = north * SIN[d] + cur_a
            w = (1.0 / 6.0) - (c * c) * (1.0 / 6.0)
            flux_a = c * (0.5 * (n1 + c * n1) - w * jnp.where(c >= 0.0, n2 - 2.0 * n1, n1))
            c = north * SIN[d] + cur_m
            w = (c * c) * (1.0 / 6.0) - (1.0 / 6.0)
            flux_m = jnp.where(c >= 0.0, c * w, 0.0) * n1
            at = pl.multiple_of(g * (HALF * 16) + d * 16, 8)
            cells_a.append(base[pl.ds(at, 8), :] + kap_a * flux_a - mu_a * flux_m)
            cells_b.append(base[pl.ds(at + 8, 8), :] + mu_b * flux_m)
        square_a = square_b = 0.0
        for d, v in enumerate(turn(cells_a, speeds * tan_a)):
            at = pl.multiple_of(g * (HALF * 16) + d * 16, 8)
            turned[pl.ds(at, 8), :] = v
            square_a = square_a + v * v
        for d, v in enumerate(turn(cells_b, speeds * tan_b)):
            at = pl.multiple_of(g * (HALF * 16) + d * 16 + 8, 8)
            turned[pl.ds(at, 8), :] = v
            square_b = square_b + v * v
        return (
            speeds * FREQ_STEP**-GF,
            weight + GF / NF,
            sum_a + weight * square_a,
            sum_b + weight * square_b,
        )

    speeds = group_speed() * FREQ_STEP ** -(GF * first)
    weight = freq_weight() + GF * first / NF
    carry = (speeds, weight, total[0:8, :], total[8:16, :])
    return lax.fori_loop(0, count, one_group, carry)[2:]


def fetch(bands, first, count, straight, split, ahead, sem):
    me = lax.axis_index("band")
    middle = jnp.logical_or(me == bands // 2 - 1, me == bands // 2)
    rows = count * GROUP_ROWS

    @pl.when(middle)
    def _():
        copy = pltpu.make_async_copy(split, ahead, sem)
        copy.start()
        copy.wait()

    @pl.when(jnp.logical_not(middle))
    def _():
        copy = pltpu.make_async_copy(straight.at[pl.ds(first * GROUP_ROWS, rows)], ahead, sem)
        copy.start()
        copy.wait()


def first_kernel(bands, par, base, straight, split, turned, total, ahead, sem):
    odd = lax.rem(lax.axis_index("band"), 2)
    fetch(bands, 0, DIRECT_GROUPS, straight, split, ahead, sem)
    total[...] = jnp.zeros((16, LANES), jnp.float32)
    sums = finish_groups(0, DIRECT_GROUPS, par, base, ahead, turned, odd, total)
    total[0:8, :] = sums[0]
    total[8:16, :] = sums[1]


def last_kernel(bands, par, base, straight, split, done, total, out, ahead, turned, sem):
    odd = lax.rem(lax.axis_index("band"), 2)
    later = GROUPS - DIRECT_GROUPS
    fetch(bands, DIRECT_GROUPS, later, straight, split, ahead, sem)
    sums = finish_groups(DIRECT_GROUPS, later, par, base, ahead, turned, odd, total)
    scale = 2.0 / (NF * ND)
    steep_a = jnp.sum(sums[0], axis=0, keepdims=True) * scale
    steep_b = jnp.sum(sums[1], axis=0, keepdims=True) * scale
    sea_a, sea_b = wide_row(par, SEA_A), wide_row(par, SEA_B)
    w0_a, w0_b = wide_row(par, W0_A), wide_row(par, W0_B)
    w1_a, w1_b = wide_row(par, W1_A), wide_row(par, W1_B)

    def one_group(first, ref, g, carry):
        coupling, weight = carry
        start = (first + g) * GROUP_ROWS
        gain_a = sea_a / (1.0 + weight * steep_a)
        gain_b = sea_b / (1.0 + weight * steep_b)
        wa0, wa1 = w0_a * coupling, w1_a * coupling
        wb0, wb1 = w0_b * coupling, w1_b * coupling
        for d in range(HALF):
            at = pl.multiple_of(g * (HALF * 16) + d * 16, 8)
            growth_a = jnp.maximum(wa0 * COS[d] + wa1 * SIN[d] + (1.0 - GROWTH), 1.0)
            growth_b = jnp.maximum(wb0 * COS[d] + wb1 * SIN[d] + (1.0 - GROWTH), 1.0)
            out[pl.ds(start + 2 * d + odd, 8, stride=ND), :] = (
                ref[pl.ds(at, 8), :] * gain_a * growth_a
            )
            out[pl.ds(start + 2 * d + 1 - odd, 8, stride=ND), :] = (
                ref[pl.ds(at + 8, 8), :] * gain_b * growth_b
            )
        return coupling * FREQ_STEP**GF, weight + GF / NF

    k = lax.broadcasted_iota(jnp.int32, (8, LANES), 0)
    coupling = jnp.zeros((8, LANES), jnp.float32)
    for i in range(GF):
        for h in range(2):
            value = GROWTH * WIND_COUPLING * FREQ_STEP**i * (1.0 - 2.0 * h)
            coupling = jnp.where(k == 2 * i + h, value, coupling)
    carry = (coupling, freq_weight())
    carry = lax.fori_loop(0, DIRECT_GROUPS, functools.partial(one_group, 0, done), carry)
    lax.fori_loop(0, later, functools.partial(one_group, DIRECT_GROUPS, turned), carry)


def geometry_table(bands):
    total = 2 * bands

    def angle(position):
        return (LAT_SOUTH + (LAT_NORTH - LAT_SOUTH) * position / total) * (math.pi / 180.0)

    table = np.zeros((bands, 8), np.float32)
    for b in range(bands):
        cells = [angle(2 * b + 0.5), angle(2 * b + 1.5)]
        faces = [angle(2 * b), angle(2 * b + 1), angle(2 * b + 2)]
        icos = [1.0 / math.cos(v) for v in cells]
        near, far = (0, 1) if b % 2 == 0 else (1, 0)
        face_a, face_b = (faces[0], faces[2]) if b % 2 == 0 else (faces[2], faces[0])
        table[b] = [
            icos[0],
            icos[1],
            math.cos(face_a) * icos[near],
            math.cos(faces[1]) * icos[near],
            math.cos(faces[1]) * icos[far],
            math.cos(face_b) * icos[far],
            -TURNING * math.tan(cells[near]),
            -TURNING * math.tan(cells[far]),
        ]
    return table


def speed_table():
    table = np.zeros((2, WIDE), np.float32)
    for k in range(NF * ND):
        value = SPEED_TOP * FREQ_STEP ** -(k // ND) * math.cos(2.0 * math.pi * (k % ND) / ND)
        table[0, 2 * k] = value
        table[1, 2 * k + 1] = value
    return table


VMEM = pl.BlockSpec(memory_space=pltpu.VMEM)
SMEM = pl.BlockSpec(memory_space=pltpu.SMEM)
ANY = pl.BlockSpec(memory_space=pl.ANY)
PARAMS = pltpu.CompilerParams(vmem_limit_bytes=40 * 1024 * 1024)


def call(kernel, name, operands, specs, shapes, scratch, micros):
    outs = [jax.ShapeDtypeStruct(s, jnp.float32) for s in shapes]
    return pl.pallas_call(
        kernel,
        name=name,
        out_shape=outs,
        in_specs=specs,
        out_specs=[VMEM] * len(outs),
        scratch_shapes=scratch,
        compiler_params=PARAMS,
        cost_estimate=pl.CostEstimate(
            flops=0, bytes_accessed=int(micros * 3.0e6), transcendentals=0
        ),
    )(*operands)


def per_device(bands, spec_count, spectra, sea_mask, wind, current):
    comp_count, row_count, col_count = spectra.shape
    cells = spectra.reshape(comp_count * row_count, col_count)
    middle = bands // 2 - 1
    direct_rows = DIRECT_GROUPS * GROUP_ROWS

    side_pairs = [(b, b + 1) for b in range(1, bands - 1, 2) if b != middle]
    both_ways = side_pairs + [(t, s) for s, t in side_pairs]
    straight = lax.ppermute(cells, "band", both_ways)
    relay = lax.ppermute(
        cells[direct_rows:], "band", [(middle, bands - 1), (middle + 1, 0)]
    )
    direct = lax.ppermute(
        cells[:direct_rows], "band", [(middle, middle + 1), (middle + 1, middle)]
    )
    relayed = lax.ppermute(relay, "band", [(bands - 1, middle + 1), (0, middle)])

    pairs = [(b, b + 1) for b in range(0, bands, 2)]
    beyond = lax.ppermute(cells, "band", pairs + [(t, s) for s, t in pairs])

    (packed,) = call(
        functools.partial(pack_kernel, bands),
        "pack_forcing",
        (wind, current, sea_mask),
        [VMEM] * 3,
        [(bands, 16, LANES)],
        [pltpu.VMEM((4, 16 + wind.shape[1], LANES), jnp.float32)],
        0.5,
    )
    relaid = lax.all_to_all(packed, "band", split_axis=0, concat_axis=0, tiled=True)
    par, west, east = call(
        functools.partial(edge_kernel, bands),
        "edges",
        (jnp.asarray(geometry_table(bands)), relaid, cells, sea_mask),
        [SMEM, VMEM, VMEM, VMEM],
        [(PAR_ROWS, LANES), (2, WIDE), (2, WIDE)],
        [pltpu.VMEM((LANES, LANES), jnp.float32)],
        1.5,
    )
    ring = [(s, (s + 1) % spec_count) for s in range(spec_count)]
    from_west = lax.ppermute(east, "spec", ring)
    from_east = lax.ppermute(west, "spec", [(t, s) for s, t in ring])
    (base,) = call(
        base_kernel,
        "base",
        (jnp.asarray(speed_table()), par, cells, beyond, west, east, from_west, from_east),
        [VMEM] * 8,
        [(ROWS, LANES)],
        [pltpu.VMEM((LANES, WIDE), jnp.float32), pltpu.VMEM((WIDE, LANES), jnp.float32)],
        6.0,
    )
    later_rows = ROWS - direct_rows
    turned, total = call(
        functools.partial(first_kernel, bands),
        "first_groups",
        (par, base[:direct_rows], straight, direct),
        [VMEM, VMEM, ANY, ANY],
        [(direct_rows, LANES), (16, LANES)],
        [pltpu.VMEM((direct_rows, LANES), jnp.float32), pltpu.SemaphoreType.DMA],
        2.0,
    )
    (out,) = call(
        functools.partial(last_kernel, bands),
        "last_groups",
        (par, base[direct_rows:], straight, relayed, turned, total),
        [VMEM, VMEM, ANY, ANY, VMEM, VMEM],
        [(ROWS, LANES)],
        [
            pltpu.VMEM((later_rows, LANES), jnp.float32),
            pltpu.VMEM((later_rows, LANES), jnp.float32),
            pltpu.SemaphoreType.DMA,
        ],
        3.0,
    )
    return out.reshape(comp_count, row_count, col_count)


def solution(mesh):
    placed = (
        P(None, "band", "spec"),
        P("band", "spec"),
        P(None, None, ("spec", "band")),
        P(None, None, ("spec", "band")),
    )
    return jax.shard_map(
        functools.partial(per_device, mesh.shape["band"], mesh.shape["spec"]),
        mesh=mesh,
        in_specs=placed,
        out_specs=P(None, "band", "spec"),
        check_vma=False,
    )
```

```python
import functools
import math

import jax
import jax.numpy as jnp
import numpy as np
from jax import lax
from jax.experimental import pallas as pl
from jax.experimental.pallas import tpu as pltpu
from jax.sharding import PartitionSpec as P

NF = 36
ND = 36
HALF = ND // 2
LAT_SOUTH = 30.0
LAT_NORTH = 55.0
SPEED_TOP = 0.35
FREQ_STEP = 1.1
TURNING = 1.5
GROWTH = 0.05
WIND_COUPLING = 0.04

GF = 4
GROUPS = NF // GF
GROUP_ROWS = GF * ND * 2
FIRST_GROUPS = 4
LANES = 128
ROWS = NF * ND * 2
WIDE = -(-(ROWS + 2) // LANES) * LANES

COS = [math.cos(2.0 * math.pi * d / ND) for d in range(HALF + 1)]
SIN = [math.sin(2.0 * math.pi * d / ND) for d in range(HALF + 1)]

(
    CUR_A,
    CUR_M,
    CUR_B,
    CX_A,
    CX_B,
    W0_A,
    W0_B,
    W1_A,
    W1_B,
    SEA_A,
    SEA_B,
    SEA_A1,
    SEA_A2,
    SEA_B1,
    SEA_B2,
    TAU,
    ICOS_A,
    ICOS_B,
    KAP_A,
    MU_A,
    MU_B,
    KAP_B,
    TAN_A,
    TAN_B,
    ICOS_0,
    ICOS_1,
) = range(26)
PAR_ROWS = 32


def flux(lo2, lo1, hi1, hi2, c):
    forward = c >= 0.0
    source = jnp.where(forward, lo1, hi1)
    upwind = jnp.where(forward, lo2, hi2)
    both = lo1 + hi1
    bend = both - 3.0 * source + upwind
    w = (1.0 / 6.0) - (c * c) * (1.0 / 6.0)
    return c * (0.5 * (both - c * (hi1 - lo1)) - w * bend)


def group_speed():
    k = lax.broadcasted_iota(jnp.int32, (8, LANES), 0)
    speed = jnp.zeros((8, LANES), jnp.float32)
    for i in range(GF):
        for h in range(2):
            value = SPEED_TOP * FREQ_STEP**-i * (1.0 - 2.0 * h)
            speed = jnp.where(k == 2 * i + h, value, speed)
    return speed


def freq_weight():
    k = lax.broadcasted_iota(jnp.int32, (8, LANES), 0)
    weight = jnp.zeros((8, LANES), jnp.float32)
    for i in range(GF):
        weight = jnp.where(lax.div(k, 2) == i, (i + 1.0) / NF, weight)
    return weight


def swap_halves(v):
    k = lax.broadcasted_iota(jnp.int32, (8, LANES), 0)
    return jnp.where(lax.rem(k, 2) == 0, pltpu.roll(v, 7, 0), pltpu.roll(v, 1, 0))


def wide_row(par, index):
    return jnp.broadcast_to(par[index : index + 1, :], (8, LANES))


def pack_kernel(wind, current, sea, out):
    me = lax.axis_index("band")
    rows, strip = wind.shape[1], wind.shape[2]
    empty = jnp.zeros((rows, LANES - strip), jnp.float32)
    for part, ref in enumerate((current, wind)):
        for axis in range(2):
            wide = jnp.concatenate([ref[axis], empty], axis=1)
            out[2 * part + axis] = pltpu.roll(wide, me * strip, 1)
    out[4] = jnp.zeros((rows, LANES), jnp.float32)
    seas = sea[...].astype(jnp.float32)
    out[4, pl.ds(2 * me, 1), :] = seas[0:1]
    out[4, pl.ds(2 * me + 1, 1), :] = seas[1:2]


def split_kernel(spectra, relayed, direct):
    relayed[...] = spectra[0 : relayed.shape[0], :]
    direct[...] = spectra[relayed.shape[0] :, :]


def edge_kernel(bands, geometry, forcing, spectra, par, west, east, line):
    me = lax.axis_index("band")
    is_even = lax.rem(me, 2) == 0
    row = 2 * me
    has_south = jnp.where(me > 0, 1.0, 0.0)
    has_north = jnp.where(me < bands - 1, 1.0, 0.0)

    def around(part):
        south = [jnp.maximum(row - 2, 0), jnp.maximum(row - 1, 0)]
        north = [jnp.minimum(row + 2, 2 * bands - 1), jnp.minimum(row + 3, 2 * bands - 1)]
        return (
            [forcing[part, pl.ds(i, 1), :] * has_south for i in south]
            + [forcing[part, pl.ds(row + i, 1), :] for i in range(2)]
            + [forcing[part, pl.ds(i, 1), :] * has_north for i in north]
        )

    seas = around(4)

    def pick(low, high):
        return jnp.where(is_even, low, high)

    def put(index, value):
        par[index : index + 1, :] = jnp.broadcast_to(value, (1, LANES))

    tau = jnp.where(is_even, 1.0, -1.0)
    north = around(1)
    face = [0.5 * (north[i] + north[i + 1]) for i in range(1, 4)]
    put(CUR_A, tau * pick(face[0], face[2]))
    put(CUR_M, tau * face[1])
    put(CUR_B, tau * pick(face[2], face[0]))
    lane = lax.broadcasted_iota(jnp.int32, (1, LANES), 1)
    inside = jnp.where(lane == 0, 0.0, 1.0)
    east_speed = around(0)[2:4]
    wind_0, wind_1 = around(2)[2:4], around(3)[2:4]
    shifted = [0.5 * inside * (v + pltpu.roll(v, 1, 1)) for v in east_speed]
    put(CX_A, pick(shifted[0], shifted[1]))
    put(CX_B, pick(shifted[1], shifted[0]))
    put(W0_A, pick(wind_0[0], wind_0[1]))
    put(W0_B, pick(wind_0[1], wind_0[0]))
    put(W1_A, pick(wind_1[0], wind_1[1]))
    put(W1_B, pick(wind_1[1], wind_1[0]))
    put(SEA_A, pick(seas[2], seas[3]))
    put(SEA_B, pick(seas[3], seas[2]))
    put(SEA_A1, pick(seas[1], seas[4]))
    put(SEA_A2, pick(seas[0], seas[5]))
    put(SEA_B1, pick(seas[4], seas[1]))
    put(SEA_B2, pick(seas[5], seas[0]))
    put(TAU, tau)
    icos = [geometry[me, 0], geometry[me, 1]]
    put(ICOS_A, inside * pick(icos[0], icos[1]))
    put(ICOS_B, inside * pick(icos[1], icos[0]))
    put(KAP_A, geometry[me, 2])
    put(MU_A, geometry[me, 3])
    put(MU_B, geometry[me, 4])
    put(KAP_B, geometry[me, 5])
    put(TAN_A, geometry[me, 6])
    put(TAN_B, geometry[me, 7])
    put(ICOS_0, icos[0])
    put(ICOS_1, icos[1])
    par[26:32, :] = jnp.zeros((6, LANES), jnp.float32)

    sub = lax.broadcasted_iota(jnp.int32, (LANES, LANES), 0)
    both = jnp.where(
        lax.rem(sub, 2) == 0,
        jnp.broadcast_to(seas[2], (LANES, LANES)),
        jnp.broadcast_to(seas[3], (LANES, LANES)),
    )
    full = ROWS // LANES
    for block in range(WIDE // LANES):
        at = block * LANES
        if block < full:
            cells = spectra[at : at + LANES, :] * both
        else:
            left = ROWS - at
            line[...] = jnp.zeros((LANES, LANES), jnp.float32)
            line[0:left, :] = spectra[at : at + left, :] * both[0:left]
            line[left : left + 1, :] = east_speed[0]
            line[left + 1 : left + 2, :] = east_speed[1]
            cells = line[...]
        turned = cells.T
        west[:, at : at + LANES] = turned[0:2]
        east[:, at : at + LANES] = turned[LANES - 2 : LANES]


def fix_kernel(table, par, west, east, from_west, from_east, fix, tall):
    lane = lax.broadcasted_iota(jnp.int32, (1, WIDE), 1)
    even_row = lax.rem(lane, 2) == 0
    speed = table[0:1] * par[ICOS_0 : ICOS_0 + 1, 0:1] + table[1:2] * par[ICOS_1 : ICOS_1 + 1, 0:1]

    def column(ref, row):
        cells = ref[row : row + 1, :]
        drift = jnp.where(even_row, cells[:, ROWS : ROWS + 1], cells[:, ROWS + 1 : ROWS + 2])
        return cells, drift

    xm2, _ = column(from_west, 0)
    xm1, dm1 = column(from_west, 1)
    x0, d0 = column(west, 0)
    x1, d1 = column(west, 1)
    y2, d2 = column(east, 0)
    y1, dy1 = column(east, 1)
    z0, dz0 = column(from_east, 0)
    z1, _ = column(from_east, 1)
    first = flux(xm2, xm1, x0, x1, speed + 0.5 * (dm1 + d0))
    last = flux(y2, y1, z0, z1, speed + 0.5 * (dy1 + dz0))
    c = speed + 0.5 * (d0 + d1)
    second = jnp.where(c >= 0.0, -c * (1.0 - c * c) * (1.0 / 6.0), 0.0) * (xm1 - y1)
    c = speed + 0.5 * (d2 + dy1)
    before = jnp.where(c >= 0.0, 0.0, -c * (1.0 - c * c) * (1.0 / 6.0)) * (z0 - x0)
    tall[...] = jnp.zeros((LANES, WIDE), jnp.float32)
    tall[0:1, :] = first - second
    tall[1:2, :] = second
    tall[LANES - 2 : LANES - 1, :] = -before
    tall[LANES - 1 : LANES, :] = before - last
    for block in range(WIDE // LANES):
        at = block * LANES
        fix[at : at + LANES, :] = tall[:, at : at + LANES].T


def base_kernel(par, spectra, beyond, base_first, base_last):
    odd = lax.rem(lax.axis_index("band"), 2)
    sea_a, sea_b = wide_row(par, SEA_A), wide_row(par, SEA_B)
    sea_b1, sea_b2 = wide_row(par, SEA_B1), wide_row(par, SEA_B2)
    cur_a, cur_m, cur_b = wide_row(par, CUR_A), wide_row(par, CUR_M), wide_row(par, CUR_B)
    cx_a, cx_b = wide_row(par, CX_A), wide_row(par, CX_B)
    kap_a, mu_a = wide_row(par, KAP_A), wide_row(par, MU_A)
    mu_b, kap_b = wide_row(par, MU_B), wide_row(par, KAP_B)
    tau = wide_row(par, TAU)
    icos_a, icos_b = wide_row(par, ICOS_A), wide_row(par, ICOS_B)

    def along_east(x, speed_x, current_x, cosine):
        crossing = flux(
            pltpu.roll(x, 2, 1),
            pltpu.roll(x, 1, 1),
            x,
            pltpu.roll(x, LANES - 1, 1),
            speed_x * cosine + current_x,
        )
        return crossing - pltpu.roll(crossing, LANES - 1, 1)

    def one_group(base, first, g, speeds):
        start = (first + g) * GROUP_ROWS
        north = speeds * tau
        east_a, east_b = speeds * icos_a, speeds * icos_b
        for d in range(HALF):
            row_a = pl.ds(start + 2 * d + odd, 8, stride=ND)
            row_b = pl.ds(start + 2 * d + 1 - odd, 8, stride=ND)
            a = spectra[row_a, :] * sea_a
            b = spectra[row_b, :] * sea_b
            b1 = beyond[row_a, :] * sea_b1
            b2 = beyond[row_b, :] * sea_b2
            c = north * SIN[d] + cur_a
            w = (1.0 / 6.0) - (c * c) * (1.0 / 6.0)
            flux_a = c * (0.5 * (a - c * a) - w * jnp.where(c >= 0.0, a, b - 2.0 * a))
            flux_m = flux(0.0, a, b, b1, north * SIN[d] + cur_m)
            flux_b = flux(a, b, b1, b2, north * SIN[d] + cur_b)
            to_a = along_east(a, east_a, cx_a, COS[d])
            to_b = along_east(b, east_b, cx_b, COS[d])
            at = pl.multiple_of(g * (HALF * 16) + d * 16, 8)
            base[pl.ds(at, 8), :] = a + to_a + kap_a * flux_a - mu_a * flux_m
            base[pl.ds(at + 8, 8), :] = b + to_b + mu_b * flux_m - kap_b * flux_b
        return speeds * FREQ_STEP**-GF

    speeds = lax.fori_loop(
        0, FIRST_GROUPS, functools.partial(one_group, base_first, 0), group_speed()
    )
    lax.fori_loop(
        0, GROUPS - FIRST_GROUPS, functools.partial(one_group, base_last, FIRST_GROUPS), speeds
    )


def turn(cells, rate):
    after = [swap_halves(cells[0]), swap_halves(cells[1])]
    lower = swap_halves(cells[HALF - 1])
    ring = [lower] + cells + after
    fluxes = []
    for d in range(HALF):
        mean = 0.5 * (COS[d] + COS[d + 1])
        fluxes.append(flux(ring[d], ring[d + 1], ring[d + 2], ring[d + 3], rate * mean))
    last = swap_halves(fluxes[HALF - 1])
    return [cells[d] - (fluxes[d] - (fluxes[d - 1] if d else last)) for d in range(HALF)]


def finish_groups(first, count, skip, par, base, fix, ahead, turned, total):
    odd = lax.rem(lax.axis_index("band"), 2)
    sea_a1, sea_a2 = wide_row(par, SEA_A1), wide_row(par, SEA_A2)
    cur_a, cur_m = wide_row(par, CUR_A), wide_row(par, CUR_M)
    kap_a, mu_a, mu_b = wide_row(par, KAP_A), wide_row(par, MU_A), wide_row(par, MU_B)
    tau = wide_row(par, TAU)
    tan_a, tan_b = wide_row(par, TAN_A), wide_row(par, TAN_B)

    def one_group(g, carry):
        speeds, weight, sum_a, sum_b = carry
        start = (skip + g) * GROUP_ROWS
        fix_start = (first + g) * GROUP_ROWS
        north = speeds * tau
        cells_a, cells_b = [], []
        for d in range(HALF):
            n1 = ahead[pl.ds(start + 2 * d + 1 - odd, 8, stride=ND), :] * sea_a1
            n2 = ahead[pl.ds(start + 2 * d + odd, 8, stride=ND), :] * sea_a2
            fix_a = fix[pl.ds(fix_start + 2 * d + odd, 8, stride=ND), :]
            fix_b = fix[pl.ds(fix_start + 2 * d + 1 - odd, 8, stride=ND), :]
            c = north * SIN[d] + cur_a
            w = (1.0 / 6.0) - (c * c) * (1.0 / 6.0)
            flux_a = c * (0.5 * (n1 + c * n1) - w * jnp.where(c >= 0.0, n2 - 2.0 * n1, n1))
            c = north * SIN[d] + cur_m
            w = (c * c) * (1.0 / 6.0) - (1.0 / 6.0)
            flux_m = jnp.where(c >= 0.0, c * w, 0.0) * n1
            at = pl.multiple_of(g * (HALF * 16) + d * 16, 8)
            cells_a.append(base[pl.ds(at, 8), :] + fix_a + kap_a * flux_a - mu_a * flux_m)
            cells_b.append(base[pl.ds(at + 8, 8), :] + fix_b + mu_b * flux_m)
        square_a = square_b = 0.0
        for d, v in enumerate(turn(cells_a, speeds * tan_a)):
            at = pl.multiple_of(g * (HALF * 16) + d * 16, 8)
            turned[pl.ds(at, 8), :] = v
            square_a = square_a + v * v
        for d, v in enumerate(turn(cells_b, speeds * tan_b)):
            at = pl.multiple_of(g * (HALF * 16) + d * 16 + 8, 8)
            turned[pl.ds(at, 8), :] = v
            square_b = square_b + v * v
        return (
            speeds * FREQ_STEP**-GF,
            weight + GF / NF,
            sum_a + weight * square_a,
            sum_b + weight * square_b,
        )

    speeds = group_speed() * FREQ_STEP ** -(GF * first)
    weight = freq_weight() + GF * first / NF
    carry = (speeds, weight, total[0:8, :], total[8:16, :])
    _, _, total[0:8, :], total[8:16, :] = lax.fori_loop(0, count, one_group, carry)


def finish_either(bands, first, count, par, base, fix, straight, split, turned, total):
    me = lax.axis_index("band")
    middle = jnp.logical_or(me == bands // 2 - 1, me == bands // 2)

    @pl.when(middle)
    def _():
        finish_groups(first, count, 0, par, base, fix, split, turned, total)

    @pl.when(jnp.logical_not(middle))
    def _():
        finish_groups(first, count, first, par, base, fix, straight, turned, total)


def first_kernel(bands, par, base, fix, straight, split, turned, total):
    total[...] = jnp.zeros((16, LANES), jnp.float32)
    finish_either(bands, 0, FIRST_GROUPS, par, base, fix, straight, split, turned, total)


def last_kernel(bands, par, base, fix, straight, split, done, before, out, turned, total):
    odd = lax.rem(lax.axis_index("band"), 2)
    later = GROUPS - FIRST_GROUPS
    total[...] = before[...]
    finish_either(bands, FIRST_GROUPS, later, par, base, fix, straight, split, turned, total)
    scale = 2.0 / (NF * ND)
    steep_a = jnp.sum(total[0:8, :], axis=0, keepdims=True) * scale
    steep_b = jnp.sum(total[8:16, :], axis=0, keepdims=True) * scale
    sea_a, sea_b = wide_row(par, SEA_A), wide_row(par, SEA_B)
    w0_a, w0_b = wide_row(par, W0_A), wide_row(par, W0_B)
    w1_a, w1_b = wide_row(par, W1_A), wide_row(par, W1_B)

    def one_group(first, ref, g, carry):
        coupling, weight = carry
        start = (first + g) * GROUP_ROWS
        gain_a = sea_a / (1.0 + weight * steep_a)
        gain_b = sea_b / (1.0 + weight * steep_b)
        wa0, wa1 = w0_a * coupling, w1_a * coupling
        wb0, wb1 = w0_b * coupling, w1_b * coupling
        for d in range(HALF):
            at = pl.multiple_of(g * (HALF * 16) + d * 16, 8)
            growth_a = jnp.maximum(wa0 * COS[d] + wa1 * SIN[d] + (1.0 - GROWTH), 1.0)
            growth_b = jnp.maximum(wb0 * COS[d] + wb1 * SIN[d] + (1.0 - GROWTH), 1.0)
            out[pl.ds(start + 2 * d + odd, 8, stride=ND), :] = (
                ref[pl.ds(at, 8), :] * gain_a * growth_a
            )
            out[pl.ds(start + 2 * d + 1 - odd, 8, stride=ND), :] = (
                ref[pl.ds(at + 8, 8), :] * gain_b * growth_b
            )
        return coupling * FREQ_STEP**GF, weight + GF / NF

    k = lax.broadcasted_iota(jnp.int32, (8, LANES), 0)
    coupling = jnp.zeros((8, LANES), jnp.float32)
    for i in range(GF):
        for h in range(2):
            value = GROWTH * WIND_COUPLING * FREQ_STEP**i * (1.0 - 2.0 * h)
            coupling = jnp.where(k == 2 * i + h, value, coupling)
    carry = (coupling, freq_weight())
    carry = lax.fori_loop(0, FIRST_GROUPS, functools.partial(one_group, 0, done), carry)
    lax.fori_loop(0, later, functools.partial(one_group, FIRST_GROUPS, turned), carry)


def geometry_table(bands):
    total = 2 * bands

    def angle(position):
        return (LAT_SOUTH + (LAT_NORTH - LAT_SOUTH) * position / total) * (math.pi / 180.0)

    table = np.zeros((bands, 8), np.float32)
    for b in range(bands):
        cells = [angle(2 * b + 0.5), angle(2 * b + 1.5)]
        faces = [angle(2 * b), angle(2 * b + 1), angle(2 * b + 2)]
        icos = [1.0 / math.cos(v) for v in cells]
        near, far = (0, 1) if b % 2 == 0 else (1, 0)
        face_a, face_b = (faces[0], faces[2]) if b % 2 == 0 else (faces[2], faces[0])
        table[b] = [
            icos[0],
            icos[1],
            math.cos(face_a) * icos[near],
            math.cos(faces[1]) * icos[near],
            math.cos(faces[1]) * icos[far],
            math.cos(face_b) * icos[far],
            -TURNING * math.tan(cells[near]),
            -TURNING * math.tan(cells[far]),
        ]
    return table


def speed_table():
    table = np.zeros((2, WIDE), np.float32)
    for k in range(NF * ND):
        value = SPEED_TOP * FREQ_STEP ** -(k // ND) * math.cos(2.0 * math.pi * (k % ND) / ND)
        table[0, 2 * k] = value
        table[1, 2 * k + 1] = value
    return table


VMEM = pl.BlockSpec(memory_space=pltpu.VMEM)
SMEM = pl.BlockSpec(memory_space=pltpu.SMEM)
ANY = pl.BlockSpec(memory_space=pl.ANY)
PARAMS = pltpu.CompilerParams(vmem_limit_bytes=40 * 1024 * 1024)


def call(kernel, name, operands, specs, shapes, scratch, micros):
    outs = [jax.ShapeDtypeStruct(s, jnp.float32) for s in shapes]
    return pl.pallas_call(
        kernel,
        name=name,
        out_shape=outs,
        in_specs=specs,
        out_specs=[VMEM] * len(outs),
        scratch_shapes=scratch,
        compiler_params=PARAMS,
        cost_estimate=pl.CostEstimate(
            flops=0, bytes_accessed=int(micros * 3.0e6), transcendentals=0
        ),
    )(*operands)


def swapped(pairs):
    return pairs + [(t, s) for s, t in pairs]


def per_device(bands, spec_count, spectra, sea_mask, wind, current):
    comp_count, row_count, col_count = spectra.shape
    cells = spectra.reshape(comp_count * row_count, col_count)
    middle = bands // 2 - 1
    first_rows = FIRST_GROUPS * GROUP_ROWS
    last_rows = ROWS - first_rows

    straight = lax.ppermute(
        cells, "band", swapped([(b, b + 1) for b in range(1, bands - 1, 2) if b != middle])
    )
    pairs = [(b, b + 1) for b in range(0, bands, 2)]
    beyond = lax.ppermute(cells, "band", swapped(pairs))
    part_relayed, part_direct = call(
        split_kernel,
        "split",
        (cells,),
        [VMEM],
        [(first_rows, LANES), (last_rows, LANES)],
        [],
        0.3,
    )

    (forcing,) = call(
        pack_kernel,
        "pack_forcing",
        (wind, current, sea_mask),
        [VMEM] * 3,
        [(5, wind.shape[1], LANES)],
        [],
        0.3,
    )
    forcing = forcing + lax.ppermute(forcing, "band", swapped(pairs))
    bit = 4
    while bit < bands:
        turnabout = [(b, b ^ bit) for b in range(bands)]
        forcing = forcing + lax.ppermute(forcing, "band", turnabout)
        bit *= 2
    part_relayed, forcing = lax.optimization_barrier((part_relayed, forcing))
    relay = lax.ppermute(part_relayed, "band", [(middle, bands - 1), (middle + 1, 0)])
    free = [2 * chip + chip % 2 for chip in range(bands // 2)]
    across = lax.ppermute(
        forcing, "band", [(b, free[chip ^ 1]) for chip, b in enumerate(free)]
    )
    along = lax.ppermute(across, "band", [(b, b ^ 1) for b in free])
    forcing = forcing + across + along
    part_direct, forcing = lax.optimization_barrier((part_direct, forcing))
    direct = lax.ppermute(
        part_direct, "band", [(middle, middle + 1), (middle + 1, middle)]
    )
    relayed = lax.ppermute(relay, "band", [(bands - 1, middle + 1), (0, middle)])

    par, west, east = call(
        functools.partial(edge_kernel, bands),
        "edges",
        (jnp.asarray(geometry_table(bands)), forcing, cells),
        [SMEM, VMEM, VMEM],
        [(PAR_ROWS, LANES), (2, WIDE), (2, WIDE)],
        [pltpu.VMEM((LANES, LANES), jnp.float32)],
        1.0,
    )
    ring = [(s, (s + 1) % spec_count) for s in range(spec_count)]
    from_west = lax.ppermute(east, "spec", ring)
    from_east = lax.ppermute(west, "spec", [(t, s) for s, t in ring])
    base_first, base_last = call(
        base_kernel,
        "base",
        (par, cells, beyond),
        [VMEM] * 3,
        [(first_rows, LANES), (last_rows, LANES)],
        [],
        4.0,
    )
    base_first, from_west, from_east = lax.optimization_barrier((base_first, from_west, from_east))
    (fix,) = call(
        fix_kernel,
        "fix",
        (jnp.asarray(speed_table()), par, west, east, from_west, from_east),
        [VMEM] * 6,
        [(WIDE, LANES)],
        [pltpu.VMEM((LANES, WIDE), jnp.float32)],
        1.0,
    )
    turned, total = call(
        functools.partial(first_kernel, bands),
        "first_groups",
        (par, base_first, fix, straight, relayed),
        [VMEM] * 5,
        [(first_rows, LANES), (16, LANES)],
        [],
        1.0,
    )
    (out,) = call(
        functools.partial(last_kernel, bands),
        "last_groups",
        (par, base_last, fix, straight, direct, turned, total),
        [VMEM] * 7,
        [(ROWS, LANES)],
        [pltpu.VMEM((last_rows, LANES), jnp.float32), pltpu.VMEM((16, LANES), jnp.float32)],
        2.0,
    )
    return out.reshape(comp_count, row_count, col_count)


def solution(mesh):
    placed = (
        P(None, "band", "spec"),
        P("band", "spec"),
        P(None, None, ("spec", "band")),
        P(None, None, ("spec", "band")),
    )
    return jax.shard_map(
        functools.partial(per_device, mesh.shape["band"], mesh.shape["spec"]),
        mesh=mesh,
        in_specs=placed,
        out_specs=P(None, "band", "spec"),
        check_vma=False,
    )
```

```python
import functools
import math

import jax
import jax.numpy as jnp
import numpy as np
from jax import lax
from jax.experimental import pallas as pl
from jax.experimental.pallas import tpu as pltpu
from jax.sharding import PartitionSpec as P

NF = 36
ND = 36
HALF = ND // 2
LAT_SOUTH = 30.0
LAT_NORTH = 55.0
SPEED_TOP = 0.35
FREQ_STEP = 1.1
TURNING = 1.5
GROWTH = 0.05
WIND_COUPLING = 0.04

GF = 4
GROUPS = NF // GF
GROUP_ROWS = GF * ND * 2
FIRST_GROUPS = 4
LANES = 128
ROWS = NF * ND * 2
WIDE = -(-(ROWS + 2) // LANES) * LANES

COS = [math.cos(2.0 * math.pi * d / ND) for d in range(HALF + 1)]
SIN = [math.sin(2.0 * math.pi * d / ND) for d in range(HALF + 1)]

(
    CUR_A,
    CUR_M,
    CUR_B,
    CX_A,
    CX_B,
    W0_A,
    W0_B,
    W1_A,
    W1_B,
    SEA_A,
    SEA_B,
    SEA_A1,
    SEA_A2,
    SEA_B1,
    SEA_B2,
    TAU,
    ICOS_A,
    ICOS_B,
    KAP_A,
    MU_A,
    MU_B,
    KAP_B,
    TAN_A,
    TAN_B,
    ICOS_0,
    ICOS_1,
) = range(26)
PAR_ROWS = 32


def flux(lo2, lo1, hi1, hi2, c):
    forward = c >= 0.0
    source = jnp.where(forward, lo1, hi1)
    upwind = jnp.where(forward, lo2, hi2)
    both = lo1 + hi1
    bend = both - 3.0 * source + upwind
    w = (1.0 / 6.0) - (c * c) * (1.0 / 6.0)
    return c * (0.5 * (both - c * (hi1 - lo1)) - w * bend)


def group_speed():
    k = lax.broadcasted_iota(jnp.int32, (8, LANES), 0)
    speed = jnp.zeros((8, LANES), jnp.float32)
    for i in range(GF):
        for h in range(2):
            value = SPEED_TOP * FREQ_STEP**-i * (1.0 - 2.0 * h)
            speed = jnp.where(k == 2 * i + h, value, speed)
    return speed


def freq_weight():
    k = lax.broadcasted_iota(jnp.int32, (8, LANES), 0)
    weight = jnp.zeros((8, LANES), jnp.float32)
    for i in range(GF):
        weight = jnp.where(lax.div(k, 2) == i, (i + 1.0) / NF, weight)
    return weight


def swap_halves(v):
    k = lax.broadcasted_iota(jnp.int32, (8, LANES), 0)
    return jnp.where(lax.rem(k, 2) == 0, pltpu.roll(v, 7, 0), pltpu.roll(v, 1, 0))


def wide_row(par, index):
    return jnp.broadcast_to(par[index : index + 1, :], (8, LANES))


def pack_kernel(wind, current, sea, out, wind_here, current_here, sea_here, sems):
    me = lax.axis_index("band")
    rows, strip = wind.shape[1], wind.shape[2]
    copies = [
        pltpu.make_async_copy(wind, wind_here, sems.at[0]),
        pltpu.make_async_copy(current, current_here, sems.at[1]),
        pltpu.make_async_copy(sea, sea_here, sems.at[2]),
    ]
    for copy in copies:
        copy.start()
    out[4] = jnp.zeros((rows, LANES), jnp.float32)
    empty = jnp.zeros((rows, LANES - strip), jnp.float32)
    for copy in copies:
        copy.wait()
    for part, ref in enumerate((current_here, wind_here)):
        for axis in range(2):
            wide = jnp.concatenate([ref[axis], empty], axis=1)
            out[2 * part + axis] = pltpu.roll(wide, me * strip, 1)
    seas = sea_here[...].astype(jnp.float32)
    out[4, pl.ds(2 * me, 1), :] = seas[0:1]
    out[4, pl.ds(2 * me + 1, 1), :] = seas[1:2]


def split_kernel(source, mask, relayed, direct, west, east, spectra, sea, line, sems):
    first = relayed.shape[0]
    whole = pltpu.make_async_copy(source, spectra, sems.at[0])
    parts = [
        pltpu.make_async_copy(source.at[0:first], relayed, sems.at[1]),
        pltpu.make_async_copy(source.at[first:ROWS], direct, sems.at[2]),
    ]
    masking = pltpu.make_async_copy(mask, sea, sems.at[3])
    masking.start()
    whole.start()
    for part in parts:
        part.start()
    masking.wait()
    whole.wait()
    seas = sea[...].astype(jnp.float32)
    sub = lax.broadcasted_iota(jnp.int32, (LANES, LANES), 0)
    both = jnp.where(
        lax.rem(sub, 2) == 0,
        jnp.broadcast_to(seas[0:1], (LANES, LANES)),
        jnp.broadcast_to(seas[1:2], (LANES, LANES)),
    )
    full = ROWS // LANES
    for block in range(WIDE // LANES):
        at = block * LANES
        if block < full:
            cells = spectra[at : at + LANES, :] * both
        else:
            left = ROWS - at
            line[...] = jnp.zeros((LANES, LANES), jnp.float32)
            line[0:left, :] = spectra[at : at + left, :] * both[0:left]
            cells = line[...]
        turned = cells.T
        west[:, at : at + LANES] = turned[0:2]
        east[:, at : at + LANES] = turned[LANES - 2 : LANES]
    for part in parts:
        part.wait()


def table_kernel(bands, geometry, forcing, west_in, east_in, par, west, east):
    me = lax.axis_index("band")
    is_even = lax.rem(me, 2) == 0
    row = 2 * me
    has_south = jnp.where(me > 0, 1.0, 0.0)
    has_north = jnp.where(me < bands - 1, 1.0, 0.0)

    def around(part):
        south = [jnp.maximum(row - 2, 0), jnp.maximum(row - 1, 0)]
        north = [jnp.minimum(row + 2, 2 * bands - 1), jnp.minimum(row + 3, 2 * bands - 1)]
        return (
            [forcing[part, pl.ds(i, 1), :] * has_south for i in south]
            + [forcing[part, pl.ds(row + i, 1), :] for i in range(2)]
            + [forcing[part, pl.ds(i, 1), :] * has_north for i in north]
        )

    seas = around(4)

    def pick(low, high):
        return jnp.where(is_even, low, high)

    def put(index, value):
        par[index : index + 1, :] = jnp.broadcast_to(value, (1, LANES))

    tau = jnp.where(is_even, 1.0, -1.0)
    north = around(1)
    face = [0.5 * (north[i] + north[i + 1]) for i in range(1, 4)]
    put(CUR_A, tau * pick(face[0], face[2]))
    put(CUR_M, tau * face[1])
    put(CUR_B, tau * pick(face[2], face[0]))
    lane = lax.broadcasted_iota(jnp.int32, (1, LANES), 1)
    inside = jnp.where(lane == 0, 0.0, 1.0)
    east_speed = around(0)[2:4]
    wind_0, wind_1 = around(2)[2:4], around(3)[2:4]
    shifted = [0.5 * inside * (v + pltpu.roll(v, 1, 1)) for v in east_speed]
    put(CX_A, pick(shifted[0], shifted[1]))
    put(CX_B, pick(shifted[1], shifted[0]))
    put(W0_A, pick(wind_0[0], wind_0[1]))
    put(W0_B, pick(wind_0[1], wind_0[0]))
    put(W1_A, pick(wind_1[0], wind_1[1]))
    put(W1_B, pick(wind_1[1], wind_1[0]))
    put(SEA_A, pick(seas[2], seas[3]))
    put(SEA_B, pick(seas[3], seas[2]))
    put(SEA_A1, pick(seas[1], seas[4]))
    put(SEA_A2, pick(seas[0], seas[5]))
    put(SEA_B1, pick(seas[4], seas[1]))
    put(SEA_B2, pick(seas[5], seas[0]))
    put(TAU, tau)
    icos = [geometry[me, 0], geometry[me, 1]]
    put(ICOS_A, inside * pick(icos[0], icos[1]))
    put(ICOS_B, inside * pick(icos[1], icos[0]))
    put(KAP_A, geometry[me, 2])
    put(MU_A, geometry[me, 3])
    put(MU_B, geometry[me, 4])
    put(KAP_B, geometry[me, 5])
    put(TAN_A, geometry[me, 6])
    put(TAN_B, geometry[me, 7])
    put(ICOS_0, icos[0])
    put(ICOS_1, icos[1])
    par[26:32, :] = jnp.zeros((6, LANES), jnp.float32)

    west[...] = west_in[...]
    east[...] = east_in[...]
    for i in range(2):
        west[:, ROWS + i : ROWS + i + 1] = jnp.concatenate(
            [east_speed[i][:, j : j + 1] for j in range(2)], axis=0
        )
        east[:, ROWS + i : ROWS + i + 1] = jnp.concatenate(
            [east_speed[i][:, j : j + 1] for j in (LANES - 2, LANES - 1)], axis=0
        )


def fix_kernel(table, par, west, east, from_west, from_east, fix, tall):
    lane = lax.broadcasted_iota(jnp.int32, (1, WIDE), 1)
    even_row = lax.rem(lane, 2) == 0
    speed = table[0:1] * par[ICOS_0 : ICOS_0 + 1, 0:1] + table[1:2] * par[ICOS_1 : ICOS_1 + 1, 0:1]

    def column(ref, row):
        cells = ref[row : row + 1, :]
        drift = jnp.where(even_row, cells[:, ROWS : ROWS + 1], cells[:, ROWS + 1 : ROWS + 2])
        return cells, drift

    xm2, _ = column(from_west, 0)
    xm1, dm1 = column(from_west, 1)
    x0, d0 = column(west, 0)
    x1, d1 = column(west, 1)
    y2, d2 = column(east, 0)
    y1, dy1 = column(east, 1)
    z0, dz0 = column(from_east, 0)
    z1, _ = column(from_east, 1)
    first = flux(xm2, xm1, x0, x1, speed + 0.5 * (dm1 + d0))
    last = flux(y2, y1, z0, z1, speed + 0.5 * (dy1 + dz0))
    c = speed + 0.5 * (d0 + d1)
    second = jnp.where(c >= 0.0, -c * (1.0 - c * c) * (1.0 / 6.0), 0.0) * (xm1 - y1)
    c = speed + 0.5 * (d2 + dy1)
    before = jnp.where(c >= 0.0, 0.0, -c * (1.0 - c * c) * (1.0 / 6.0)) * (z0 - x0)
    tall[...] = jnp.zeros((LANES, WIDE), jnp.float32)
    tall[0:1, :] = first - second
    tall[1:2, :] = second
    tall[LANES - 2 : LANES - 1, :] = -before
    tall[LANES - 1 : LANES, :] = before - last
    for block in range(WIDE // LANES):
        at = block * LANES
        fix[at : at + LANES, :] = tall[:, at : at + LANES].T


def base_kernel(par, spectra, beyond, base_first, base_last):
    odd = lax.rem(lax.axis_index("band"), 2)
    sea_a, sea_b = wide_row(par, SEA_A), wide_row(par, SEA_B)
    sea_b1, sea_b2 = wide_row(par, SEA_B1), wide_row(par, SEA_B2)
    cur_a, cur_m, cur_b = wide_row(par, CUR_A), wide_row(par, CUR_M), wide_row(par, CUR_B)
    cx_a, cx_b = wide_row(par, CX_A), wide_row(par, CX_B)
    kap_a, mu_a = wide_row(par, KAP_A), wide_row(par, MU_A)
    mu_b, kap_b = wide_row(par, MU_B), wide_row(par, KAP_B)
    tau = wide_row(par, TAU)
    icos_a, icos_b = wide_row(par, ICOS_A), wide_row(par, ICOS_B)

    def along_east(x, speed_x, current_x, cosine):
        crossing = flux(
            pltpu.roll(x, 2, 1),
            pltpu.roll(x, 1, 1),
            x,
            pltpu.roll(x, LANES - 1, 1),
            speed_x * cosine + current_x,
        )
        return crossing - pltpu.roll(crossing, LANES - 1, 1)

    def one_group(base, first, g, speeds):
        start = (first + g) * GROUP_ROWS
        north = speeds * tau
        east_a, east_b = speeds * icos_a, speeds * icos_b
        for d in range(HALF):
            row_a = pl.ds(start + 2 * d + odd, 8, stride=ND)
            row_b = pl.ds(start + 2 * d + 1 - odd, 8, stride=ND)
            a = spectra[row_a, :] * sea_a
            b = spectra[row_b, :] * sea_b
            b1 = beyond[row_a, :] * sea_b1
            b2 = beyond[row_b, :] * sea_b2
            c = north * SIN[d] + cur_a
            w = (1.0 / 6.0) - (c * c) * (1.0 / 6.0)
            flux_a = c * (0.5 * (a - c * a) - w * jnp.where(c >= 0.0, a, b - 2.0 * a))
            flux_m = flux(0.0, a, b, b1, north * SIN[d] + cur_m)
            flux_b = flux(a, b, b1, b2, north * SIN[d] + cur_b)
            to_a = along_east(a, east_a, cx_a, COS[d])
            to_b = along_east(b, east_b, cx_b, COS[d])
            at = pl.multiple_of(g * (HALF * 16) + d * 16, 8)
            base[pl.ds(at, 8), :] = a + to_a + kap_a * flux_a - mu_a * flux_m
            base[pl.ds(at + 8, 8), :] = b + to_b + mu_b * flux_m - kap_b * flux_b
        return speeds * FREQ_STEP**-GF

    speeds = lax.fori_loop(
        0, FIRST_GROUPS, functools.partial(one_group, base_first, 0), group_speed()
    )
    lax.fori_loop(
        0, GROUPS - FIRST_GROUPS, functools.partial(one_group, base_last, FIRST_GROUPS), speeds
    )


def turn(cells, rate):
    after = [swap_halves(cells[0]), swap_halves(cells[1])]
    lower = swap_halves(cells[HALF - 1])
    ring = [lower] + cells + after
    fluxes = []
    for d in range(HALF):
        mean = 0.5 * (COS[d] + COS[d + 1])
        fluxes.append(flux(ring[d], ring[d + 1], ring[d + 2], ring[d + 3], rate * mean))
    last = swap_halves(fluxes[HALF - 1])
    return [cells[d] - (fluxes[d] - (fluxes[d - 1] if d else last)) for d in range(HALF)]


def finish_groups(first, count, skip, par, base, fix, ahead, turned, total):
    odd = lax.rem(lax.axis_index("band"), 2)
    sea_a1, sea_a2 = wide_row(par, SEA_A1), wide_row(par, SEA_A2)
    cur_a, cur_m = wide_row(par, CUR_A), wide_row(par, CUR_M)
    kap_a, mu_a, mu_b = wide_row(par, KAP_A), wide_row(par, MU_A), wide_row(par, MU_B)
    tau = wide_row(par, TAU)
    tan_a, tan_b = wide_row(par, TAN_A), wide_row(par, TAN_B)

    def one_group(g, carry):
        speeds, weight, sum_a, sum_b = carry
        start = (skip + g) * GROUP_ROWS
        fix_start = (first + g) * GROUP_ROWS
        north = speeds * tau
        cells_a, cells_b = [], []
        for d in range(HALF):
            n1 = ahead[pl.ds(start + 2 * d + 1 - odd, 8, stride=ND), :] * sea_a1
            n2 = ahead[pl.ds(start + 2 * d + odd, 8, stride=ND), :] * sea_a2
            fix_a = fix[pl.ds(fix_start + 2 * d + odd, 8, stride=ND), :]
            fix_b = fix[pl.ds(fix_start + 2 * d + 1 - odd, 8, stride=ND), :]
            c = north * SIN[d] + cur_a
            w = (1.0 / 6.0) - (c * c) * (1.0 / 6.0)
            flux_a = c * (0.5 * (n1 + c * n1) - w * jnp.where(c >= 0.0, n2 - 2.0 * n1, n1))
            c = north * SIN[d] + cur_m
            w = (c * c) * (1.0 / 6.0) - (1.0 / 6.0)
            flux_m = jnp.where(c >= 0.0, c * w, 0.0) * n1
            at = pl.multiple_of(g * (HALF * 16) + d * 16, 8)
            cells_a.append(base[pl.ds(at, 8), :] + fix_a + kap_a * flux_a - mu_a * flux_m)
            cells_b.append(base[pl.ds(at + 8, 8), :] + fix_b + mu_b * flux_m)
        square_a = square_b = 0.0
        for d, v in enumerate(turn(cells_a, speeds * tan_a)):
            at = pl.multiple_of(g * (HALF * 16) + d * 16, 8)
            turned[pl.ds(at, 8), :] = v
            square_a = square_a + v * v
        for d, v in enumerate(turn(cells_b, speeds * tan_b)):
            at = pl.multiple_of(g * (HALF * 16) + d * 16 + 8, 8)
            turned[pl.ds(at, 8), :] = v
            square_b = square_b + v * v
        return (
            speeds * FREQ_STEP**-GF,
            weight + GF / NF,
            sum_a + weight * square_a,
            sum_b + weight * square_b,
        )

    speeds = group_speed() * FREQ_STEP ** -(GF * first)
    weight = freq_weight() + GF * first / NF
    carry = (speeds, weight, total[0:8, :], total[8:16, :])
    _, _, total[0:8, :], total[8:16, :] = lax.fori_loop(0, count, one_group, carry)


def finish_either(bands, first, count, par, base, fix, straight, split, turned, total):
    me = lax.axis_index("band")
    middle = jnp.logical_or(me == bands // 2 - 1, me == bands // 2)

    @pl.when(middle)
    def _():
        finish_groups(first, count, 0, par, base, fix, split, turned, total)

    @pl.when(jnp.logical_not(middle))
    def _():
        finish_groups(first, count, first, par, base, fix, straight, turned, total)


def first_kernel(bands, par, base, fix, straight, split, turned, total):
    total[...] = jnp.zeros((16, LANES), jnp.float32)
    finish_either(bands, 0, FIRST_GROUPS, par, base, fix, straight, split, turned, total)


def last_kernel(bands, par, base, fix, straight, split, done, before, out, turned, total):
    odd = lax.rem(lax.axis_index("band"), 2)
    later = GROUPS - FIRST_GROUPS
    total[...] = before[...]
    finish_either(bands, FIRST_GROUPS, later, par, base, fix, straight, split, turned, total)
    scale = 2.0 / (NF * ND)
    steep_a = jnp.sum(total[0:8, :], axis=0, keepdims=True) * scale
    steep_b = jnp.sum(total[8:16, :], axis=0, keepdims=True) * scale
    sea_a, sea_b = wide_row(par, SEA_A), wide_row(par, SEA_B)
    w0_a, w0_b = wide_row(par, W0_A), wide_row(par, W0_B)
    w1_a, w1_b = wide_row(par, W1_A), wide_row(par, W1_B)

    def one_group(first, ref, g, carry):
        coupling, weight = carry
        start = (first + g) * GROUP_ROWS
        gain_a = sea_a / (1.0 + weight * steep_a)
        gain_b = sea_b / (1.0 + weight * steep_b)
        wa0, wa1 = w0_a * coupling, w1_a * coupling
        wb0, wb1 = w0_b * coupling, w1_b * coupling
        for d in range(HALF):
            at = pl.multiple_of(g * (HALF * 16) + d * 16, 8)
            growth_a = jnp.maximum(wa0 * COS[d] + wa1 * SIN[d] + (1.0 - GROWTH), 1.0)
            growth_b = jnp.maximum(wb0 * COS[d] + wb1 * SIN[d] + (1.0 - GROWTH), 1.0)
            out[pl.ds(start + 2 * d + odd, 8, stride=ND), :] = (
                ref[pl.ds(at, 8), :] * gain_a * growth_a
            )
            out[pl.ds(start + 2 * d + 1 - odd, 8, stride=ND), :] = (
                ref[pl.ds(at + 8, 8), :] * gain_b * growth_b
            )
        return coupling * FREQ_STEP**GF, weight + GF / NF

    k = lax.broadcasted_iota(jnp.int32, (8, LANES), 0)
    coupling = jnp.zeros((8, LANES), jnp.float32)
    for i in range(GF):
        for h in range(2):
            value = GROWTH * WIND_COUPLING * FREQ_STEP**i * (1.0 - 2.0 * h)
            coupling = jnp.where(k == 2 * i + h, value, coupling)
    carry = (coupling, freq_weight())
    carry = lax.fori_loop(0, FIRST_GROUPS, functools.partial(one_group, 0, done), carry)
    lax.fori_loop(0, later, functools.partial(one_group, FIRST_GROUPS, turned), carry)


def geometry_table(bands):
    total = 2 * bands

    def angle(position):
        return (LAT_SOUTH + (LAT_NORTH - LAT_SOUTH) * position / total) * (math.pi / 180.0)

    table = np.zeros((bands, 8), np.float32)
    for b in range(bands):
        cells = [angle(2 * b + 0.5), angle(2 * b + 1.5)]
        faces = [angle(2 * b), angle(2 * b + 1), angle(2 * b + 2)]
        icos = [1.0 / math.cos(v) for v in cells]
        near, far = (0, 1) if b % 2 == 0 else (1, 0)
        face_a, face_b = (faces[0], faces[2]) if b % 2 == 0 else (faces[2], faces[0])
        table[b] = [
            icos[0],
            icos[1],
            math.cos(face_a) * icos[near],
            math.cos(faces[1]) * icos[near],
            math.cos(faces[1]) * icos[far],
            math.cos(face_b) * icos[far],
            -TURNING * math.tan(cells[near]),
            -TURNING * math.tan(cells[far]),
        ]
    return table


def speed_table():
    table = np.zeros((2, WIDE), np.float32)
    for k in range(NF * ND):
        value = SPEED_TOP * FREQ_STEP ** -(k // ND) * math.cos(2.0 * math.pi * (k % ND) / ND)
        table[0, 2 * k] = value
        table[1, 2 * k + 1] = value
    return table


VMEM = pl.BlockSpec(memory_space=pltpu.VMEM)
SMEM = pl.BlockSpec(memory_space=pltpu.SMEM)
HBM = pl.BlockSpec(memory_space=pltpu.HBM)
PARAMS = pltpu.CompilerParams(vmem_limit_bytes=40 * 1024 * 1024)


def call(kernel, name, operands, specs, shapes, scratch, micros):
    outs = [jax.ShapeDtypeStruct(s, jnp.float32) for s in shapes]
    return pl.pallas_call(
        kernel,
        name=name,
        out_shape=outs,
        in_specs=specs,
        out_specs=[VMEM] * len(outs),
        scratch_shapes=scratch,
        compiler_params=PARAMS,
        cost_estimate=pl.CostEstimate(
            flops=0, bytes_accessed=int(micros * 3.0e6), transcendentals=0
        ),
    )(*operands)


def swapped(pairs):
    return pairs + [(t, s) for s, t in pairs]


def per_device(bands, spec_count, spectra, sea_mask, wind, current):
    comp_count, row_count, col_count = spectra.shape
    cells = spectra.reshape(comp_count * row_count, col_count)
    middle = bands // 2 - 1
    first_rows = FIRST_GROUPS * GROUP_ROWS
    last_rows = ROWS - first_rows

    (own,) = call(
        pack_kernel,
        "pack_forcing",
        tuple(pltpu.with_memory_space_constraint(v, pltpu.HBM) for v in (wind, current, sea_mask)),
        [HBM] * 3,
        [(5, wind.shape[1], LANES)],
        [
            pltpu.VMEM(wind.shape, jnp.float32),
            pltpu.VMEM(current.shape, jnp.float32),
            pltpu.VMEM(sea_mask.shape, jnp.int32),
            pltpu.SemaphoreType.DMA((3,)),
        ],
        0.3,
    )
    forcing = own + lax.ppermute(own, "band", [(b, b ^ 2) for b in range(bands)])

    rows_after, forcing = lax.optimization_barrier((cells, forcing))
    straight = lax.ppermute(
        rows_after, "band", swapped([(b, b + 1) for b in range(1, bands - 1, 2) if b != middle])
    )
    pairs = [(b, b + 1) for b in range(0, bands, 2)]
    beyond = lax.ppermute(rows_after, "band", swapped(pairs))
    part_relayed, part_direct, west, east = call(
        split_kernel,
        "split",
        tuple(pltpu.with_memory_space_constraint(v, pltpu.HBM) for v in (cells, sea_mask)),
        [HBM, HBM],
        [(first_rows, LANES), (last_rows, LANES), (2, WIDE), (2, WIDE)],
        [
            pltpu.VMEM((ROWS, LANES), jnp.float32),
            pltpu.VMEM(sea_mask.shape, jnp.int32),
            pltpu.VMEM((LANES, LANES), jnp.float32),
            pltpu.SemaphoreType.DMA((4,)),
        ],
        1.0,
    )

    bit = 4
    while bit < bands:
        forcing = forcing + lax.ppermute(forcing, "band", [(b, b ^ bit) for b in range(bands)])
        bit *= 2
    part_relayed, forcing = lax.optimization_barrier((part_relayed, forcing))
    relay = lax.ppermute(part_relayed, "band", [(middle, bands - 1), (middle + 1, 0)])
    forcing = forcing + lax.ppermute(forcing, "band", swapped(pairs))
    part_direct, forcing = lax.optimization_barrier((part_direct, forcing))
    direct = lax.ppermute(
        part_direct, "band", [(middle, middle + 1), (middle + 1, middle)]
    )

    par, west, east = call(
        functools.partial(table_kernel, bands),
        "tables",
        (jnp.asarray(geometry_table(bands)), forcing, west, east),
        [SMEM, VMEM, VMEM, VMEM],
        [(PAR_ROWS, LANES), (2, WIDE), (2, WIDE)],
        [],
        0.3,
    )
    relayed = lax.ppermute(relay, "band", [(bands - 1, middle + 1), (0, middle)])
    ring = [(s, (s + 1) % spec_count) for s in range(spec_count)]
    from_west = lax.ppermute(east, "spec", ring)
    from_east = lax.ppermute(west, "spec", [(t, s) for s, t in ring])
    base_first, base_last = call(
        base_kernel,
        "base",
        (par, cells, beyond),
        [VMEM] * 3,
        [(first_rows, LANES), (last_rows, LANES)],
        [],
        4.0,
    )
    base_first, from_west, from_east = lax.optimization_barrier((base_first, from_west, from_east))
    (fix,) = call(
        fix_kernel,
        "fix",
        (jnp.asarray(speed_table()), par, west, east, from_west, from_east),
        [VMEM] * 6,
        [(WIDE, LANES)],
        [pltpu.VMEM((LANES, WIDE), jnp.float32)],
        1.0,
    )
    turned, total = call(
        functools.partial(first_kernel, bands),
        "first_groups",
        (par, base_first, fix, straight, relayed),
        [VMEM] * 5,
        [(first_rows, LANES), (16, LANES)],
        [],
        1.0,
    )
    (out,) = call(
        functools.partial(last_kernel, bands),
        "last_groups",
        (par, base_last, fix, straight, direct, turned, total),
        [VMEM] * 7,
        [(ROWS, LANES)],
        [pltpu.VMEM((last_rows, LANES), jnp.float32), pltpu.VMEM((16, LANES), jnp.float32)],
        2.0,
    )
    return out.reshape(comp_count, row_count, col_count)


def solution(mesh):
    placed = (
        P(None, "band", "spec"),
        P("band", "spec"),
        P(None, None, ("spec", "band")),
        P(None, None, ("spec", "band")),
    )
    return jax.shard_map(
        functools.partial(per_device, mesh.shape["band"], mesh.shape["spec"]),
        mesh=mesh,
        in_specs=placed,
        out_specs=P(None, "band", "spec"),
        check_vma=False,
    )
```

```python
import functools
import math

import jax
import jax.numpy as jnp
import numpy as np
from jax import lax
from jax.experimental import pallas as pl
from jax.experimental.pallas import tpu as pltpu
from jax.sharding import PartitionSpec as P

NF = 36
ND = 36
HALF = ND // 2
LAT_SOUTH = 30.0
LAT_NORTH = 55.0
SPEED_TOP = 0.35
FREQ_STEP = 1.1
TURNING = 1.5
GROWTH = 0.05
WIND_COUPLING = 0.04

GF = 4
GROUPS = NF // GF
GROUP_ROWS = GF * ND * 2
FIRST_GROUPS = 4
LANES = 128
ROWS = NF * ND * 2
WIDE = -(-(ROWS + 2) // LANES) * LANES

COS = [math.cos(2.0 * math.pi * d / ND) for d in range(HALF + 1)]
SIN = [math.sin(2.0 * math.pi * d / ND) for d in range(HALF + 1)]

(
    CUR_A,
    CUR_M,
    CUR_B,
    CX_A,
    CX_B,
    W0_A,
    W0_B,
    W1_A,
    W1_B,
    SEA_A,
    SEA_B,
    SEA_A1,
    SEA_A2,
    SEA_B1,
    SEA_B2,
    TAU,
    ICOS_A,
    ICOS_B,
    KAP_A,
    MU_A,
    MU_B,
    KAP_B,
    TAN_A,
    TAN_B,
    ICOS_0,
    ICOS_1,
) = range(26)
PAR_ROWS = 32


def flux(lo2, lo1, hi1, hi2, c):
    forward = c >= 0.0
    source = jnp.where(forward, lo1, hi1)
    upwind = jnp.where(forward, lo2, hi2)
    both = lo1 + hi1
    bend = both - 3.0 * source + upwind
    w = (1.0 / 6.0) - (c * c) * (1.0 / 6.0)
    return c * (0.5 * (both - c * (hi1 - lo1)) - w * bend)


def group_speed():
    k = lax.broadcasted_iota(jnp.int32, (8, LANES), 0)
    speed = jnp.zeros((8, LANES), jnp.float32)
    for i in range(GF):
        for h in range(2):
            value = SPEED_TOP * FREQ_STEP**-i * (1.0 - 2.0 * h)
            speed = jnp.where(k == 2 * i + h, value, speed)
    return speed


def freq_weight():
    k = lax.broadcasted_iota(jnp.int32, (8, LANES), 0)
    weight = jnp.zeros((8, LANES), jnp.float32)
    for i in range(GF):
        weight = jnp.where(lax.div(k, 2) == i, (i + 1.0) / NF, weight)
    return weight


def swap_halves(v):
    k = lax.broadcasted_iota(jnp.int32, (8, LANES), 0)
    return jnp.where(lax.rem(k, 2) == 0, pltpu.roll(v, 7, 0), pltpu.roll(v, 1, 0))


def wide_row(par, index):
    return jnp.broadcast_to(par[index : index + 1, :], (8, LANES))


def pack_kernel(wind, current, sea, out, wind_here, current_here, sea_here, sems):
    me = lax.axis_index("band")
    rows, strip = wind.shape[1], wind.shape[2]
    copies = [
        pltpu.make_async_copy(wind, wind_here, sems.at[0]),
        pltpu.make_async_copy(current, current_here, sems.at[1]),
        pltpu.make_async_copy(sea, sea_here, sems.at[2]),
    ]
    for copy in copies:
        copy.start()
    out[4] = jnp.zeros((rows, LANES), jnp.float32)
    empty = jnp.zeros((rows, LANES - strip), jnp.float32)
    for copy in copies:
        copy.wait()
    for part, ref in enumerate((current_here, wind_here)):
        for axis in range(2):
            wide = jnp.concatenate([ref[axis], empty], axis=1)
            out[2 * part + axis] = pltpu.roll(wide, me * strip, 1)
    seas = sea_here[...].astype(jnp.float32)
    out[4, pl.ds(2 * me, 1), :] = seas[0:1]
    out[4, pl.ds(2 * me + 1, 1), :] = seas[1:2]


def split_kernel(source, relayed, direct, sems):
    first = relayed.shape[0]
    parts = [
        pltpu.make_async_copy(source.at[0:first], relayed, sems.at[0]),
        pltpu.make_async_copy(source.at[first:ROWS], direct, sems.at[1]),
    ]
    for part in parts:
        part.start()
    for part in parts:
        part.wait()


def ends_kernel(spectra, sea, west, east, line):
    seas = sea[...].astype(jnp.float32)
    sub = lax.broadcasted_iota(jnp.int32, (LANES, LANES), 0)
    both = jnp.where(
        lax.rem(sub, 2) == 0,
        jnp.broadcast_to(seas[0:1], (LANES, LANES)),
        jnp.broadcast_to(seas[1:2], (LANES, LANES)),
    )
    full = ROWS // LANES
    for block in range(WIDE // LANES):
        at = block * LANES
        if block < full:
            cells = spectra[at : at + LANES, :] * both
        else:
            left = ROWS - at
            line[...] = jnp.zeros((LANES, LANES), jnp.float32)
            line[0:left, :] = spectra[at : at + left, :] * both[0:left]
            cells = line[...]
        turned = cells.T
        west[:, at : at + LANES] = turned[0:2]
        east[:, at : at + LANES] = turned[LANES - 2 : LANES]


def table_kernel(bands, geometry, forcing, west_in, east_in, par, west, east):
    me = lax.axis_index("band")
    is_even = lax.rem(me, 2) == 0
    row = 2 * me
    has_south = jnp.where(me > 0, 1.0, 0.0)
    has_north = jnp.where(me < bands - 1, 1.0, 0.0)

    def around(part):
        south = [jnp.maximum(row - 2, 0), jnp.maximum(row - 1, 0)]
        north = [jnp.minimum(row + 2, 2 * bands - 1), jnp.minimum(row + 3, 2 * bands - 1)]
        return (
            [forcing[part, pl.ds(i, 1), :] * has_south for i in south]
            + [forcing[part, pl.ds(row + i, 1), :] for i in range(2)]
            + [forcing[part, pl.ds(i, 1), :] * has_north for i in north]
        )

    seas = around(4)

    def pick(low, high):
        return jnp.where(is_even, low, high)

    def put(index, value):
        par[index : index + 1, :] = jnp.broadcast_to(value, (1, LANES))

    tau = jnp.where(is_even, 1.0, -1.0)
    north = around(1)
    face = [0.5 * (north[i] + north[i + 1]) for i in range(1, 4)]
    put(CUR_A, tau * pick(face[0], face[2]))
    put(CUR_M, tau * face[1])
    put(CUR_B, tau * pick(face[2], face[0]))
    lane = lax.broadcasted_iota(jnp.int32, (1, LANES), 1)
    inside = jnp.where(lane == 0, 0.0, 1.0)
    east_speed = around(0)[2:4]
    wind_0, wind_1 = around(2)[2:4], around(3)[2:4]
    shifted = [0.5 * inside * (v + pltpu.roll(v, 1, 1)) for v in east_speed]
    put(CX_A, pick(shifted[0], shifted[1]))
    put(CX_B, pick(shifted[1], shifted[0]))
    put(W0_A, pick(wind_0[0], wind_0[1]))
    put(W0_B, pick(wind_0[1], wind_0[0]))
    put(W1_A, pick(wind_1[0], wind_1[1]))
    put(W1_B, pick(wind_1[1], wind_1[0]))
    put(SEA_A, pick(seas[2], seas[3]))
    put(SEA_B, pick(seas[3], seas[2]))
    put(SEA_A1, pick(seas[1], seas[4]))
    put(SEA_A2, pick(seas[0], seas[5]))
    put(SEA_B1, pick(seas[4], seas[1]))
    put(SEA_B2, pick(seas[5], seas[0]))
    put(TAU, tau)
    icos = [geometry[me, 0], geometry[me, 1]]
    put(ICOS_A, inside * pick(icos[0], icos[1]))
    put(ICOS_B, inside * pick(icos[1], icos[0]))
    put(KAP_A, geometry[me, 2])
    put(MU_A, geometry[me, 3])
    put(MU_B, geometry[me, 4])
    put(KAP_B, geometry[me, 5])
    put(TAN_A, geometry[me, 6])
    put(TAN_B, geometry[me, 7])
    put(ICOS_0, icos[0])
    put(ICOS_1, icos[1])
    par[26:32, :] = jnp.zeros((6, LANES), jnp.float32)

    west[...] = west_in[...]
    east[...] = east_in[...]
    for i in range(2):
        west[:, ROWS + i : ROWS + i + 1] = jnp.concatenate(
            [east_speed[i][:, j : j + 1] for j in range(2)], axis=0
        )
        east[:, ROWS + i : ROWS + i + 1] = jnp.concatenate(
            [east_speed[i][:, j : j + 1] for j in (LANES - 2, LANES - 1)], axis=0
        )


def fix_kernel(table, par, west, east, from_west, from_east, fix, tall):
    lane = lax.broadcasted_iota(jnp.int32, (1, WIDE), 1)
    even_row = lax.rem(lane, 2) == 0
    speed = table[0:1] * par[ICOS_0 : ICOS_0 + 1, 0:1] + table[1:2] * par[ICOS_1 : ICOS_1 + 1, 0:1]

    def column(ref, row):
        cells = ref[row : row + 1, :]
        drift = jnp.where(even_row, cells[:, ROWS : ROWS + 1], cells[:, ROWS + 1 : ROWS + 2])
        return cells, drift

    xm2, _ = column(from_west, 0)
    xm1, dm1 = column(from_west, 1)
    x0, d0 = column(west, 0)
    x1, d1 = column(west, 1)
    y2, d2 = column(east, 0)
    y1, dy1 = column(east, 1)
    z0, dz0 = column(from_east, 0)
    z1, _ = column(from_east, 1)
    first = flux(xm2, xm1, x0, x1, speed + 0.5 * (dm1 + d0))
    last = flux(y2, y1, z0, z1, speed + 0.5 * (dy1 + dz0))
    c = speed + 0.5 * (d0 + d1)
    second = jnp.where(c >= 0.0, -c * (1.0 - c * c) * (1.0 / 6.0), 0.0) * (xm1 - y1)
    c = speed + 0.5 * (d2 + dy1)
    before = jnp.where(c >= 0.0, 0.0, -c * (1.0 - c * c) * (1.0 / 6.0)) * (z0 - x0)
    tall[...] = jnp.zeros((LANES, WIDE), jnp.float32)
    tall[0:1, :] = first - second
    tall[1:2, :] = second
    tall[LANES - 2 : LANES - 1, :] = -before
    tall[LANES - 1 : LANES, :] = before - last
    for block in range(WIDE // LANES):
        at = block * LANES
        fix[at : at + LANES, :] = tall[:, at : at + LANES].T


def base_kernel(par, spectra, beyond_first, beyond_last, base_first, base_last):
    odd = lax.rem(lax.axis_index("band"), 2)
    sea_a, sea_b = wide_row(par, SEA_A), wide_row(par, SEA_B)
    sea_b1, sea_b2 = wide_row(par, SEA_B1), wide_row(par, SEA_B2)
    cur_a, cur_m, cur_b = wide_row(par, CUR_A), wide_row(par, CUR_M), wide_row(par, CUR_B)
    cx_a, cx_b = wide_row(par, CX_A), wide_row(par, CX_B)
    kap_a, mu_a = wide_row(par, KAP_A), wide_row(par, MU_A)
    mu_b, kap_b = wide_row(par, MU_B), wide_row(par, KAP_B)
    tau = wide_row(par, TAU)
    icos_a, icos_b = wide_row(par, ICOS_A), wide_row(par, ICOS_B)

    def along_east(x, speed_x, current_x, cosine):
        crossing = flux(
            pltpu.roll(x, 2, 1),
            pltpu.roll(x, 1, 1),
            x,
            pltpu.roll(x, LANES - 1, 1),
            speed_x * cosine + current_x,
        )
        return crossing - pltpu.roll(crossing, LANES - 1, 1)

    def one_group(base, beyond, first, g, speeds):
        start = (first + g) * GROUP_ROWS
        far = g * GROUP_ROWS
        north = speeds * tau
        east_a, east_b = speeds * icos_a, speeds * icos_b
        for d in range(HALF):
            row_a = pl.ds(start + 2 * d + odd, 8, stride=ND)
            row_b = pl.ds(start + 2 * d + 1 - odd, 8, stride=ND)
            a = spectra[row_a, :] * sea_a
            b = spectra[row_b, :] * sea_b
            b1 = beyond[pl.ds(far + 2 * d + odd, 8, stride=ND), :] * sea_b1
            b2 = beyond[pl.ds(far + 2 * d + 1 - odd, 8, stride=ND), :] * sea_b2
            c = north * SIN[d] + cur_a
            w = (1.0 / 6.0) - (c * c) * (1.0 / 6.0)
            flux_a = c * (0.5 * (a - c * a) - w * jnp.where(c >= 0.0, a, b - 2.0 * a))
            flux_m = flux(0.0, a, b, b1, north * SIN[d] + cur_m)
            flux_b = flux(a, b, b1, b2, north * SIN[d] + cur_b)
            to_a = along_east(a, east_a, cx_a, COS[d])
            to_b = along_east(b, east_b, cx_b, COS[d])
            at = pl.multiple_of(g * (HALF * 16) + d * 16, 8)
            base[pl.ds(at, 8), :] = a + to_a + kap_a * flux_a - mu_a * flux_m
            base[pl.ds(at + 8, 8), :] = b + to_b + mu_b * flux_m - kap_b * flux_b
        return speeds * FREQ_STEP**-GF

    speeds = lax.fori_loop(
        0, FIRST_GROUPS, functools.partial(one_group, base_first, beyond_first, 0), group_speed()
    )
    lax.fori_loop(
        0,
        GROUPS - FIRST_GROUPS,
        functools.partial(one_group, base_last, beyond_last, FIRST_GROUPS),
        speeds,
    )


def turn(cells, rate):
    after = [swap_halves(cells[0]), swap_halves(cells[1])]
    lower = swap_halves(cells[HALF - 1])
    ring = [lower] + cells + after
    fluxes = []
    for d in range(HALF):
        mean = 0.5 * (COS[d] + COS[d + 1])
        fluxes.append(flux(ring[d], ring[d + 1], ring[d + 2], ring[d + 3], rate * mean))
    last = swap_halves(fluxes[HALF - 1])
    return [cells[d] - (fluxes[d] - (fluxes[d - 1] if d else last)) for d in range(HALF)]


def finish_groups(first, count, skip, par, base, fix, ahead, turned, total):
    odd = lax.rem(lax.axis_index("band"), 2)
    sea_a1, sea_a2 = wide_row(par, SEA_A1), wide_row(par, SEA_A2)
    cur_a, cur_m = wide_row(par, CUR_A), wide_row(par, CUR_M)
    kap_a, mu_a, mu_b = wide_row(par, KAP_A), wide_row(par, MU_A), wide_row(par, MU_B)
    tau = wide_row(par, TAU)
    tan_a, tan_b = wide_row(par, TAN_A), wide_row(par, TAN_B)

    def one_group(g, carry):
        speeds, weight, sum_a, sum_b = carry
        start = (skip + g) * GROUP_ROWS
        fix_start = (first + g) * GROUP_ROWS
        north = speeds * tau
        cells_a, cells_b = [], []
        for d in range(HALF):
            n1 = ahead[pl.ds(start + 2 * d + 1 - odd, 8, stride=ND), :] * sea_a1
            n2 = ahead[pl.ds(start + 2 * d + odd, 8, stride=ND), :] * sea_a2
            fix_a = fix[pl.ds(fix_start + 2 * d + odd, 8, stride=ND), :]
            fix_b = fix[pl.ds(fix_start + 2 * d + 1 - odd, 8, stride=ND), :]
            c = north * SIN[d] + cur_a
            w = (1.0 / 6.0) - (c * c) * (1.0 / 6.0)
            flux_a = c * (0.5 * (n1 + c * n1) - w * jnp.where(c >= 0.0, n2 - 2.0 * n1, n1))
            c = north * SIN[d] + cur_m
            w = (c * c) * (1.0 / 6.0) - (1.0 / 6.0)
            flux_m = jnp.where(c >= 0.0, c * w, 0.0) * n1
            at = pl.multiple_of(g * (HALF * 16) + d * 16, 8)
            cells_a.append(base[pl.ds(at, 8), :] + fix_a + kap_a * flux_a - mu_a * flux_m)
            cells_b.append(base[pl.ds(at + 8, 8), :] + fix_b + mu_b * flux_m)
        square_a = square_b = 0.0
        for d, v in enumerate(turn(cells_a, speeds * tan_a)):
            at = pl.multiple_of(g * (HALF * 16) + d * 16, 8)
            turned[pl.ds(at, 8), :] = v
            square_a = square_a + v * v
        for d, v in enumerate(turn(cells_b, speeds * tan_b)):
            at = pl.multiple_of(g * (HALF * 16) + d * 16 + 8, 8)
            turned[pl.ds(at, 8), :] = v
            square_b = square_b + v * v
        return (
            speeds * FREQ_STEP**-GF,
            weight + GF / NF,
            sum_a + weight * square_a,
            sum_b + weight * square_b,
        )

    speeds = group_speed() * FREQ_STEP ** -(GF * first)
    weight = freq_weight() + GF * first / NF
    carry = (speeds, weight, total[0:8, :], total[8:16, :])
    _, _, total[0:8, :], total[8:16, :] = lax.fori_loop(0, count, one_group, carry)


def finish_either(bands, first, count, par, base, fix, straight, split, turned, total):
    me = lax.axis_index("band")
    middle = jnp.logical_or(me == bands // 2 - 1, me == bands // 2)

    @pl.when(middle)
    def _():
        finish_groups(first, count, 0, par, base, fix, split, turned, total)

    @pl.when(jnp.logical_not(middle))
    def _():
        finish_groups(first, count, first, par, base, fix, straight, turned, total)


def first_kernel(bands, par, base, fix, straight, split, turned, total):
    total[...] = jnp.zeros((16, LANES), jnp.float32)
    finish_either(bands, 0, FIRST_GROUPS, par, base, fix, straight, split, turned, total)


def last_kernel(bands, par, base, fix, straight, split, done, before, out, turned, total):
    odd = lax.rem(lax.axis_index("band"), 2)
    later = GROUPS - FIRST_GROUPS
    total[...] = before[...]
    finish_either(bands, FIRST_GROUPS, later, par, base, fix, straight, split, turned, total)
    scale = 2.0 / (NF * ND)
    steep_a = jnp.sum(total[0:8, :], axis=0, keepdims=True) * scale
    steep_b = jnp.sum(total[8:16, :], axis=0, keepdims=True) * scale
    sea_a, sea_b = wide_row(par, SEA_A), wide_row(par, SEA_B)
    w0_a, w0_b = wide_row(par, W0_A), wide_row(par, W0_B)
    w1_a, w1_b = wide_row(par, W1_A), wide_row(par, W1_B)

    def one_group(first, ref, g, carry):
        coupling, weight = carry
        start = (first + g) * GROUP_ROWS
        gain_a = sea_a / (1.0 + weight * steep_a)
        gain_b = sea_b / (1.0 + weight * steep_b)
        wa0, wa1 = w0_a * coupling, w1_a * coupling
        wb0, wb1 = w0_b * coupling, w1_b * coupling
        for d in range(HALF):
            at = pl.multiple_of(g * (HALF * 16) + d * 16, 8)
            growth_a = jnp.maximum(wa0 * COS[d] + wa1 * SIN[d] + (1.0 - GROWTH), 1.0)
            growth_b = jnp.maximum(wb0 * COS[d] + wb1 * SIN[d] + (1.0 - GROWTH), 1.0)
            out[pl.ds(start + 2 * d + odd, 8, stride=ND), :] = (
                ref[pl.ds(at, 8), :] * gain_a * growth_a
            )
            out[pl.ds(start + 2 * d + 1 - odd, 8, stride=ND), :] = (
                ref[pl.ds(at + 8, 8), :] * gain_b * growth_b
            )
        return coupling * FREQ_STEP**GF, weight + GF / NF

    k = lax.broadcasted_iota(jnp.int32, (8, LANES), 0)
    coupling = jnp.zeros((8, LANES), jnp.float32)
    for i in range(GF):
        for h in range(2):
            value = GROWTH * WIND_COUPLING * FREQ_STEP**i * (1.0 - 2.0 * h)
            coupling = jnp.where(k == 2 * i + h, value, coupling)
    carry = (coupling, freq_weight())
    carry = lax.fori_loop(0, FIRST_GROUPS, functools.partial(one_group, 0, done), carry)
    lax.fori_loop(0, later, functools.partial(one_group, FIRST_GROUPS, turned), carry)


def geometry_table(bands):
    total = 2 * bands

    def angle(position):
        return (LAT_SOUTH + (LAT_NORTH - LAT_SOUTH) * position / total) * (math.pi / 180.0)

    table = np.zeros((bands, 8), np.float32)
    for b in range(bands):
        cells = [angle(2 * b + 0.5), angle(2 * b + 1.5)]
        faces = [angle(2 * b), angle(2 * b + 1), angle(2 * b + 2)]
        icos = [1.0 / math.cos(v) for v in cells]
        near, far = (0, 1) if b % 2 == 0 else (1, 0)
        face_a, face_b = (faces[0], faces[2]) if b % 2 == 0 else (faces[2], faces[0])
        table[b] = [
            icos[0],
            icos[1],
            math.cos(face_a) * icos[near],
            math.cos(faces[1]) * icos[near],
            math.cos(faces[1]) * icos[far],
            math.cos(face_b) * icos[far],
            -TURNING * math.tan(cells[near]),
            -TURNING * math.tan(cells[far]),
        ]
    return table


def speed_table():
    table = np.zeros((2, WIDE), np.float32)
    for k in range(NF * ND):
        value = SPEED_TOP * FREQ_STEP ** -(k // ND) * math.cos(2.0 * math.pi * (k % ND) / ND)
        table[0, 2 * k] = value
        table[1, 2 * k + 1] = value
    return table


VMEM = pl.BlockSpec(memory_space=pltpu.VMEM)
SMEM = pl.BlockSpec(memory_space=pltpu.SMEM)
HBM = pl.BlockSpec(memory_space=pltpu.HBM)
PARAMS = pltpu.CompilerParams(vmem_limit_bytes=40 * 1024 * 1024)


def call(kernel, name, operands, specs, shapes, scratch, micros):
    outs = [jax.ShapeDtypeStruct(s, jnp.float32) for s in shapes]
    return pl.pallas_call(
        kernel,
        name=name,
        out_shape=outs,
        in_specs=specs,
        out_specs=[VMEM] * len(outs),
        scratch_shapes=scratch,
        compiler_params=PARAMS,
        cost_estimate=pl.CostEstimate(
            flops=0, bytes_accessed=int(micros * 3.0e6), transcendentals=0
        ),
    )(*operands)


def swapped(pairs):
    return pairs + [(t, s) for s, t in pairs]


def per_device(bands, spec_count, spectra, sea_mask, wind, current):
    comp_count, row_count, col_count = spectra.shape
    cells = spectra.reshape(comp_count * row_count, col_count)
    middle = bands // 2 - 1
    first_rows = FIRST_GROUPS * GROUP_ROWS
    last_rows = ROWS - first_rows

    (own,) = call(
        pack_kernel,
        "pack_forcing",
        tuple(pltpu.with_memory_space_constraint(v, pltpu.HBM) for v in (wind, current, sea_mask)),
        [HBM] * 3,
        [(5, wind.shape[1], LANES)],
        [
            pltpu.VMEM(wind.shape, jnp.float32),
            pltpu.VMEM(current.shape, jnp.float32),
            pltpu.VMEM(sea_mask.shape, jnp.int32),
            pltpu.SemaphoreType.DMA((3,)),
        ],
        0.3,
    )
    forcing = own + lax.ppermute(own, "band", [(b, b ^ 2) for b in range(bands)])

    part_relayed, part_direct = call(
        split_kernel,
        "split",
        (pltpu.with_memory_space_constraint(cells, pltpu.HBM),),
        [HBM],
        [(first_rows, LANES), (last_rows, LANES)],
        [pltpu.SemaphoreType.DMA((2,))],
        1.0,
    )
    part_relayed, part_direct, forcing, rows_after = lax.optimization_barrier(
        (part_relayed, part_direct, forcing, cells)
    )
    straight = lax.ppermute(
        rows_after, "band", swapped([(b, b + 1) for b in range(1, bands - 1, 2) if b != middle])
    )
    west, east = call(
        ends_kernel,
        "ends",
        (cells, sea_mask),
        [VMEM] * 2,
        [(2, WIDE), (2, WIDE)],
        [pltpu.VMEM((LANES, LANES), jnp.float32)],
        1.0,
    )
    bit = 4
    while bit < bands:
        forcing = forcing + lax.ppermute(forcing, "band", [(b, b ^ bit) for b in range(bands)])
        bit *= 2
    part_relayed, part_direct, forcing, west, east = lax.optimization_barrier(
        (part_relayed, part_direct, forcing, west, east)
    )
    relay = lax.ppermute(part_relayed, "band", [(middle, bands - 1), (middle + 1, 0)])
    pairs = [(b, b + 1) for b in range(0, bands, 2)]
    forcing = forcing + lax.ppermute(forcing, "band", swapped(pairs))
    beyond = [lax.ppermute(part, "band", swapped(pairs)) for part in (part_relayed, part_direct)]
    part_direct, forcing = lax.optimization_barrier((part_direct, forcing))
    direct = lax.ppermute(
        part_direct, "band", [(middle, middle + 1), (middle + 1, middle)]
    )

    par, west, east = call(
        functools.partial(table_kernel, bands),
        "tables",
        (jnp.asarray(geometry_table(bands)), forcing, west, east),
        [SMEM, VMEM, VMEM, VMEM],
        [(PAR_ROWS, LANES), (2, WIDE), (2, WIDE)],
        [],
        0.3,
    )
    relay, par = lax.optimization_barrier((relay, par))
    relayed = lax.ppermute(relay, "band", [(bands - 1, middle + 1), (0, middle)])
    ring = [(s, (s + 1) % spec_count) for s in range(spec_count)]
    from_west = lax.ppermute(east, "spec", ring)
    from_east = lax.ppermute(west, "spec", [(t, s) for s, t in ring])
    base_first, base_last = call(
        base_kernel,
        "base",
        (par, cells, *beyond),
        [VMEM] * 4,
        [(first_rows, LANES), (last_rows, LANES)],
        [],
        4.0,
    )
    base_first, from_west, from_east = lax.optimization_barrier((base_first, from_west, from_east))
    (fix,) = call(
        fix_kernel,
        "fix",
        (jnp.asarray(speed_table()), par, west, east, from_west, from_east),
        [VMEM] * 6,
        [(WIDE, LANES)],
        [pltpu.VMEM((LANES, WIDE), jnp.float32)],
        1.0,
    )
    turned, total = call(
        functools.partial(first_kernel, bands),
        "first_groups",
        (par, base_first, fix, straight, relayed),
        [VMEM] * 5,
        [(first_rows, LANES), (16, LANES)],
        [],
        1.0,
    )
    (out,) = call(
        functools.partial(last_kernel, bands),
        "last_groups",
        (par, base_last, fix, straight, direct, turned, total),
        [VMEM] * 7,
        [(ROWS, LANES)],
        [pltpu.VMEM((last_rows, LANES), jnp.float32), pltpu.VMEM((16, LANES), jnp.float32)],
        2.0,
    )
    return out.reshape(comp_count, row_count, col_count)


def solution(mesh):
    placed = (
        P(None, "band", "spec"),
        P("band", "spec"),
        P(None, None, ("spec", "band")),
        P(None, None, ("spec", "band")),
    )
    return jax.shard_map(
        functools.partial(per_device, mesh.shape["band"], mesh.shape["spec"]),
        mesh=mesh,
        in_specs=placed,
        out_specs=P(None, "band", "spec"),
        check_vma=False,
    )
```

```python
import functools
import math

import jax
import jax.numpy as jnp
import numpy as np
from jax import lax
from jax.experimental import pallas as pl
from jax.experimental.pallas import tpu as pltpu
from jax.sharding import PartitionSpec as P

NF = 36
ND = 36
HALF = ND // 2
LAT_SOUTH = 30.0
LAT_NORTH = 55.0
SPEED_TOP = 0.35
FREQ_STEP = 1.1
TURNING = 1.5
GROWTH = 0.05
WIND_COUPLING = 0.04

GF = 4
GROUPS = NF // GF
GROUP_ROWS = GF * ND * 2
FIRST_GROUPS = 4
LANES = 128
ROWS = NF * ND * 2
WIDE = -(-(ROWS + 2) // LANES) * LANES

COS = [math.cos(2.0 * math.pi * d / ND) for d in range(HALF + 1)]
SIN = [math.sin(2.0 * math.pi * d / ND) for d in range(HALF + 1)]

(
    CUR_A,
    CUR_M,
    CUR_B,
    CX_A,
    CX_B,
    W0_A,
    W0_B,
    W1_A,
    W1_B,
    SEA_A,
    SEA_B,
    SEA_A1,
    SEA_A2,
    SEA_B1,
    SEA_B2,
    TAU,
    ICOS_A,
    ICOS_B,
    KAP_A,
    MU_A,
    MU_B,
    KAP_B,
    TAN_A,
    TAN_B,
    ICOS_0,
    ICOS_1,
) = range(26)
PAR_ROWS = 32


def flux(lo2, lo1, hi1, hi2, c):
    forward = c >= 0.0
    source = jnp.where(forward, lo1, hi1)
    upwind = jnp.where(forward, lo2, hi2)
    both = lo1 + hi1
    bend = both - 3.0 * source + upwind
    w = (1.0 / 6.0) - (c * c) * (1.0 / 6.0)
    return c * (0.5 * (both - c * (hi1 - lo1)) - w * bend)


def group_speed():
    k = lax.broadcasted_iota(jnp.int32, (8, LANES), 0)
    speed = jnp.zeros((8, LANES), jnp.float32)
    for i in range(GF):
        for h in range(2):
            value = SPEED_TOP * FREQ_STEP**-i * (1.0 - 2.0 * h)
            speed = jnp.where(k == 2 * i + h, value, speed)
    return speed


def freq_weight():
    k = lax.broadcasted_iota(jnp.int32, (8, LANES), 0)
    weight = jnp.zeros((8, LANES), jnp.float32)
    for i in range(GF):
        weight = jnp.where(lax.div(k, 2) == i, (i + 1.0) / NF, weight)
    return weight


def swap_halves(v):
    k = lax.broadcasted_iota(jnp.int32, (8, LANES), 0)
    return jnp.where(lax.rem(k, 2) == 0, pltpu.roll(v, 7, 0), pltpu.roll(v, 1, 0))


def wide_row(par, index):
    return jnp.broadcast_to(par[index : index + 1, :], (8, LANES))


def pack_kernel(wind, current, sea, out, wind_here, current_here, sea_here, sems):
    rows, strip = wind.shape[1], wind.shape[2]
    copies = [
        pltpu.make_async_copy(wind, wind_here, sems.at[0]),
        pltpu.make_async_copy(current, current_here, sems.at[1]),
        pltpu.make_async_copy(sea, sea_here, sems.at[2]),
    ]
    for copy in copies:
        copy.start()
    empty = jnp.zeros((8, LANES - strip), jnp.float32)
    for copy in copies:
        copy.wait()
    packed = jnp.zeros((8, LANES), jnp.float32)
    piece = 0
    for ref in (current_here, wind_here):
        for axis in range(2):
            for row in range(0, rows, 8):
                wide = jnp.concatenate([ref[axis, row : row + 8, :], empty], axis=1)
                packed = packed + (pltpu.roll(wide, piece * strip, 1) if piece else wide)
                piece += 1
    out[0:8, :] = packed
    out[8:10, :] = sea_here[...].astype(jnp.float32)
    out[10:16, :] = jnp.zeros((6, LANES), jnp.float32)


def split_kernel(source, own, relayed, direct, sems):
    del own
    first = relayed.shape[0]
    parts = [
        pltpu.make_async_copy(source.at[0:first], relayed, sems.at[0]),
        pltpu.make_async_copy(source.at[first:ROWS], direct, sems.at[1]),
    ]
    for part in parts:
        part.start()
    for part in parts:
        part.wait()


def ends_kernel(spectra, sea, west, east, line):
    seas = sea[...].astype(jnp.float32)
    sub = lax.broadcasted_iota(jnp.int32, (LANES, LANES), 0)
    both = jnp.where(
        lax.rem(sub, 2) == 0,
        jnp.broadcast_to(seas[0:1], (LANES, LANES)),
        jnp.broadcast_to(seas[1:2], (LANES, LANES)),
    )
    full = ROWS // LANES
    for block in range(WIDE // LANES):
        at = block * LANES
        if block < full:
            cells = spectra[at : at + LANES, :] * both
        else:
            left = ROWS - at
            line[...] = jnp.zeros((LANES, LANES), jnp.float32)
            line[0:left, :] = spectra[at : at + left, :] * both[0:left]
            cells = line[...]
        turned = cells.T
        west[:, at : at + LANES] = turned[0:2]
        east[:, at : at + LANES] = turned[LANES - 2 : LANES]


def table_kernel(bands, order, geometry, slots, west_in, east_in, par, west, east, line):
    me = lax.axis_index("band")
    is_even = lax.rem(me, 2) == 0
    rows = 2 * bands
    strip = LANES // bands
    block = lax.div(lax.broadcasted_iota(jnp.int32, (8, LANES), 1), strip)
    sources = [jnp.bitwise_xor(me, r) for r in order]
    moved = [
        pltpu.roll(slots[16 * k : 16 * k + 8, :], source * strip, 1)
        for k, source in enumerate(sources)
    ]
    for piece in range(rows // 2):
        row = jnp.zeros((8, LANES), jnp.float32)
        for source, values in zip(sources, moved):
            row = jnp.where(block == lax.rem(source + piece, bands), values, row)
        line[8 * piece : 8 * piece + 8, :] = (
            pltpu.roll(row, LANES - piece * strip, 1) if piece else row
        )

    def mask_of(band):
        found = jnp.zeros((2, LANES), jnp.float32)
        for k, source in enumerate(sources):
            found = jnp.where(source == band, slots[16 * k + 8 : 16 * k + 10, :], found)
        return [found[0:1], found[1:2]]

    seas = mask_of(me - 1) + mask_of(me) + mask_of(me + 1)
    row = 2 * me
    has_south = jnp.where(me > 0, 1.0, 0.0)
    has_north = jnp.where(me < bands - 1, 1.0, 0.0)

    def around(part):
        first = part * rows
        south = line[pl.ds(first + jnp.maximum(row - 1, 0), 1), :] * has_south
        north = line[pl.ds(first + jnp.minimum(row + 2, rows - 1), 1), :] * has_north
        return [south] + [line[pl.ds(first + row + i, 1), :] for i in range(2)] + [north]

    def pick(low, high):
        return jnp.where(is_even, low, high)

    def put(index, value):
        par[index : index + 1, :] = jnp.broadcast_to(value, (1, LANES))

    tau = jnp.where(is_even, 1.0, -1.0)
    north = around(1)
    face = [0.5 * (north[i] + north[i + 1]) for i in range(3)]
    put(CUR_A, tau * pick(face[0], face[2]))
    put(CUR_M, tau * face[1])
    put(CUR_B, tau * pick(face[2], face[0]))
    lane = lax.broadcasted_iota(jnp.int32, (1, LANES), 1)
    inside = jnp.where(lane == 0, 0.0, 1.0)
    east_speed = around(0)[1:3]
    wind_0, wind_1 = around(2)[1:3], around(3)[1:3]
    shifted = [0.5 * inside * (v + pltpu.roll(v, 1, 1)) for v in east_speed]
    put(CX_A, pick(shifted[0], shifted[1]))
    put(CX_B, pick(shifted[1], shifted[0]))
    put(W0_A, pick(wind_0[0], wind_0[1]))
    put(W0_B, pick(wind_0[1], wind_0[0]))
    put(W1_A, pick(wind_1[0], wind_1[1]))
    put(W1_B, pick(wind_1[1], wind_1[0]))
    put(SEA_A, pick(seas[2], seas[3]))
    put(SEA_B, pick(seas[3], seas[2]))
    put(SEA_A1, pick(seas[1], seas[4]))
    put(SEA_A2, pick(seas[0], seas[5]))
    put(SEA_B1, pick(seas[4], seas[1]))
    put(SEA_B2, pick(seas[5], seas[0]))
    put(TAU, tau)
    icos = [geometry[me, 0], geometry[me, 1]]
    put(ICOS_A, inside * pick(icos[0], icos[1]))
    put(ICOS_B, inside * pick(icos[1], icos[0]))
    put(KAP_A, geometry[me, 2])
    put(MU_A, geometry[me, 3])
    put(MU_B, geometry[me, 4])
    put(KAP_B, geometry[me, 5])
    put(TAN_A, geometry[me, 6])
    put(TAN_B, geometry[me, 7])
    put(ICOS_0, icos[0])
    put(ICOS_1, icos[1])
    par[26:32, :] = jnp.zeros((6, LANES), jnp.float32)

    west[...] = west_in[...]
    east[...] = east_in[...]
    for i in range(2):
        west[:, ROWS + i : ROWS + i + 1] = jnp.concatenate(
            [east_speed[i][:, j : j + 1] for j in range(2)], axis=0
        )
        east[:, ROWS + i : ROWS + i + 1] = jnp.concatenate(
            [east_speed[i][:, j : j + 1] for j in (LANES - 2, LANES - 1)], axis=0
        )


def fix_kernel(table, par, west, east, from_west, from_east, fix, tall):
    lane = lax.broadcasted_iota(jnp.int32, (1, WIDE), 1)
    even_row = lax.rem(lane, 2) == 0
    speed = table[0:1] * par[ICOS_0 : ICOS_0 + 1, 0:1] + table[1:2] * par[ICOS_1 : ICOS_1 + 1, 0:1]

    def column(ref, row):
        cells = ref[row : row + 1, :]
        drift = jnp.where(even_row, cells[:, ROWS : ROWS + 1], cells[:, ROWS + 1 : ROWS + 2])
        return cells, drift

    xm2, _ = column(from_west, 0)
    xm1, dm1 = column(from_west, 1)
    x0, d0 = column(west, 0)
    x1, d1 = column(west, 1)
    y2, d2 = column(east, 0)
    y1, dy1 = column(east, 1)
    z0, dz0 = column(from_east, 0)
    z1, _ = column(from_east, 1)
    first = flux(xm2, xm1, x0, x1, speed + 0.5 * (dm1 + d0))
    last = flux(y2, y1, z0, z1, speed + 0.5 * (dy1 + dz0))
    c = speed + 0.5 * (d0 + d1)
    second = jnp.where(c >= 0.0, -c * (1.0 - c * c) * (1.0 / 6.0), 0.0) * (xm1 - y1)
    c = speed + 0.5 * (d2 + dy1)
    before = jnp.where(c >= 0.0, 0.0, -c * (1.0 - c * c) * (1.0 / 6.0)) * (z0 - x0)
    tall[...] = jnp.zeros((LANES, WIDE), jnp.float32)
    tall[0:1, :] = first - second
    tall[1:2, :] = second
    tall[LANES - 2 : LANES - 1, :] = -before
    tall[LANES - 1 : LANES, :] = before - last
    for block in range(WIDE // LANES):
        at = block * LANES
        fix[at : at + LANES, :] = tall[:, at : at + LANES].T


def base_kernel(par, spectra, beyond_first, beyond_last, base_first, base_last, gain_first, gain_last):
    odd = lax.rem(lax.axis_index("band"), 2)
    sea_a, sea_b = wide_row(par, SEA_A), wide_row(par, SEA_B)
    sea_b1, sea_b2 = wide_row(par, SEA_B1), wide_row(par, SEA_B2)
    sea_a1 = wide_row(par, SEA_A1)
    into_a1 = wide_row(par, KAP_A) * sea_a1
    into_a2 = wide_row(par, KAP_A) * wide_row(par, SEA_A2)
    over_a, over_b = wide_row(par, MU_A) * sea_a1, wide_row(par, MU_B) * sea_a1
    cur_a, cur_m, cur_b = wide_row(par, CUR_A), wide_row(par, CUR_M), wide_row(par, CUR_B)
    cx_a, cx_b = wide_row(par, CX_A), wide_row(par, CX_B)
    kap_a, mu_a = wide_row(par, KAP_A), wide_row(par, MU_A)
    mu_b, kap_b = wide_row(par, MU_B), wide_row(par, KAP_B)
    tau = wide_row(par, TAU)
    icos_a, icos_b = wide_row(par, ICOS_A), wide_row(par, ICOS_B)

    def along_east(x, speed_x, current_x, cosine):
        crossing = flux(
            pltpu.roll(x, 2, 1),
            pltpu.roll(x, 1, 1),
            x,
            pltpu.roll(x, LANES - 1, 1),
            speed_x * cosine + current_x,
        )
        return crossing - pltpu.roll(crossing, LANES - 1, 1)

    def one_group(base, gain, beyond, first, g, speeds):
        start = (first + g) * GROUP_ROWS
        far = g * GROUP_ROWS
        north = speeds * tau
        east_a, east_b = speeds * icos_a, speeds * icos_b
        for d in range(HALF):
            row_a = pl.ds(start + 2 * d + odd, 8, stride=ND)
            row_b = pl.ds(start + 2 * d + 1 - odd, 8, stride=ND)
            a = spectra[row_a, :] * sea_a
            b = spectra[row_b, :] * sea_b
            b1 = beyond[pl.ds(far + 2 * d + odd, 8, stride=ND), :] * sea_b1
            b2 = beyond[pl.ds(far + 2 * d + 1 - odd, 8, stride=ND), :] * sea_b2
            c = north * SIN[d] + cur_a
            w = (1.0 / 6.0) - (c * c) * (1.0 / 6.0)
            inward = c >= 0.0
            cw = c * w
            half = 0.5 * c
            flux_a = (half - half * c) * a - cw * jnp.where(inward, a, b - 2.0 * a)
            cm = north * SIN[d] + cur_m
            flux_m = flux(0.0, a, b, b1, cm)
            away = jnp.where(cm >= 0.0, cm * ((cm * cm) * (1.0 / 6.0) - (1.0 / 6.0)), 0.0)
            flux_b = flux(a, b, b1, b2, north * SIN[d] + cur_b)
            to_a = along_east(a, east_a, cx_a, COS[d])
            to_b = along_east(b, east_b, cx_b, COS[d])
            at = pl.multiple_of(g * (HALF * 16) + d * 16, 8)
            base[pl.ds(at, 8), :] = a + to_a + kap_a * flux_a - mu_a * flux_m
            base[pl.ds(at + 8, 8), :] = b + to_b + mu_b * flux_m - kap_b * flux_b
            at = pl.multiple_of(g * (HALF * 24) + d * 24, 8)
            near = half + half * c + jnp.where(inward, 2.0 * cw, -cw)
            gain[pl.ds(at, 8), :] = into_a1 * near - over_a * away
            gain[pl.ds(at + 8, 8), :] = into_a2 * jnp.where(inward, -cw, 0.0)
            gain[pl.ds(at + 16, 8), :] = over_b * away
        return speeds * FREQ_STEP**-GF

    speeds = lax.fori_loop(
        0, FIRST_GROUPS, functools.partial(one_group, base_first, gain_first, beyond_first, 0), group_speed()
    )
    lax.fori_loop(
        0,
        GROUPS - FIRST_GROUPS,
        functools.partial(one_group, base_last, gain_last, beyond_last, FIRST_GROUPS),
        speeds,
    )


def turn(cells, rate):
    k = lax.broadcasted_iota(jnp.int32, (8, LANES), 0)
    first = lax.rem(k, 2) == 0
    cube = rate * rate * rate
    ring = [swap_halves(cells[HALF - 1])] + cells
    ring = ring + [swap_halves(cells[0]), swap_halves(cells[1])]
    steps = [high - low for low, high in zip(ring, ring[1:])]
    bends = [high - low for low, high in zip(steps, steps[1:])]
    fluxes = []
    for d in range(HALF):
        mean = 0.5 * (COS[d] + COS[d + 1])
        low, high = (bends[d + 1], bends[d]) if mean > 0 else (bends[d], bends[d + 1])
        bend = jnp.where(first, low, high)
        both = ring[d + 1] + ring[d + 2]
        weight = rate * (mean / 6.0) - cube * (mean**3 / 6.0)
        fluxes.append(
            (rate * (0.5 * mean)) * (both - (rate * mean) * steps[d + 1]) - weight * bend
        )
    last = swap_halves(fluxes[HALF - 1])
    return [cells[d] - (fluxes[d] - (fluxes[d - 1] if d else last)) for d in range(HALF)]


def finish_groups(first, count, skip, par, base, gain, fix, ahead, turned, total):
    odd = lax.rem(lax.axis_index("band"), 2)
    tan_a, tan_b = wide_row(par, TAN_A), wide_row(par, TAN_B)

    def one_group(g, carry):
        speeds, weight, sum_a, sum_b = carry
        start = (skip + g) * GROUP_ROWS
        fix_start = (first + g) * GROUP_ROWS
        cells_a, cells_b = [], []
        for d in range(HALF):
            n1 = ahead[pl.ds(start + 2 * d + 1 - odd, 8, stride=ND), :]
            n2 = ahead[pl.ds(start + 2 * d + odd, 8, stride=ND), :]
            fix_a = fix[pl.ds(fix_start + 2 * d + odd, 8, stride=ND), :]
            fix_b = fix[pl.ds(fix_start + 2 * d + 1 - odd, 8, stride=ND), :]
            at = pl.multiple_of(g * (HALF * 16) + d * 16, 8)
            by = pl.multiple_of(g * (HALF * 24) + d * 24, 8)
            cells_a.append(
                base[pl.ds(at, 8), :]
                + fix_a
                + gain[pl.ds(by, 8), :] * n1
                + gain[pl.ds(by + 8, 8), :] * n2
            )
            cells_b.append(base[pl.ds(at + 8, 8), :] + fix_b + gain[pl.ds(by + 16, 8), :] * n1)
        square_a = square_b = 0.0
        for d, v in enumerate(turn(cells_a, speeds * tan_a)):
            at = pl.multiple_of(g * (HALF * 16) + d * 16, 8)
            turned[pl.ds(at, 8), :] = v
            square_a = square_a + v * v
        for d, v in enumerate(turn(cells_b, speeds * tan_b)):
            at = pl.multiple_of(g * (HALF * 16) + d * 16 + 8, 8)
            turned[pl.ds(at, 8), :] = v
            square_b = square_b + v * v
        return (
            speeds * FREQ_STEP**-GF,
            weight + GF / NF,
            sum_a + weight * square_a,
            sum_b + weight * square_b,
        )

    speeds = group_speed() * FREQ_STEP ** -(GF * first)
    weight = freq_weight() + GF * first / NF
    carry = (speeds, weight, total[0:8, :], total[8:16, :])
    _, _, total[0:8, :], total[8:16, :] = lax.fori_loop(0, count, one_group, carry)


def finish_either(bands, first, count, par, base, gain, fix, straight, split, turned, total):
    me = lax.axis_index("band")
    middle = jnp.logical_or(me == bands // 2 - 1, me == bands // 2)

    @pl.when(middle)
    def _():
        finish_groups(first, count, 0, par, base, gain, fix, split, turned, total)

    @pl.when(jnp.logical_not(middle))
    def _():
        finish_groups(first, count, first, par, base, gain, fix, straight, turned, total)


def first_kernel(bands, par, base, gain, fix, straight, split, turned, total):
    total[...] = jnp.zeros((16, LANES), jnp.float32)
    finish_either(bands, 0, FIRST_GROUPS, par, base, gain, fix, straight, split, turned, total)


def last_kernel(
    bands, par, base, gain, fix, straight, split, done, before, result, turned, total, out, sems
):
    odd = lax.rem(lax.axis_index("band"), 2)
    later = GROUPS - FIRST_GROUPS
    total[...] = before[...]
    finish_either(bands, FIRST_GROUPS, later, par, base, gain, fix, straight, split, turned, total)
    scale = 2.0 / (NF * ND)
    steep_a = jnp.sum(total[0:8, :], axis=0, keepdims=True) * scale
    steep_b = jnp.sum(total[8:16, :], axis=0, keepdims=True) * scale
    sea_a, sea_b = wide_row(par, SEA_A), wide_row(par, SEA_B)
    w0_a, w0_b = wide_row(par, W0_A), wide_row(par, W0_B)
    w1_a, w1_b = wide_row(par, W1_A), wide_row(par, W1_B)

    def copy_out(g):
        rows = pl.ds(pl.multiple_of(g * GROUP_ROWS, 8), GROUP_ROWS)
        return pltpu.make_async_copy(out.at[rows], result.at[rows], sems.at[g])

    def one_group(first, ref, g, carry):
        coupling, weight = carry
        start = (first + g) * GROUP_ROWS
        gain_a = sea_a / (1.0 + weight * steep_a)
        gain_b = sea_b / (1.0 + weight * steep_b)
        wa0, wa1 = w0_a * coupling, w1_a * coupling
        wb0, wb1 = w0_b * coupling, w1_b * coupling
        for d in range(HALF):
            at = pl.multiple_of(g * (HALF * 16) + d * 16, 8)
            growth_a = jnp.maximum(wa0 * COS[d] + wa1 * SIN[d] + (1.0 - GROWTH), 1.0)
            growth_b = jnp.maximum(wb0 * COS[d] + wb1 * SIN[d] + (1.0 - GROWTH), 1.0)
            out[pl.ds(start + 2 * d + odd, 8, stride=ND), :] = (
                ref[pl.ds(at, 8), :] * gain_a * growth_a
            )
            out[pl.ds(start + 2 * d + 1 - odd, 8, stride=ND), :] = (
                ref[pl.ds(at + 8, 8), :] * gain_b * growth_b
            )
        copy_out(first + g).start()
        return coupling * FREQ_STEP**GF, weight + GF / NF

    k = lax.broadcasted_iota(jnp.int32, (8, LANES), 0)
    coupling = jnp.zeros((8, LANES), jnp.float32)
    for i in range(GF):
        for h in range(2):
            value = GROWTH * WIND_COUPLING * FREQ_STEP**i * (1.0 - 2.0 * h)
            coupling = jnp.where(k == 2 * i + h, value, coupling)
    carry = (coupling, freq_weight())
    carry = lax.fori_loop(0, FIRST_GROUPS, functools.partial(one_group, 0, done), carry)
    lax.fori_loop(0, later, functools.partial(one_group, FIRST_GROUPS, turned), carry)
    for g in range(GROUPS):
        copy_out(g).wait()


def geometry_table(bands):
    total = 2 * bands

    def angle(position):
        return (LAT_SOUTH + (LAT_NORTH - LAT_SOUTH) * position / total) * (math.pi / 180.0)

    table = np.zeros((bands, 8), np.float32)
    for b in range(bands):
        cells = [angle(2 * b + 0.5), angle(2 * b + 1.5)]
        faces = [angle(2 * b), angle(2 * b + 1), angle(2 * b + 2)]
        icos = [1.0 / math.cos(v) for v in cells]
        near, far = (0, 1) if b % 2 == 0 else (1, 0)
        face_a, face_b = (faces[0], faces[2]) if b % 2 == 0 else (faces[2], faces[0])
        table[b] = [
            icos[0],
            icos[1],
            math.cos(face_a) * icos[near],
            math.cos(faces[1]) * icos[near],
            math.cos(faces[1]) * icos[far],
            math.cos(face_b) * icos[far],
            -TURNING * math.tan(cells[near]),
            -TURNING * math.tan(cells[far]),
        ]
    return table


def speed_table():
    table = np.zeros((2, WIDE), np.float32)
    for k in range(NF * ND):
        value = SPEED_TOP * FREQ_STEP ** -(k // ND) * math.cos(2.0 * math.pi * (k % ND) / ND)
        table[0, 2 * k] = value
        table[1, 2 * k + 1] = value
    return table


VMEM = pl.BlockSpec(memory_space=pltpu.VMEM)
SMEM = pl.BlockSpec(memory_space=pltpu.SMEM)
HBM = pl.BlockSpec(memory_space=pltpu.HBM)
ANY = pl.BlockSpec(memory_space=pl.ANY)
PARAMS = pltpu.CompilerParams(vmem_limit_bytes=40 * 1024 * 1024)


def call(kernel, name, operands, specs, shapes, scratch, micros, outs_in=None):
    outs = [jax.ShapeDtypeStruct(s, jnp.float32) for s in shapes]
    return pl.pallas_call(
        kernel,
        name=name,
        out_shape=outs,
        in_specs=specs,
        out_specs=[outs_in or VMEM] * len(outs),
        scratch_shapes=scratch,
        compiler_params=PARAMS,
        cost_estimate=pl.CostEstimate(
            flops=0, bytes_accessed=int(micros * 3.0e6), transcendentals=0
        ),
    )(*operands)


def swapped(pairs):
    return pairs + [(t, s) for s, t in pairs]


def per_device(bands, spec_count, spectra, sea_mask, wind, current):
    comp_count, row_count, col_count = spectra.shape
    cells = spectra.reshape(comp_count * row_count, col_count)
    middle = bands // 2 - 1
    first_rows = FIRST_GROUPS * GROUP_ROWS
    last_rows = ROWS - first_rows

    (own,) = call(
        pack_kernel,
        "pack_forcing",
        tuple(pltpu.with_memory_space_constraint(v, pltpu.HBM) for v in (wind, current, sea_mask)),
        [HBM] * 3,
        [(16, LANES)],
        [
            pltpu.VMEM(wind.shape, jnp.float32),
            pltpu.VMEM(current.shape, jnp.float32),
            pltpu.VMEM(sea_mask.shape, jnp.int32),
            pltpu.SemaphoreType.DMA((3,)),
        ],
        0.3,
    )
    order = [0]

    def gathered(values, bit):
        order.extend([r ^ bit for r in order])
        other = lax.ppermute(values, "band", [(b, b ^ bit) for b in range(bands)])
        return jnp.concatenate([values, other], axis=0)

    forcing = gathered(own, 2)

    part_relayed, part_direct = call(
        split_kernel,
        "split",
        (pltpu.with_memory_space_constraint(cells, pltpu.HBM), own),
        [HBM, VMEM],
        [(first_rows, LANES), (last_rows, LANES)],
        [pltpu.SemaphoreType.DMA((2,))],
        1.0,
    )
    part_direct, rows_after = lax.optimization_barrier((part_direct, cells))
    part_relayed, forcing, ends_sea = lax.optimization_barrier((part_relayed, forcing, sea_mask))
    straight = lax.ppermute(
        rows_after, "band", swapped([(b, b + 1) for b in range(1, bands - 1, 2) if b != middle])
    )
    west, east = call(
        ends_kernel,
        "ends",
        (cells, ends_sea),
        [VMEM] * 2,
        [(2, WIDE), (2, WIDE)],
        [pltpu.VMEM((LANES, LANES), jnp.float32)],
        1.0,
    )
    bit = 4
    while bit < bands:
        forcing = gathered(forcing, bit)
        bit *= 2
    part_relayed, part_direct, forcing, west, east = lax.optimization_barrier(
        (part_relayed, part_direct, forcing, west, east)
    )
    relay = lax.ppermute(part_relayed, "band", [(middle, bands - 1), (middle + 1, 0)])
    pairs = [(b, b + 1) for b in range(0, bands, 2)]
    forcing = gathered(forcing, 1)
    beyond = [lax.ppermute(part, "band", swapped(pairs)) for part in (part_relayed, part_direct)]
    part_direct, forcing = lax.optimization_barrier((part_direct, forcing))
    direct = lax.ppermute(
        part_direct, "band", [(middle, middle + 1), (middle + 1, middle)]
    )

    par, west, east = call(
        functools.partial(table_kernel, bands, tuple(order)),
        "tables",
        (jnp.asarray(geometry_table(bands)), forcing, west, east),
        [SMEM, VMEM, VMEM, VMEM],
        [(PAR_ROWS, LANES), (2, WIDE), (2, WIDE)],
        [pltpu.VMEM((8 * bands, LANES), jnp.float32)],
        0.3,
    )
    relay, par = lax.optimization_barrier((relay, par))
    relayed = lax.ppermute(relay, "band", [(bands - 1, middle + 1), (0, middle)])
    ring = [(s, (s + 1) % spec_count) for s in range(spec_count)]
    from_west = lax.ppermute(east, "spec", ring)
    from_east = lax.ppermute(west, "spec", [(t, s) for s, t in ring])
    base_first, base_last, gain_first, gain_last = call(
        base_kernel,
        "base",
        (par, cells, *beyond),
        [VMEM] * 4,
        [
            (first_rows, LANES),
            (last_rows, LANES),
            (first_rows * 3 // 2, LANES),
            (last_rows * 3 // 2, LANES),
        ],
        [],
        4.0,
    )
    base_first, from_west, from_east = lax.optimization_barrier((base_first, from_west, from_east))
    (fix,) = call(
        fix_kernel,
        "fix",
        (jnp.asarray(speed_table()), par, west, east, from_west, from_east),
        [VMEM] * 6,
        [(WIDE, LANES)],
        [pltpu.VMEM((LANES, WIDE), jnp.float32)],
        1.0,
    )
    turned, total = call(
        functools.partial(first_kernel, bands),
        "first_groups",
        (par, base_first, gain_first, fix, straight, relayed),
        [VMEM] * 6,
        [(first_rows, LANES), (16, LANES)],
        [],
        1.0,
    )
    (out,) = call(
        functools.partial(last_kernel, bands),
        "last_groups",
        (par, base_last, gain_last, fix, straight, direct, turned, total),
        [VMEM] * 8,
        [(ROWS, LANES)],
        [
            pltpu.VMEM((last_rows, LANES), jnp.float32),
            pltpu.VMEM((16, LANES), jnp.float32),
            pltpu.VMEM((ROWS, LANES), jnp.float32),
            pltpu.SemaphoreType.DMA((GROUPS,)),
        ],
        2.0,
        outs_in=ANY,
    )
    return out.reshape(comp_count, row_count, col_count)


def solution(mesh):
    placed = (
        P(None, "band", "spec"),
        P("band", "spec"),
        P(None, None, ("spec", "band")),
        P(None, None, ("spec", "band")),
    )
    return jax.shard_map(
        functools.partial(per_device, mesh.shape["band"], mesh.shape["spec"]),
        mesh=mesh,
        in_specs=placed,
        out_specs=P(None, "band", "spec"),
        check_vma=False,
    )
```

```python
import functools
import math

import jax
import jax.numpy as jnp
import numpy as np
from jax import lax
from jax.experimental import pallas as pl
from jax.experimental.pallas import tpu as pltpu
from jax.sharding import PartitionSpec as P

NF = 36
ND = 36
HALF = ND // 2
LAT_SOUTH = 30.0
LAT_NORTH = 55.0
SPEED_TOP = 0.35
FREQ_STEP = 1.1
TURNING = 1.5
GROWTH = 0.05
WIND_COUPLING = 0.04

GF = 4
GROUPS = NF // GF
GROUP_ROWS = GF * ND * 2
FIRST_GROUPS = 4
LANES = 128
ROWS = NF * ND * 2
WIDE = -(-(ROWS + 2) // LANES) * LANES

COS = [math.cos(2.0 * math.pi * d / ND) for d in range(HALF + 1)]
SIN = [math.sin(2.0 * math.pi * d / ND) for d in range(HALF + 1)]

(
    CUR_A,
    CUR_M,
    CUR_B,
    CX_A,
    CX_B,
    W0_A,
    W0_B,
    W1_A,
    W1_B,
    SEA_A,
    SEA_B,
    SEA_A1,
    SEA_A2,
    SEA_B1,
    SEA_B2,
    TAU,
    ICOS_A,
    ICOS_B,
    KAP_A,
    MU_A,
    MU_B,
    KAP_B,
    TAN_A,
    TAN_B,
    ICOS_0,
    ICOS_1,
) = range(26)
PAR_ROWS = 32


def flux(lo2, lo1, hi1, hi2, c):
    forward = c >= 0.0
    source = jnp.where(forward, lo1, hi1)
    upwind = jnp.where(forward, lo2, hi2)
    both = lo1 + hi1
    bend = both - 3.0 * source + upwind
    w = (1.0 / 6.0) - (c * c) * (1.0 / 6.0)
    return c * (0.5 * (both - c * (hi1 - lo1)) - w * bend)


def group_speed():
    k = lax.broadcasted_iota(jnp.int32, (8, LANES), 0)
    speed = jnp.zeros((8, LANES), jnp.float32)
    for i in range(GF):
        for h in range(2):
            value = SPEED_TOP * FREQ_STEP**-i * (1.0 - 2.0 * h)
            speed = jnp.where(k == 2 * i + h, value, speed)
    return speed


def freq_weight():
    k = lax.broadcasted_iota(jnp.int32, (8, LANES), 0)
    weight = jnp.zeros((8, LANES), jnp.float32)
    for i in range(GF):
        weight = jnp.where(lax.div(k, 2) == i, (i + 1.0) / NF, weight)
    return weight


def swap_halves(v):
    k = lax.broadcasted_iota(jnp.int32, (8, LANES), 0)
    return jnp.where(lax.rem(k, 2) == 0, pltpu.roll(v, 7, 0), pltpu.roll(v, 1, 0))


def wide_row(par, index):
    return jnp.broadcast_to(par[index : index + 1, :], (8, LANES))


def pack_kernel(wind, current, sea, out, wind_here, current_here, sea_here, sems):
    rows, strip = wind.shape[1], wind.shape[2]
    copies = [
        pltpu.make_async_copy(wind, wind_here, sems.at[0]),
        pltpu.make_async_copy(current, current_here, sems.at[1]),
        pltpu.make_async_copy(sea, sea_here, sems.at[2]),
    ]
    for copy in copies:
        copy.start()
    empty = jnp.zeros((8, LANES - strip), jnp.float32)
    for copy in copies:
        copy.wait()
    packed = jnp.zeros((8, LANES), jnp.float32)
    piece = 0
    for ref in (current_here, wind_here):
        for axis in range(2):
            for row in range(0, rows, 8):
                wide = jnp.concatenate([ref[axis, row : row + 8, :], empty], axis=1)
                packed = packed + (pltpu.roll(wide, piece * strip, 1) if piece else wide)
                piece += 1
    out[0:8, :] = packed
    out[8:10, :] = sea_here[...].astype(jnp.float32)
    out[10:16, :] = jnp.zeros((6, LANES), jnp.float32)


def split_kernel(source, own, relayed, direct, sems):
    del own
    first = relayed.shape[0]
    parts = [
        pltpu.make_async_copy(source.at[0:first], relayed, sems.at[0]),
        pltpu.make_async_copy(source.at[first:ROWS], direct, sems.at[1]),
    ]
    for part in parts:
        part.start()
    for part in parts:
        part.wait()


def ends_kernel(spectra, sea, west, east, line):
    seas = sea[...].astype(jnp.float32)
    sub = lax.broadcasted_iota(jnp.int32, (LANES, LANES), 0)
    both = jnp.where(
        lax.rem(sub, 2) == 0,
        jnp.broadcast_to(seas[0:1], (LANES, LANES)),
        jnp.broadcast_to(seas[1:2], (LANES, LANES)),
    )
    full = ROWS // LANES
    for block in range(WIDE // LANES):
        at = block * LANES
        if block < full:
            cells = spectra[at : at + LANES, :] * both
        else:
            left = ROWS - at
            line[...] = jnp.zeros((LANES, LANES), jnp.float32)
            line[0:left, :] = spectra[at : at + left, :] * both[0:left]
            cells = line[...]
        turned = cells.T
        west[:, at : at + LANES] = turned[0:2]
        east[:, at : at + LANES] = turned[LANES - 2 : LANES]


def table_kernel(bands, order, geometry, slots, west_in, east_in, par, west, east, line):
    me = lax.axis_index("band")
    is_even = lax.rem(me, 2) == 0
    rows = 2 * bands
    strip = LANES // bands
    block = lax.div(lax.broadcasted_iota(jnp.int32, (8, LANES), 1), strip)
    sources = [jnp.bitwise_xor(me, r) for r in order]
    moved = [
        pltpu.roll(slots[16 * k : 16 * k + 8, :], source * strip, 1)
        for k, source in enumerate(sources)
    ]
    for piece in range(rows // 2):
        row = jnp.zeros((8, LANES), jnp.float32)
        for source, values in zip(sources, moved):
            row = jnp.where(block == lax.rem(source + piece, bands), values, row)
        line[8 * piece : 8 * piece + 8, :] = (
            pltpu.roll(row, LANES - piece * strip, 1) if piece else row
        )

    def mask_of(band):
        found = jnp.zeros((2, LANES), jnp.float32)
        for k, source in enumerate(sources):
            found = jnp.where(source == band, slots[16 * k + 8 : 16 * k + 10, :], found)
        return [found[0:1], found[1:2]]

    seas = mask_of(me - 1) + mask_of(me) + mask_of(me + 1)
    row = 2 * me
    has_south = jnp.where(me > 0, 1.0, 0.0)
    has_north = jnp.where(me < bands - 1, 1.0, 0.0)

    def around(part):
        first = part * rows
        south = line[pl.ds(first + jnp.maximum(row - 1, 0), 1), :] * has_south
        north = line[pl.ds(first + jnp.minimum(row + 2, rows - 1), 1), :] * has_north
        return [south] + [line[pl.ds(first + row + i, 1), :] for i in range(2)] + [north]

    def pick(low, high):
        return jnp.where(is_even, low, high)

    def put(index, value):
        par[index : index + 1, :] = jnp.broadcast_to(value, (1, LANES))

    tau = jnp.where(is_even, 1.0, -1.0)
    north = around(1)
    face = [0.5 * (north[i] + north[i + 1]) for i in range(3)]
    put(CUR_A, tau * pick(face[0], face[2]))
    put(CUR_M, tau * face[1])
    put(CUR_B, tau * pick(face[2], face[0]))
    lane = lax.broadcasted_iota(jnp.int32, (1, LANES), 1)
    inside = jnp.where(lane == 0, 0.0, 1.0)
    east_speed = around(0)[1:3]
    wind_0, wind_1 = around(2)[1:3], around(3)[1:3]
    shifted = [0.5 * inside * (v + pltpu.roll(v, 1, 1)) for v in east_speed]
    put(CX_A, pick(shifted[0], shifted[1]))
    put(CX_B, pick(shifted[1], shifted[0]))
    put(W0_A, pick(wind_0[0], wind_0[1]))
    put(W0_B, pick(wind_0[1], wind_0[0]))
    put(W1_A, pick(wind_1[0], wind_1[1]))
    put(W1_B, pick(wind_1[1], wind_1[0]))
    put(SEA_A, pick(seas[2], seas[3]))
    put(SEA_B, pick(seas[3], seas[2]))
    put(SEA_A1, pick(seas[1], seas[4]))
    put(SEA_A2, pick(seas[0], seas[5]))
    put(SEA_B1, pick(seas[4], seas[1]))
    put(SEA_B2, pick(seas[5], seas[0]))
    put(TAU, tau)
    icos = [geometry[me, 0], geometry[me, 1]]
    put(ICOS_A, inside * pick(icos[0], icos[1]))
    put(ICOS_B, inside * pick(icos[1], icos[0]))
    put(KAP_A, geometry[me, 2])
    put(MU_A, geometry[me, 3])
    put(MU_B, geometry[me, 4])
    put(KAP_B, geometry[me, 5])
    put(TAN_A, geometry[me, 6])
    put(TAN_B, geometry[me, 7])
    put(ICOS_0, icos[0])
    put(ICOS_1, icos[1])
    par[26:32, :] = jnp.zeros((6, LANES), jnp.float32)

    west[...] = west_in[...]
    east[...] = east_in[...]
    for i in range(2):
        west[:, ROWS + i : ROWS + i + 1] = jnp.concatenate(
            [east_speed[i][:, j : j + 1] for j in range(2)], axis=0
        )
        east[:, ROWS + i : ROWS + i + 1] = jnp.concatenate(
            [east_speed[i][:, j : j + 1] for j in (LANES - 2, LANES - 1)], axis=0
        )


def fix_kernel(table, par, west, east, from_west, from_east, fix, tall):
    lane = lax.broadcasted_iota(jnp.int32, (1, WIDE), 1)
    even_row = lax.rem(lane, 2) == 0
    speed = table[0:1] * par[ICOS_0 : ICOS_0 + 1, 0:1] + table[1:2] * par[ICOS_1 : ICOS_1 + 1, 0:1]

    def column(ref, row):
        cells = ref[row : row + 1, :]
        drift = jnp.where(even_row, cells[:, ROWS : ROWS + 1], cells[:, ROWS + 1 : ROWS + 2])
        return cells, drift

    xm2, _ = column(from_west, 0)
    xm1, dm1 = column(from_west, 1)
    x0, d0 = column(west, 0)
    x1, d1 = column(west, 1)
    y2, d2 = column(east, 0)
    y1, dy1 = column(east, 1)
    z0, dz0 = column(from_east, 0)
    z1, _ = column(from_east, 1)
    first = flux(xm2, xm1, x0, x1, speed + 0.5 * (dm1 + d0))
    last = flux(y2, y1, z0, z1, speed + 0.5 * (dy1 + dz0))
    c = speed + 0.5 * (d0 + d1)
    second = jnp.where(c >= 0.0, -c * (1.0 - c * c) * (1.0 / 6.0), 0.0) * (xm1 - y1)
    c = speed + 0.5 * (d2 + dy1)
    before = jnp.where(c >= 0.0, 0.0, -c * (1.0 - c * c) * (1.0 / 6.0)) * (z0 - x0)
    tall[...] = jnp.zeros((LANES, WIDE), jnp.float32)
    tall[0:1, :] = first - second
    tall[1:2, :] = second
    tall[LANES - 2 : LANES - 1, :] = -before
    tall[LANES - 1 : LANES, :] = before - last
    for block in range(WIDE // LANES):
        at = block * LANES
        fix[at : at + LANES, :] = tall[:, at : at + LANES].T


def base_kernel(par, spectra, beyond_first, beyond_last, base_first, base_last, gain_first, gain_last):
    odd = lax.rem(lax.axis_index("band"), 2)
    sea_a, sea_b = wide_row(par, SEA_A), wide_row(par, SEA_B)
    sea_b1, sea_b2 = wide_row(par, SEA_B1), wide_row(par, SEA_B2)
    sea_a1 = wide_row(par, SEA_A1)
    into_a1 = wide_row(par, KAP_A) * sea_a1
    into_a2 = wide_row(par, KAP_A) * wide_row(par, SEA_A2)
    over_a, over_b = wide_row(par, MU_A) * sea_a1, wide_row(par, MU_B) * sea_a1
    cur_a, cur_m, cur_b = wide_row(par, CUR_A), wide_row(par, CUR_M), wide_row(par, CUR_B)
    cx_a, cx_b = wide_row(par, CX_A), wide_row(par, CX_B)
    kap_a, mu_a = wide_row(par, KAP_A), wide_row(par, MU_A)
    mu_b, kap_b = wide_row(par, MU_B), wide_row(par, KAP_B)
    tau = wide_row(par, TAU)
    icos_a, icos_b = wide_row(par, ICOS_A), wide_row(par, ICOS_B)

    def along_east(x, speed_x, current_x, cosine):
        crossing = flux(
            pltpu.roll(x, 2, 1),
            pltpu.roll(x, 1, 1),
            x,
            pltpu.roll(x, LANES - 1, 1),
            speed_x * cosine + current_x,
        )
        return crossing - pltpu.roll(crossing, LANES - 1, 1)

    def one_group(base, gain, beyond, first, g, speeds):
        start = (first + g) * GROUP_ROWS
        far = g * GROUP_ROWS
        north = speeds * tau
        east_a, east_b = speeds * icos_a, speeds * icos_b
        for d in range(HALF):
            row_a = pl.ds(start + 2 * d + odd, 8, stride=ND)
            row_b = pl.ds(start + 2 * d + 1 - odd, 8, stride=ND)
            a = spectra[row_a, :] * sea_a
            b = spectra[row_b, :] * sea_b
            b1 = beyond[pl.ds(far + 2 * d + odd, 8, stride=ND), :] * sea_b1
            b2 = beyond[pl.ds(far + 2 * d + 1 - odd, 8, stride=ND), :] * sea_b2
            c = north * SIN[d] + cur_a
            w = (1.0 / 6.0) - (c * c) * (1.0 / 6.0)
            inward = c >= 0.0
            cw = c * w
            half = 0.5 * c
            flux_a = (half - half * c) * a - cw * jnp.where(inward, a, b - 2.0 * a)
            cm = north * SIN[d] + cur_m
            flux_m = flux(0.0, a, b, b1, cm)
            away = jnp.where(cm >= 0.0, cm * ((cm * cm) * (1.0 / 6.0) - (1.0 / 6.0)), 0.0)
            flux_b = flux(a, b, b1, b2, north * SIN[d] + cur_b)
            to_a = along_east(a, east_a, cx_a, COS[d])
            to_b = along_east(b, east_b, cx_b, COS[d])
            at = pl.multiple_of(g * (HALF * 16) + d * 16, 8)
            base[pl.ds(at, 8), :] = a + to_a + kap_a * flux_a - mu_a * flux_m
            base[pl.ds(at + 8, 8), :] = b + to_b + mu_b * flux_m - kap_b * flux_b
            at = pl.multiple_of(g * (HALF * 24) + d * 24, 8)
            near = half + half * c + jnp.where(inward, 2.0 * cw, -cw)
            gain[pl.ds(at, 8), :] = into_a1 * near - over_a * away
            gain[pl.ds(at + 8, 8), :] = into_a2 * jnp.where(inward, -cw, 0.0)
            gain[pl.ds(at + 16, 8), :] = over_b * away
        return speeds * FREQ_STEP**-GF

    speeds = lax.fori_loop(
        0, FIRST_GROUPS, functools.partial(one_group, base_first, gain_first, beyond_first, 0), group_speed()
    )
    lax.fori_loop(
        0,
        GROUPS - FIRST_GROUPS,
        functools.partial(one_group, base_last, gain_last, beyond_last, FIRST_GROUPS),
        speeds,
    )


def turn(cells, rate):
    k = lax.broadcasted_iota(jnp.int32, (8, LANES), 0)
    first = lax.rem(k, 2) == 0
    cube = rate * rate * rate
    ring = [swap_halves(cells[HALF - 1])] + cells
    ring = ring + [swap_halves(cells[0]), swap_halves(cells[1])]
    steps = [high - low for low, high in zip(ring, ring[1:])]
    bends = [high - low for low, high in zip(steps, steps[1:])]
    fluxes = []
    for d in range(HALF):
        mean = 0.5 * (COS[d] + COS[d + 1])
        low, high = (bends[d + 1], bends[d]) if mean > 0 else (bends[d], bends[d + 1])
        bend = jnp.where(first, low, high)
        both = ring[d + 1] + ring[d + 2]
        weight = rate * (mean / 6.0) - cube * (mean**3 / 6.0)
        fluxes.append(
            (rate * (0.5 * mean)) * (both - (rate * mean) * steps[d + 1]) - weight * bend
        )
    last = swap_halves(fluxes[HALF - 1])
    return [cells[d] - (fluxes[d] - (fluxes[d - 1] if d else last)) for d in range(HALF)]


def finish_groups(first, count, skip, par, base, gain, fix, ahead, turned, total):
    odd = lax.rem(lax.axis_index("band"), 2)
    tan_a, tan_b = wide_row(par, TAN_A), wide_row(par, TAN_B)

    def one_group(g, carry):
        speeds, weight, sum_a, sum_b = carry
        start = (skip + g) * GROUP_ROWS
        fix_start = (first + g) * GROUP_ROWS
        cells_a, cells_b = [], []
        for d in range(HALF):
            n1 = ahead[pl.ds(start + 2 * d + 1 - odd, 8, stride=ND), :]
            n2 = ahead[pl.ds(start + 2 * d + odd, 8, stride=ND), :]
            fix_a = fix[pl.ds(fix_start + 2 * d + odd, 8, stride=ND), :]
            fix_b = fix[pl.ds(fix_start + 2 * d + 1 - odd, 8, stride=ND), :]
            at = pl.multiple_of(g * (HALF * 16) + d * 16, 8)
            by = pl.multiple_of(g * (HALF * 24) + d * 24, 8)
            cells_a.append(
                base[pl.ds(at, 8), :]
                + fix_a
                + gain[pl.ds(by, 8), :] * n1
                + gain[pl.ds(by + 8, 8), :] * n2
            )
            cells_b.append(base[pl.ds(at + 8, 8), :] + fix_b + gain[pl.ds(by + 16, 8), :] * n1)
        square_a = square_b = 0.0
        for d, v in enumerate(turn(cells_a, speeds * tan_a)):
            at = pl.multiple_of(g * (HALF * 16) + d * 16, 8)
            turned[pl.ds(at, 8), :] = v
            square_a = square_a + v * v
        for d, v in enumerate(turn(cells_b, speeds * tan_b)):
            at = pl.multiple_of(g * (HALF * 16) + d * 16 + 8, 8)
            turned[pl.ds(at, 8), :] = v
            square_b = square_b + v * v
        return (
            speeds * FREQ_STEP**-GF,
            weight + GF / NF,
            sum_a + weight * square_a,
            sum_b + weight * square_b,
        )

    speeds = group_speed() * FREQ_STEP ** -(GF * first)
    weight = freq_weight() + GF * first / NF
    carry = (speeds, weight, total[0:8, :], total[8:16, :])
    _, _, total[0:8, :], total[8:16, :] = lax.fori_loop(0, count, one_group, carry)


def finish_either(bands, first, count, par, base, gain, fix, straight, split, turned, total):
    me = lax.axis_index("band")
    middle = jnp.logical_or(me == bands // 2 - 1, me == bands // 2)

    @pl.when(middle)
    def _():
        finish_groups(first, count, 0, par, base, gain, fix, split, turned, total)

    @pl.when(jnp.logical_not(middle))
    def _():
        finish_groups(first, count, first, par, base, gain, fix, straight, turned, total)


def first_kernel(bands, par, base, gain, fix, straight, split, turned, total):
    total[...] = jnp.zeros((16, LANES), jnp.float32)
    finish_either(bands, 0, FIRST_GROUPS, par, base, gain, fix, straight, split, turned, total)


def last_kernel(
    bands, par, base, gain, fix, straight, split, done, before, result, turned, total, out, sems
):
    odd = lax.rem(lax.axis_index("band"), 2)
    later = GROUPS - FIRST_GROUPS
    total[...] = before[...]
    finish_either(bands, FIRST_GROUPS, later, par, base, gain, fix, straight, split, turned, total)
    scale = 2.0 / (NF * ND)
    steep_a = jnp.sum(total[0:8, :], axis=0, keepdims=True) * scale
    steep_b = jnp.sum(total[8:16, :], axis=0, keepdims=True) * scale
    sea_a, sea_b = wide_row(par, SEA_A), wide_row(par, SEA_B)
    w0_a, w0_b = wide_row(par, W0_A), wide_row(par, W0_B)
    w1_a, w1_b = wide_row(par, W1_A), wide_row(par, W1_B)

    def copy_out(g):
        rows = pl.ds(pl.multiple_of(g * GROUP_ROWS, 8), GROUP_ROWS)
        return pltpu.make_async_copy(out.at[rows], result.at[rows], sems.at[g])

    def one_group(first, ref, g, carry):
        coupling, weight = carry
        start = (first + g) * GROUP_ROWS
        gain_a = sea_a / (1.0 + weight * steep_a)
        gain_b = sea_b / (1.0 + weight * steep_b)
        wa0, wa1 = w0_a * coupling, w1_a * coupling
        wb0, wb1 = w0_b * coupling, w1_b * coupling
        for d in range(HALF):
            at = pl.multiple_of(g * (HALF * 16) + d * 16, 8)
            growth_a = jnp.maximum(wa0 * COS[d] + wa1 * SIN[d] + (1.0 - GROWTH), 1.0)
            growth_b = jnp.maximum(wb0 * COS[d] + wb1 * SIN[d] + (1.0 - GROWTH), 1.0)
            out[pl.ds(start + 2 * d + odd, 8, stride=ND), :] = (
                ref[pl.ds(at, 8), :] * gain_a * growth_a
            )
            out[pl.ds(start + 2 * d + 1 - odd, 8, stride=ND), :] = (
                ref[pl.ds(at + 8, 8), :] * gain_b * growth_b
            )
        copy_out(first + g).start()
        return coupling * FREQ_STEP**GF, weight + GF / NF

    k = lax.broadcasted_iota(jnp.int32, (8, LANES), 0)
    coupling = jnp.zeros((8, LANES), jnp.float32)
    for i in range(GF):
        for h in range(2):
            value = GROWTH * WIND_COUPLING * FREQ_STEP**i * (1.0 - 2.0 * h)
            coupling = jnp.where(k == 2 * i + h, value, coupling)
    carry = (coupling, freq_weight())
    carry = lax.fori_loop(0, FIRST_GROUPS, functools.partial(one_group, 0, done), carry)
    lax.fori_loop(0, later, functools.partial(one_group, FIRST_GROUPS, turned), carry)
    for g in range(GROUPS):
        copy_out(g).wait()


def geometry_table(bands):
    total = 2 * bands

    def angle(position):
        return (LAT_SOUTH + (LAT_NORTH - LAT_SOUTH) * position / total) * (math.pi / 180.0)

    table = np.zeros((bands, 8), np.float32)
    for b in range(bands):
        cells = [angle(2 * b + 0.5), angle(2 * b + 1.5)]
        faces = [angle(2 * b), angle(2 * b + 1), angle(2 * b + 2)]
        icos = [1.0 / math.cos(v) for v in cells]
        near, far = (0, 1) if b % 2 == 0 else (1, 0)
        face_a, face_b = (faces[0], faces[2]) if b % 2 == 0 else (faces[2], faces[0])
        table[b] = [
            icos[0],
            icos[1],
            math.cos(face_a) * icos[near],
            math.cos(faces[1]) * icos[near],
            math.cos(faces[1]) * icos[far],
            math.cos(face_b) * icos[far],
            -TURNING * math.tan(cells[near]),
            -TURNING * math.tan(cells[far]),
        ]
    return table


def speed_table():
    table = np.zeros((2, WIDE), np.float32)
    for k in range(NF * ND):
        value = SPEED_TOP * FREQ_STEP ** -(k // ND) * math.cos(2.0 * math.pi * (k % ND) / ND)
        table[0, 2 * k] = value
        table[1, 2 * k + 1] = value
    return table


VMEM = pl.BlockSpec(memory_space=pltpu.VMEM)
SMEM = pl.BlockSpec(memory_space=pltpu.SMEM)
HBM = pl.BlockSpec(memory_space=pltpu.HBM)
ANY = pl.BlockSpec(memory_space=pl.ANY)
PARAMS = pltpu.CompilerParams(vmem_limit_bytes=40 * 1024 * 1024)


def call(kernel, name, operands, specs, shapes, scratch, micros, outs_in=None, flops=0):
    outs = [jax.ShapeDtypeStruct(s, jnp.float32) for s in shapes]
    return pl.pallas_call(
        kernel,
        name=name,
        out_shape=outs,
        in_specs=specs,
        out_specs=[outs_in or VMEM] * len(outs),
        scratch_shapes=scratch,
        compiler_params=PARAMS,
        cost_estimate=pl.CostEstimate(
            flops=flops, bytes_accessed=int(micros * 3.0e6), transcendentals=0
        ),
    )(*operands)


def swapped(pairs):
    return pairs + [(t, s) for s, t in pairs]


def per_device(bands, spec_count, spectra, sea_mask, wind, current):
    comp_count, row_count, col_count = spectra.shape
    cells = spectra.reshape(comp_count * row_count, col_count)
    middle = bands // 2 - 1
    first_rows = FIRST_GROUPS * GROUP_ROWS
    last_rows = ROWS - first_rows

    (own,) = call(
        pack_kernel,
        "pack_forcing",
        tuple(pltpu.with_memory_space_constraint(v, pltpu.HBM) for v in (wind, current, sea_mask)),
        [HBM] * 3,
        [(16, LANES)],
        [
            pltpu.VMEM(wind.shape, jnp.float32),
            pltpu.VMEM(current.shape, jnp.float32),
            pltpu.VMEM(sea_mask.shape, jnp.int32),
            pltpu.SemaphoreType.DMA((3,)),
        ],
        0.3,
    )
    order = [0]

    def gathered(values, bit):
        order.extend([r ^ bit for r in order])
        other = lax.ppermute(values, "band", [(b, b ^ bit) for b in range(bands)])
        return jnp.concatenate([values, other], axis=0)

    forcing = gathered(own, 2)

    part_relayed, part_direct = call(
        split_kernel,
        "split",
        (pltpu.with_memory_space_constraint(cells, pltpu.HBM), own),
        [HBM, VMEM],
        [(first_rows, LANES), (last_rows, LANES)],
        [pltpu.SemaphoreType.DMA((2,))],
        1.0,
    )
    part_direct, rows_after = lax.optimization_barrier((part_direct, cells))
    part_relayed, forcing, ends_sea = lax.optimization_barrier((part_relayed, forcing, sea_mask))
    straight = lax.ppermute(
        rows_after, "band", swapped([(b, b + 1) for b in range(1, bands - 1, 2) if b != middle])
    )
    west, east = call(
        ends_kernel,
        "ends",
        (cells, ends_sea),
        [VMEM] * 2,
        [(2, WIDE), (2, WIDE)],
        [pltpu.VMEM((LANES, LANES), jnp.float32)],
        1.0,
    )
    part_relayed, west, east = lax.optimization_barrier((part_relayed, west, east))
    relay = lax.ppermute(part_relayed, "band", [(middle, bands - 1), (middle + 1, 0)])
    bit = 4
    while bit < bands:
        forcing = gathered(forcing, bit)
        bit *= 2
    part_relayed, part_direct, forcing, west, east = lax.optimization_barrier(
        (part_relayed, part_direct, forcing, west, east)
    )
    pairs = [(b, b + 1) for b in range(0, bands, 2)]
    forcing = gathered(forcing, 1)
    beyond = [lax.ppermute(part, "band", swapped(pairs)) for part in (part_relayed, part_direct)]
    part_direct, forcing = lax.optimization_barrier((part_direct, forcing))
    direct = lax.ppermute(
        part_direct, "band", [(middle, middle + 1), (middle + 1, middle)]
    )

    par, west, east = call(
        functools.partial(table_kernel, bands, tuple(order)),
        "tables",
        (jnp.asarray(geometry_table(bands)), forcing, west, east),
        [SMEM, VMEM, VMEM, VMEM],
        [(PAR_ROWS, LANES), (2, WIDE), (2, WIDE)],
        [pltpu.VMEM((8 * bands, LANES), jnp.float32)],
        0.3,
        flops=4200000000,
    )
    relay, par = lax.optimization_barrier((relay, par))
    relayed = lax.ppermute(relay, "band", [(bands - 1, middle + 1), (0, middle)])
    ring = [(s, (s + 1) % spec_count) for s in range(spec_count)]
    from_west = lax.ppermute(east, "spec", ring)
    from_east = lax.ppermute(west, "spec", [(t, s) for s, t in ring])
    base_first, base_last, gain_first, gain_last = call(
        base_kernel,
        "base",
        (par, cells, *beyond),
        [VMEM] * 4,
        [
            (first_rows, LANES),
            (last_rows, LANES),
            (first_rows * 3 // 2, LANES),
            (last_rows * 3 // 2, LANES),
        ],
        [],
        4.0,
    )
    base_first, from_west, from_east = lax.optimization_barrier((base_first, from_west, from_east))
    (fix,) = call(
        fix_kernel,
        "fix",
        (jnp.asarray(speed_table()), par, west, east, from_west, from_east),
        [VMEM] * 6,
        [(WIDE, LANES)],
        [pltpu.VMEM((LANES, WIDE), jnp.float32)],
        1.0,
    )
    turned, total = call(
        functools.partial(first_kernel, bands),
        "first_groups",
        (par, base_first, gain_first, fix, straight, relayed),
        [VMEM] * 6,
        [(first_rows, LANES), (16, LANES)],
        [],
        1.0,
    )
    (out,) = call(
        functools.partial(last_kernel, bands),
        "last_groups",
        (par, base_last, gain_last, fix, straight, direct, turned, total),
        [VMEM] * 8,
        [(ROWS, LANES)],
        [
            pltpu.VMEM((last_rows, LANES), jnp.float32),
            pltpu.VMEM((16, LANES), jnp.float32),
            pltpu.VMEM((ROWS, LANES), jnp.float32),
            pltpu.SemaphoreType.DMA((GROUPS,)),
        ],
        2.0,
        outs_in=ANY,
    )
    return out.reshape(comp_count, row_count, col_count)


def solution(mesh):
    placed = (
        P(None, "band", "spec"),
        P("band", "spec"),
        P(None, None, ("spec", "band")),
        P(None, None, ("spec", "band")),
    )
    return jax.shard_map(
        functools.partial(per_device, mesh.shape["band"], mesh.shape["spec"]),
        mesh=mesh,
        in_specs=placed,
        out_specs=P(None, "band", "spec"),
        check_vma=False,
    )
```

```python
import functools
import math

import jax
import jax.numpy as jnp
import numpy as np
from jax import lax
from jax.experimental import pallas as pl
from jax.experimental.pallas import tpu as pltpu
from jax.sharding import PartitionSpec as P

NF = 36
ND = 36
HALF = ND // 2
LAT_SOUTH = 30.0
LAT_NORTH = 55.0
SPEED_TOP = 0.35
FREQ_STEP = 1.1
TURNING = 1.5
GROWTH = 0.05
WIND_COUPLING = 0.04

GF = 4
GROUPS = NF // GF
GROUP_ROWS = GF * ND * 2
FIRST_GROUPS = 4
LANES = 128
ROWS = NF * ND * 2
WIDE = -(-(ROWS + 2) // LANES) * LANES

COS = [math.cos(2.0 * math.pi * d / ND) for d in range(HALF + 1)]
SIN = [math.sin(2.0 * math.pi * d / ND) for d in range(HALF + 1)]

(
    CUR_A,
    CUR_M,
    CUR_B,
    CX_A,
    CX_B,
    W0_A,
    W0_B,
    W1_A,
    W1_B,
    SEA_A,
    SEA_B,
    SEA_A1,
    SEA_A2,
    SEA_B1,
    SEA_B2,
    TAU,
    ICOS_A,
    ICOS_B,
    KAP_A,
    MU_A,
    MU_B,
    KAP_B,
    TAN_A,
    TAN_B,
    ICOS_0,
    ICOS_1,
) = range(26)
PAR_ROWS = 32


def flux(lo2, lo1, hi1, hi2, c):
    forward = c >= 0.0
    source = jnp.where(forward, lo1, hi1)
    upwind = jnp.where(forward, lo2, hi2)
    both = lo1 + hi1
    bend = both - 3.0 * source + upwind
    w = (1.0 / 6.0) - (c * c) * (1.0 / 6.0)
    return c * (0.5 * (both - c * (hi1 - lo1)) - w * bend)


def group_speed():
    k = lax.broadcasted_iota(jnp.int32, (8, LANES), 0)
    speed = jnp.zeros((8, LANES), jnp.float32)
    for i in range(GF):
        for h in range(2):
            value = SPEED_TOP * FREQ_STEP**-i * (1.0 - 2.0 * h)
            speed = jnp.where(k == 2 * i + h, value, speed)
    return speed


def freq_weight():
    k = lax.broadcasted_iota(jnp.int32, (8, LANES), 0)
    weight = jnp.zeros((8, LANES), jnp.float32)
    for i in range(GF):
        weight = jnp.where(lax.div(k, 2) == i, (i + 1.0) / NF, weight)
    return weight


def swap_halves(v):
    k = lax.broadcasted_iota(jnp.int32, (8, LANES), 0)
    return jnp.where(lax.rem(k, 2) == 0, pltpu.roll(v, 7, 0), pltpu.roll(v, 1, 0))


def wide_row(par, index):
    return jnp.broadcast_to(par[index : index + 1, :], (8, LANES))


def pack_kernel(wind, current, sea, out, wind_here, current_here, sea_here, sems):
    rows, strip = wind.shape[1], wind.shape[2]
    copies = [
        pltpu.make_async_copy(wind, wind_here, sems.at[0]),
        pltpu.make_async_copy(current, current_here, sems.at[1]),
        pltpu.make_async_copy(sea, sea_here, sems.at[2]),
    ]
    for copy in copies:
        copy.start()
    empty = jnp.zeros((8, LANES - strip), jnp.float32)
    for copy in copies:
        copy.wait()
    packed = jnp.zeros((8, LANES), jnp.float32)
    piece = 0
    for ref in (current_here, wind_here):
        for axis in range(2):
            for row in range(0, rows, 8):
                wide = jnp.concatenate([ref[axis, row : row + 8, :], empty], axis=1)
                packed = packed + (pltpu.roll(wide, piece * strip, 1) if piece else wide)
                piece += 1
    out[0:8, :] = packed
    out[8:10, :] = sea_here[...].astype(jnp.float32)
    out[10:16, :] = jnp.zeros((6, LANES), jnp.float32)


def split_kernel(source, own, relayed, direct, sems):
    del own
    first = relayed.shape[0]
    parts = [
        pltpu.make_async_copy(source.at[0:first], relayed, sems.at[0]),
        pltpu.make_async_copy(source.at[first:ROWS], direct, sems.at[1]),
    ]
    for part in parts:
        part.start()
    for part in parts:
        part.wait()


def ends_kernel(spectra, sea, west, east, line):
    seas = sea[...].astype(jnp.float32)
    sub = lax.broadcasted_iota(jnp.int32, (LANES, LANES), 0)
    both = jnp.where(
        lax.rem(sub, 2) == 0,
        jnp.broadcast_to(seas[0:1], (LANES, LANES)),
        jnp.broadcast_to(seas[1:2], (LANES, LANES)),
    )
    full = ROWS // LANES
    for block in range(WIDE // LANES):
        at = block * LANES
        if block < full:
            cells = spectra[at : at + LANES, :] * both
        else:
            left = ROWS - at
            line[...] = jnp.zeros((LANES, LANES), jnp.float32)
            line[0:left, :] = spectra[at : at + left, :] * both[0:left]
            cells = line[...]
        turned = cells.T
        west[:, at : at + LANES] = turned[0:2]
        east[:, at : at + LANES] = turned[LANES - 2 : LANES]


def table_kernel(bands, order, geometry, slots, west_in, east_in, par, first, second, line):
    me = lax.axis_index("band")
    is_even = lax.rem(me, 2) == 0
    rows = 2 * bands
    strip = LANES // bands
    block = lax.div(lax.broadcasted_iota(jnp.int32, (8, LANES), 1), strip)
    sources = [jnp.bitwise_xor(me, r) for r in order]
    moved = [
        pltpu.roll(slots[16 * k : 16 * k + 8, :], source * strip, 1)
        for k, source in enumerate(sources)
    ]
    for piece in range(rows // 2):
        row = jnp.zeros((8, LANES), jnp.float32)
        for source, values in zip(sources, moved):
            row = jnp.where(block == lax.rem(source + piece, bands), values, row)
        line[8 * piece : 8 * piece + 8, :] = (
            pltpu.roll(row, LANES - piece * strip, 1) if piece else row
        )

    def mask_of(band):
        found = jnp.zeros((2, LANES), jnp.float32)
        for k, source in enumerate(sources):
            found = jnp.where(source == band, slots[16 * k + 8 : 16 * k + 10, :], found)
        return [found[0:1], found[1:2]]

    seas = mask_of(me - 1) + mask_of(me) + mask_of(me + 1)
    row = 2 * me
    has_south = jnp.where(me > 0, 1.0, 0.0)
    has_north = jnp.where(me < bands - 1, 1.0, 0.0)

    def around(part):
        first = part * rows
        south = line[pl.ds(first + jnp.maximum(row - 1, 0), 1), :] * has_south
        north = line[pl.ds(first + jnp.minimum(row + 2, rows - 1), 1), :] * has_north
        return [south] + [line[pl.ds(first + row + i, 1), :] for i in range(2)] + [north]

    def pick(low, high):
        return jnp.where(is_even, low, high)

    def put(index, value):
        par[index : index + 1, :] = jnp.broadcast_to(value, (1, LANES))

    tau = jnp.where(is_even, 1.0, -1.0)
    north = around(1)
    face = [0.5 * (north[i] + north[i + 1]) for i in range(3)]
    put(CUR_A, tau * pick(face[0], face[2]))
    put(CUR_M, tau * face[1])
    put(CUR_B, tau * pick(face[2], face[0]))
    lane = lax.broadcasted_iota(jnp.int32, (1, LANES), 1)
    inside = jnp.where(lane == 0, 0.0, 1.0)
    east_speed = around(0)[1:3]
    wind_0, wind_1 = around(2)[1:3], around(3)[1:3]
    shifted = [0.5 * inside * (v + pltpu.roll(v, 1, 1)) for v in east_speed]
    put(CX_A, pick(shifted[0], shifted[1]))
    put(CX_B, pick(shifted[1], shifted[0]))
    put(W0_A, pick(wind_0[0], wind_0[1]))
    put(W0_B, pick(wind_0[1], wind_0[0]))
    put(W1_A, pick(wind_1[0], wind_1[1]))
    put(W1_B, pick(wind_1[1], wind_1[0]))
    put(SEA_A, pick(seas[2], seas[3]))
    put(SEA_B, pick(seas[3], seas[2]))
    put(SEA_A1, pick(seas[1], seas[4]))
    put(SEA_A2, pick(seas[0], seas[5]))
    put(SEA_B1, pick(seas[4], seas[1]))
    put(SEA_B2, pick(seas[5], seas[0]))
    put(TAU, tau)
    icos = [geometry[me, 0], geometry[me, 1]]
    put(ICOS_A, inside * pick(icos[0], icos[1]))
    put(ICOS_B, inside * pick(icos[1], icos[0]))
    put(KAP_A, geometry[me, 2])
    put(MU_A, geometry[me, 3])
    put(MU_B, geometry[me, 4])
    put(KAP_B, geometry[me, 5])
    put(TAN_A, geometry[me, 6])
    put(TAN_B, geometry[me, 7])
    put(ICOS_0, icos[0])
    put(ICOS_1, icos[1])
    par[26:32, :] = jnp.zeros((6, LANES), jnp.float32)

    ends = []
    for values, columns in ((west_in[...], (0, 1)), (east_in[...], (LANES - 2, LANES - 1))):
        lane = lax.broadcasted_iota(jnp.int32, values.shape, 1)
        for i in range(2):
            pair = jnp.concatenate([east_speed[i][:, j : j + 1] for j in columns], axis=0)
            values = jnp.where(lane == ROWS + i, pair, values)
        ends.append(values)
    even_spec = lax.rem(lax.axis_index("spec"), 2) == 0
    first[...] = jnp.where(even_spec, ends[0], ends[1])
    second[...] = jnp.where(even_spec, ends[1], ends[0])


def fix_kernel(table, par, first_here, second_here, first_there, second_there, fix, tall):
    even_spec = lax.rem(lax.axis_index("spec"), 2) == 0
    west = jnp.where(even_spec, first_here[...], second_here[...])
    east = jnp.where(even_spec, second_here[...], first_here[...])
    from_west = jnp.where(even_spec, first_there[...], second_there[...])
    from_east = jnp.where(even_spec, second_there[...], first_there[...])
    lane = lax.broadcasted_iota(jnp.int32, (1, WIDE), 1)
    even_row = lax.rem(lane, 2) == 0
    speed = table[0:1] * par[ICOS_0 : ICOS_0 + 1, 0:1] + table[1:2] * par[ICOS_1 : ICOS_1 + 1, 0:1]

    def column(ref, row):
        cells = ref[row : row + 1, :]
        drift = jnp.where(even_row, cells[:, ROWS : ROWS + 1], cells[:, ROWS + 1 : ROWS + 2])
        return cells, drift

    xm2, _ = column(from_west, 0)
    xm1, dm1 = column(from_west, 1)
    x0, d0 = column(west, 0)
    x1, d1 = column(west, 1)
    y2, d2 = column(east, 0)
    y1, dy1 = column(east, 1)
    z0, dz0 = column(from_east, 0)
    z1, _ = column(from_east, 1)
    first = flux(xm2, xm1, x0, x1, speed + 0.5 * (dm1 + d0))
    last = flux(y2, y1, z0, z1, speed + 0.5 * (dy1 + dz0))
    c = speed + 0.5 * (d0 + d1)
    second = jnp.where(c >= 0.0, -c * (1.0 - c * c) * (1.0 / 6.0), 0.0) * (xm1 - y1)
    c = speed + 0.5 * (d2 + dy1)
    before = jnp.where(c >= 0.0, 0.0, -c * (1.0 - c * c) * (1.0 / 6.0)) * (z0 - x0)
    tall[...] = jnp.zeros((LANES, WIDE), jnp.float32)
    tall[0:1, :] = first - second
    tall[1:2, :] = second
    tall[LANES - 2 : LANES - 1, :] = -before
    tall[LANES - 1 : LANES, :] = before - last
    for block in range(WIDE // LANES):
        at = block * LANES
        fix[at : at + LANES, :] = tall[:, at : at + LANES].T


def base_kernel(par, spectra, beyond_first, beyond_last, base_first, base_last, gain_first, gain_last):
    odd = lax.rem(lax.axis_index("band"), 2)
    sea_a, sea_b = wide_row(par, SEA_A), wide_row(par, SEA_B)
    sea_b1, sea_b2 = wide_row(par, SEA_B1), wide_row(par, SEA_B2)
    sea_a1 = wide_row(par, SEA_A1)
    into_a1 = wide_row(par, KAP_A) * sea_a1
    into_a2 = wide_row(par, KAP_A) * wide_row(par, SEA_A2)
    over_a, over_b = wide_row(par, MU_A) * sea_a1, wide_row(par, MU_B) * sea_a1
    cur_a, cur_m, cur_b = wide_row(par, CUR_A), wide_row(par, CUR_M), wide_row(par, CUR_B)
    cx_a, cx_b = wide_row(par, CX_A), wide_row(par, CX_B)
    kap_a, mu_a = wide_row(par, KAP_A), wide_row(par, MU_A)
    mu_b, kap_b = wide_row(par, MU_B), wide_row(par, KAP_B)
    tau = wide_row(par, TAU)
    icos_a, icos_b = wide_row(par, ICOS_A), wide_row(par, ICOS_B)

    def along_east(x, speed_x, current_x, cosine):
        crossing = flux(
            pltpu.roll(x, 2, 1),
            pltpu.roll(x, 1, 1),
            x,
            pltpu.roll(x, LANES - 1, 1),
            speed_x * cosine + current_x,
        )
        return crossing - pltpu.roll(crossing, LANES - 1, 1)

    def one_group(base, gain, beyond, first, g, speeds):
        start = (first + g) * GROUP_ROWS
        far = g * GROUP_ROWS
        north = speeds * tau
        east_a, east_b = speeds * icos_a, speeds * icos_b
        for d in range(HALF):
            row_a = pl.ds(start + 2 * d + odd, 8, stride=ND)
            row_b = pl.ds(start + 2 * d + 1 - odd, 8, stride=ND)
            a = spectra[row_a, :] * sea_a
            b = spectra[row_b, :] * sea_b
            b1 = beyond[pl.ds(far + 2 * d + odd, 8, stride=ND), :] * sea_b1
            b2 = beyond[pl.ds(far + 2 * d + 1 - odd, 8, stride=ND), :] * sea_b2
            c = north * SIN[d] + cur_a
            w = (1.0 / 6.0) - (c * c) * (1.0 / 6.0)
            inward = c >= 0.0
            cw = c * w
            half = 0.5 * c
            flux_a = (half - half * c) * a - cw * jnp.where(inward, a, b - 2.0 * a)
            cm = north * SIN[d] + cur_m
            flux_m = flux(0.0, a, b, b1, cm)
            away = jnp.where(cm >= 0.0, cm * ((cm * cm) * (1.0 / 6.0) - (1.0 / 6.0)), 0.0)
            flux_b = flux(a, b, b1, b2, north * SIN[d] + cur_b)
            to_a = along_east(a, east_a, cx_a, COS[d])
            to_b = along_east(b, east_b, cx_b, COS[d])
            at = pl.multiple_of(g * (HALF * 16) + d * 16, 8)
            base[pl.ds(at, 8), :] = a + to_a + kap_a * flux_a - mu_a * flux_m
            base[pl.ds(at + 8, 8), :] = b + to_b + mu_b * flux_m - kap_b * flux_b
            at = pl.multiple_of(g * (HALF * 24) + d * 24, 8)
            near = half + half * c + jnp.where(inward, 2.0 * cw, -cw)
            gain[pl.ds(at, 8), :] = into_a1 * near - over_a * away
            gain[pl.ds(at + 8, 8), :] = into_a2 * jnp.where(inward, -cw, 0.0)
            gain[pl.ds(at + 16, 8), :] = over_b * away
        return speeds * FREQ_STEP**-GF

    speeds = lax.fori_loop(
        0, FIRST_GROUPS, functools.partial(one_group, base_first, gain_first, beyond_first, 0), group_speed()
    )
    lax.fori_loop(
        0,
        GROUPS - FIRST_GROUPS,
        functools.partial(one_group, base_last, gain_last, beyond_last, FIRST_GROUPS),
        speeds,
    )


def turn(cells, rate):
    k = lax.broadcasted_iota(jnp.int32, (8, LANES), 0)
    first = lax.rem(k, 2) == 0
    cube = rate * rate * rate
    ring = [swap_halves(cells[HALF - 1])] + cells
    ring = ring + [swap_halves(cells[0]), swap_halves(cells[1])]
    steps = [high - low for low, high in zip(ring, ring[1:])]
    bends = [high - low for low, high in zip(steps, steps[1:])]
    fluxes = []
    for d in range(HALF):
        mean = 0.5 * (COS[d] + COS[d + 1])
        low, high = (bends[d + 1], bends[d]) if mean > 0 else (bends[d], bends[d + 1])
        bend = jnp.where(first, low, high)
        both = ring[d + 1] + ring[d + 2]
        weight = rate * (mean / 6.0) - cube * (mean**3 / 6.0)
        fluxes.append(
            (rate * (0.5 * mean)) * (both - (rate * mean) * steps[d + 1]) - weight * bend
        )
    last = swap_halves(fluxes[HALF - 1])
    return [cells[d] - (fluxes[d] - (fluxes[d - 1] if d else last)) for d in range(HALF)]


def finish_groups(first, count, skip, par, base, gain, fix, ahead, turned, total):
    odd = lax.rem(lax.axis_index("band"), 2)
    tan_a, tan_b = wide_row(par, TAN_A), wide_row(par, TAN_B)

    def one_group(g, carry):
        speeds, weight, sum_a, sum_b = carry
        start = (skip + g) * GROUP_ROWS
        fix_start = (first + g) * GROUP_ROWS
        cells_a, cells_b = [], []
        for d in range(HALF):
            n1 = ahead[pl.ds(start + 2 * d + 1 - odd, 8, stride=ND), :]
            n2 = ahead[pl.ds(start + 2 * d + odd, 8, stride=ND), :]
            fix_a = fix[pl.ds(fix_start + 2 * d + odd, 8, stride=ND), :]
            fix_b = fix[pl.ds(fix_start + 2 * d + 1 - odd, 8, stride=ND), :]
            at = pl.multiple_of(g * (HALF * 16) + d * 16, 8)
            by = pl.multiple_of(g * (HALF * 24) + d * 24, 8)
            cells_a.append(
                base[pl.ds(at, 8), :]
                + fix_a
                + gain[pl.ds(by, 8), :] * n1
                + gain[pl.ds(by + 8, 8), :] * n2
            )
            cells_b.append(base[pl.ds(at + 8, 8), :] + fix_b + gain[pl.ds(by + 16, 8), :] * n1)
        square_a = square_b = 0.0
        for d, v in enumerate(turn(cells_a, speeds * tan_a)):
            at = pl.multiple_of(g * (HALF * 16) + d * 16, 8)
            turned[pl.ds(at, 8), :] = v
            square_a = square_a + v * v
        for d, v in enumerate(turn(cells_b, speeds * tan_b)):
            at = pl.multiple_of(g * (HALF * 16) + d * 16 + 8, 8)
            turned[pl.ds(at, 8), :] = v
            square_b = square_b + v * v
        return (
            speeds * FREQ_STEP**-GF,
            weight + GF / NF,
            sum_a + weight * square_a,
            sum_b + weight * square_b,
        )

    speeds = group_speed() * FREQ_STEP ** -(GF * first)
    weight = freq_weight() + GF * first / NF
    carry = (speeds, weight, total[0:8, :], total[8:16, :])
    _, _, total[0:8, :], total[8:16, :] = lax.fori_loop(0, count, one_group, carry)


def finish_either(bands, first, count, par, base, gain, fix, straight, split, turned, total):
    me = lax.axis_index("band")
    middle = jnp.logical_or(me == bands // 2 - 1, me == bands // 2)

    @pl.when(middle)
    def _():
        finish_groups(first, count, 0, par, base, gain, fix, split, turned, total)

    @pl.when(jnp.logical_not(middle))
    def _():
        finish_groups(first, count, first, par, base, gain, fix, straight, turned, total)


def first_kernel(bands, par, base, gain, fix, straight, split, turned, total):
    total[...] = jnp.zeros((16, LANES), jnp.float32)
    finish_either(bands, 0, FIRST_GROUPS, par, base, gain, fix, straight, split, turned, total)


def last_kernel(
    bands, par, base, gain, fix, straight, split, done, before, result, turned, total, out, sems
):
    odd = lax.rem(lax.axis_index("band"), 2)
    later = GROUPS - FIRST_GROUPS
    total[...] = before[...]
    finish_either(bands, FIRST_GROUPS, later, par, base, gain, fix, straight, split, turned, total)
    scale = 2.0 / (NF * ND)
    steep_a = jnp.sum(total[0:8, :], axis=0, keepdims=True) * scale
    steep_b = jnp.sum(total[8:16, :], axis=0, keepdims=True) * scale
    sea_a, sea_b = wide_row(par, SEA_A), wide_row(par, SEA_B)
    w0_a, w0_b = wide_row(par, W0_A), wide_row(par, W0_B)
    w1_a, w1_b = wide_row(par, W1_A), wide_row(par, W1_B)

    def copy_out(g):
        rows = pl.ds(pl.multiple_of(g * GROUP_ROWS, 8), GROUP_ROWS)
        return pltpu.make_async_copy(out.at[rows], result.at[rows], sems.at[g])

    def one_group(first, ref, g, carry):
        coupling, weight = carry
        start = (first + g) * GROUP_ROWS
        gain_a = sea_a / (1.0 + weight * steep_a)
        gain_b = sea_b / (1.0 + weight * steep_b)
        wa0, wa1 = w0_a * coupling, w1_a * coupling
        wb0, wb1 = w0_b * coupling, w1_b * coupling
        for d in range(HALF):
            at = pl.multiple_of(g * (HALF * 16) + d * 16, 8)
            growth_a = jnp.maximum(wa0 * COS[d] + wa1 * SIN[d] + (1.0 - GROWTH), 1.0)
            growth_b = jnp.maximum(wb0 * COS[d] + wb1 * SIN[d] + (1.0 - GROWTH), 1.0)
            out[pl.ds(start + 2 * d + odd, 8, stride=ND), :] = (
                ref[pl.ds(at, 8), :] * gain_a * growth_a
            )
            out[pl.ds(start + 2 * d + 1 - odd, 8, stride=ND), :] = (
                ref[pl.ds(at + 8, 8), :] * gain_b * growth_b
            )
        copy_out(first + g).start()
        return coupling * FREQ_STEP**GF, weight + GF / NF

    k = lax.broadcasted_iota(jnp.int32, (8, LANES), 0)
    coupling = jnp.zeros((8, LANES), jnp.float32)
    for i in range(GF):
        for h in range(2):
            value = GROWTH * WIND_COUPLING * FREQ_STEP**i * (1.0 - 2.0 * h)
            coupling = jnp.where(k == 2 * i + h, value, coupling)
    carry = (coupling, freq_weight())
    carry = lax.fori_loop(0, FIRST_GROUPS, functools.partial(one_group, 0, done), carry)
    lax.fori_loop(0, later, functools.partial(one_group, FIRST_GROUPS, turned), carry)
    for g in range(GROUPS):
        copy_out(g).wait()


def geometry_table(bands):
    total = 2 * bands

    def angle(position):
        return (LAT_SOUTH + (LAT_NORTH - LAT_SOUTH) * position / total) * (math.pi / 180.0)

    table = np.zeros((bands, 8), np.float32)
    for b in range(bands):
        cells = [angle(2 * b + 0.5), angle(2 * b + 1.5)]
        faces = [angle(2 * b), angle(2 * b + 1), angle(2 * b + 2)]
        icos = [1.0 / math.cos(v) for v in cells]
        near, far = (0, 1) if b % 2 == 0 else (1, 0)
        face_a, face_b = (faces[0], faces[2]) if b % 2 == 0 else (faces[2], faces[0])
        table[b] = [
            icos[0],
            icos[1],
            math.cos(face_a) * icos[near],
            math.cos(faces[1]) * icos[near],
            math.cos(faces[1]) * icos[far],
            math.cos(face_b) * icos[far],
            -TURNING * math.tan(cells[near]),
            -TURNING * math.tan(cells[far]),
        ]
    return table


def speed_table():
    table = np.zeros((2, WIDE), np.float32)
    for k in range(NF * ND):
        value = SPEED_TOP * FREQ_STEP ** -(k // ND) * math.cos(2.0 * math.pi * (k % ND) / ND)
        table[0, 2 * k] = value
        table[1, 2 * k + 1] = value
    return table


VMEM = pl.BlockSpec(memory_space=pltpu.VMEM)
SMEM = pl.BlockSpec(memory_space=pltpu.SMEM)
HBM = pl.BlockSpec(memory_space=pltpu.HBM)
ANY = pl.BlockSpec(memory_space=pl.ANY)
PARAMS = pltpu.CompilerParams(vmem_limit_bytes=40 * 1024 * 1024)


def call(kernel, name, operands, specs, shapes, scratch, micros, outs_in=None, flops=0):
    outs = [jax.ShapeDtypeStruct(s, jnp.float32) for s in shapes]
    return pl.pallas_call(
        kernel,
        name=name,
        out_shape=outs,
        in_specs=specs,
        out_specs=[outs_in or VMEM] * len(outs),
        scratch_shapes=scratch,
        compiler_params=PARAMS,
        cost_estimate=pl.CostEstimate(
            flops=flops, bytes_accessed=int(micros * 3.0e6), transcendentals=0
        ),
    )(*operands)


def swapped(pairs):
    return pairs + [(t, s) for s, t in pairs]


def per_device(bands, spec_count, spectra, sea_mask, wind, current):
    comp_count, row_count, col_count = spectra.shape
    cells = spectra.reshape(comp_count * row_count, col_count)
    middle = bands // 2 - 1
    first_rows = FIRST_GROUPS * GROUP_ROWS
    last_rows = ROWS - first_rows

    (own,) = call(
        pack_kernel,
        "pack_forcing",
        tuple(pltpu.with_memory_space_constraint(v, pltpu.HBM) for v in (wind, current, sea_mask)),
        [HBM] * 3,
        [(16, LANES)],
        [
            pltpu.VMEM(wind.shape, jnp.float32),
            pltpu.VMEM(current.shape, jnp.float32),
            pltpu.VMEM(sea_mask.shape, jnp.int32),
            pltpu.SemaphoreType.DMA((3,)),
        ],
        0.3,
    )
    order = [0]

    def gathered(values, bit):
        order.extend([r ^ bit for r in order])
        other = lax.ppermute(values, "band", [(b, b ^ bit) for b in range(bands)])
        return jnp.concatenate([values, other], axis=0)

    forcing = gathered(own, 2)

    part_relayed, part_direct = call(
        split_kernel,
        "split",
        (pltpu.with_memory_space_constraint(cells, pltpu.HBM), own),
        [HBM, VMEM],
        [(first_rows, LANES), (last_rows, LANES)],
        [pltpu.SemaphoreType.DMA((2,))],
        1.0,
    )
    part_relayed, forcing, ends_sea = lax.optimization_barrier((part_relayed, forcing, sea_mask))
    straight = lax.ppermute(
        cells, "band", swapped([(b, b + 1) for b in range(1, bands - 1, 2) if b != middle])
    )
    west, east = call(
        ends_kernel,
        "ends",
        (cells, ends_sea),
        [VMEM] * 2,
        [(2, WIDE), (2, WIDE)],
        [pltpu.VMEM((LANES, LANES), jnp.float32)],
        1.0,
    )
    part_relayed, west, east = lax.optimization_barrier((part_relayed, west, east))
    relay = lax.ppermute(part_relayed, "band", [(middle, bands - 1), (middle + 1, 0)])
    bit = 4
    while bit < bands:
        forcing = gathered(forcing, bit)
        bit *= 2
    part_relayed, part_direct, forcing, west, east = lax.optimization_barrier(
        (part_relayed, part_direct, forcing, west, east)
    )
    pairs = [(b, b + 1) for b in range(0, bands, 2)]
    forcing = gathered(forcing, 1)
    beyond = [lax.ppermute(part, "band", swapped(pairs)) for part in (part_relayed, part_direct)]
    part_direct, forcing = lax.optimization_barrier((part_direct, forcing))
    direct = lax.ppermute(
        part_direct, "band", [(middle, middle + 1), (middle + 1, middle)]
    )

    par, first_here, second_here = call(
        functools.partial(table_kernel, bands, tuple(order)),
        "tables",
        (jnp.asarray(geometry_table(bands)), forcing, west, east),
        [SMEM, VMEM, VMEM, VMEM],
        [(PAR_ROWS, LANES), (2, WIDE), (2, WIDE)],
        [pltpu.VMEM((8 * bands, LANES), jnp.float32)],
        0.3,
        flops=4300000000,
    )
    relay, par = lax.optimization_barrier((relay, par))
    relayed = lax.ppermute(relay, "band", [(bands - 1, middle + 1), (0, middle)])
    ring = [(s, (s + 1) % spec_count) for s in range(spec_count)]
    first_there = lax.ppermute(first_here, "spec", swapped(ring[1::2]))
    second_there = lax.ppermute(second_here, "spec", swapped(ring[0::2]))
    base_first, base_last, gain_first, gain_last = call(
        base_kernel,
        "base",
        (par, cells, *beyond),
        [VMEM] * 4,
        [
            (first_rows, LANES),
            (last_rows, LANES),
            (first_rows * 3 // 2, LANES),
            (last_rows * 3 // 2, LANES),
        ],
        [],
        4.0,
    )
    base_first, first_there, second_there = lax.optimization_barrier(
        (base_first, first_there, second_there)
    )
    (fix,) = call(
        fix_kernel,
        "fix",
        (jnp.asarray(speed_table()), par, first_here, second_here, first_there, second_there),
        [VMEM] * 6,
        [(WIDE, LANES)],
        [pltpu.VMEM((LANES, WIDE), jnp.float32)],
        1.0,
    )
    turned, total = call(
        functools.partial(first_kernel, bands),
        "first_groups",
        (par, base_first, gain_first, fix, straight, relayed),
        [VMEM] * 6,
        [(first_rows, LANES), (16, LANES)],
        [],
        1.0,
    )
    (out,) = call(
        functools.partial(last_kernel, bands),
        "last_groups",
        (par, base_last, gain_last, fix, straight, direct, turned, total),
        [VMEM] * 8,
        [(ROWS, LANES)],
        [
            pltpu.VMEM((last_rows, LANES), jnp.float32),
            pltpu.VMEM((16, LANES), jnp.float32),
            pltpu.VMEM((ROWS, LANES), jnp.float32),
            pltpu.SemaphoreType.DMA((GROUPS,)),
        ],
        2.0,
        outs_in=ANY,
    )
    return out.reshape(comp_count, row_count, col_count)


def solution(mesh):
    placed = (
        P(None, "band", "spec"),
        P("band", "spec"),
        P(None, None, ("spec", "band")),
        P(None, None, ("spec", "band")),
    )
    return jax.shard_map(
        functools.partial(per_device, mesh.shape["band"], mesh.shape["spec"]),
        mesh=mesh,
        in_specs=placed,
        out_specs=P(None, "band", "spec"),
        check_vma=False,
    )
```

```python
import functools
import math

import jax
import jax.numpy as jnp
import numpy as np
from jax import lax
from jax.experimental import pallas as pl
from jax.experimental.pallas import tpu as pltpu
from jax.sharding import PartitionSpec as P

NF = 36
ND = 36
HALF = ND // 2
LAT_SOUTH = 30.0
LAT_NORTH = 55.0
SPEED_TOP = 0.35
FREQ_STEP = 1.1
TURNING = 1.5
GROWTH = 0.05
WIND_COUPLING = 0.04

GF = 4
GROUPS = NF // GF
GROUP_ROWS = GF * ND * 2
FIRST_GROUPS = 4
LANES = 128
ROWS = NF * ND * 2
WIDE = -(-(ROWS + 2) // LANES) * LANES

COS = [math.cos(2.0 * math.pi * d / ND) for d in range(HALF + 1)]
SIN = [math.sin(2.0 * math.pi * d / ND) for d in range(HALF + 1)]

(
    CUR_A,
    CUR_M,
    CUR_B,
    CX_A,
    CX_B,
    W0_A,
    W0_B,
    W1_A,
    W1_B,
    SEA_A,
    SEA_B,
    SEA_A1,
    SEA_A2,
    SEA_B1,
    SEA_B2,
    TAU,
    ICOS_A,
    ICOS_B,
    KAP_A,
    MU_A,
    MU_B,
    KAP_B,
    TAN_A,
    TAN_B,
    ICOS_0,
    ICOS_1,
) = range(26)
PAR_ROWS = 32


def flux(lo2, lo1, hi1, hi2, c):
    forward = c >= 0.0
    source = jnp.where(forward, lo1, hi1)
    upwind = jnp.where(forward, lo2, hi2)
    both = lo1 + hi1
    bend = both - 3.0 * source + upwind
    w = (1.0 / 6.0) - (c * c) * (1.0 / 6.0)
    return c * (0.5 * (both - c * (hi1 - lo1)) - w * bend)


def group_speed():
    k = lax.broadcasted_iota(jnp.int32, (8, LANES), 0)
    speed = jnp.zeros((8, LANES), jnp.float32)
    for i in range(GF):
        for h in range(2):
            value = SPEED_TOP * FREQ_STEP**-i * (1.0 - 2.0 * h)
            speed = jnp.where(k == 2 * i + h, value, speed)
    return speed


def freq_weight():
    k = lax.broadcasted_iota(jnp.int32, (8, LANES), 0)
    weight = jnp.zeros((8, LANES), jnp.float32)
    for i in range(GF):
        weight = jnp.where(lax.div(k, 2) == i, (i + 1.0) / NF, weight)
    return weight


def swap_halves(v):
    k = lax.broadcasted_iota(jnp.int32, (8, LANES), 0)
    return jnp.where(lax.rem(k, 2) == 0, pltpu.roll(v, 7, 0), pltpu.roll(v, 1, 0))


def wide_row(par, index):
    return jnp.broadcast_to(par[index : index + 1, :], (8, LANES))


def pack_kernel(wind, current, sea, out, wind_here, current_here, sea_here, sems):
    rows, strip = wind.shape[1], wind.shape[2]
    copies = [
        pltpu.make_async_copy(wind, wind_here, sems.at[0]),
        pltpu.make_async_copy(current, current_here, sems.at[1]),
        pltpu.make_async_copy(sea, sea_here, sems.at[2]),
    ]
    for copy in copies:
        copy.start()
    empty = jnp.zeros((8, LANES - strip), jnp.float32)
    for copy in copies:
        copy.wait()
    packed = jnp.zeros((8, LANES), jnp.float32)
    piece = 0
    for ref in (current_here, wind_here):
        for axis in range(2):
            for row in range(0, rows, 8):
                wide = jnp.concatenate([ref[axis, row : row + 8, :], empty], axis=1)
                packed = packed + (pltpu.roll(wide, piece * strip, 1) if piece else wide)
                piece += 1
    out[0:8, :] = packed
    out[8:10, :] = sea_here[...].astype(jnp.float32)
    out[10:16, :] = jnp.zeros((6, LANES), jnp.float32)


def part_kernel(first, source, when, part, sem):
    del when
    copy = pltpu.make_async_copy(source.at[first : first + part.shape[0]], part, sem)
    copy.start()
    copy.wait()


def ends_kernel(spectra, sea, west, east, line):
    seas = sea[...].astype(jnp.float32)
    sub = lax.broadcasted_iota(jnp.int32, (LANES, LANES), 0)
    both = jnp.where(
        lax.rem(sub, 2) == 0,
        jnp.broadcast_to(seas[0:1], (LANES, LANES)),
        jnp.broadcast_to(seas[1:2], (LANES, LANES)),
    )
    full = ROWS // LANES
    for block in range(WIDE // LANES):
        at = block * LANES
        if block < full:
            cells = spectra[at : at + LANES, :] * both
        else:
            left = ROWS - at
            line[...] = jnp.zeros((LANES, LANES), jnp.float32)
            line[0:left, :] = spectra[at : at + left, :] * both[0:left]
            cells = line[...]
        turned = cells.T
        west[:, at : at + LANES] = turned[0:2]
        east[:, at : at + LANES] = turned[LANES - 2 : LANES]


def table_kernel(bands, order, geometry, slots, west_in, east_in, par, first, second, line):
    me = lax.axis_index("band")
    is_even = lax.rem(me, 2) == 0
    rows = 2 * bands
    strip = LANES // bands
    block = lax.div(lax.broadcasted_iota(jnp.int32, (8, LANES), 1), strip)
    sources = [jnp.bitwise_xor(me, r) for r in order]
    moved = [
        pltpu.roll(slots[16 * k : 16 * k + 8, :], source * strip, 1)
        for k, source in enumerate(sources)
    ]
    for piece in range(rows // 2):
        row = jnp.zeros((8, LANES), jnp.float32)
        for source, values in zip(sources, moved):
            row = jnp.where(block == lax.rem(source + piece, bands), values, row)
        line[8 * piece : 8 * piece + 8, :] = (
            pltpu.roll(row, LANES - piece * strip, 1) if piece else row
        )

    def mask_of(band):
        found = jnp.zeros((2, LANES), jnp.float32)
        for k, source in enumerate(sources):
            found = jnp.where(source == band, slots[16 * k + 8 : 16 * k + 10, :], found)
        return [found[0:1], found[1:2]]

    seas = mask_of(me - 1) + mask_of(me) + mask_of(me + 1)
    row = 2 * me
    has_south = jnp.where(me > 0, 1.0, 0.0)
    has_north = jnp.where(me < bands - 1, 1.0, 0.0)

    def around(part):
        first = part * rows
        south = line[pl.ds(first + jnp.maximum(row - 1, 0), 1), :] * has_south
        north = line[pl.ds(first + jnp.minimum(row + 2, rows - 1), 1), :] * has_north
        return [south] + [line[pl.ds(first + row + i, 1), :] for i in range(2)] + [north]

    def pick(low, high):
        return jnp.where(is_even, low, high)

    def put(index, value):
        par[index : index + 1, :] = jnp.broadcast_to(value, (1, LANES))

    tau = jnp.where(is_even, 1.0, -1.0)
    north = around(1)
    face = [0.5 * (north[i] + north[i + 1]) for i in range(3)]
    put(CUR_A, tau * pick(face[0], face[2]))
    put(CUR_M, tau * face[1])
    put(CUR_B, tau * pick(face[2], face[0]))
    lane = lax.broadcasted_iota(jnp.int32, (1, LANES), 1)
    inside = jnp.where(lane == 0, 0.0, 1.0)
    east_speed = around(0)[1:3]
    wind_0, wind_1 = around(2)[1:3], around(3)[1:3]
    shifted = [0.5 * inside * (v + pltpu.roll(v, 1, 1)) for v in east_speed]
    put(CX_A, pick(shifted[0], shifted[1]))
    put(CX_B, pick(shifted[1], shifted[0]))
    put(W0_A, pick(wind_0[0], wind_0[1]))
    put(W0_B, pick(wind_0[1], wind_0[0]))
    put(W1_A, pick(wind_1[0], wind_1[1]))
    put(W1_B, pick(wind_1[1], wind_1[0]))
    put(SEA_A, pick(seas[2], seas[3]))
    put(SEA_B, pick(seas[3], seas[2]))
    put(SEA_A1, pick(seas[1], seas[4]))
    put(SEA_A2, pick(seas[0], seas[5]))
    put(SEA_B1, pick(seas[4], seas[1]))
    put(SEA_B2, pick(seas[5], seas[0]))
    put(TAU, tau)
    icos = [geometry[me, 0], geometry[me, 1]]
    put(ICOS_A, inside * pick(icos[0], icos[1]))
    put(ICOS_B, inside * pick(icos[1], icos[0]))
    put(KAP_A, geometry[me, 2])
    put(MU_A, geometry[me, 3])
    put(MU_B, geometry[me, 4])
    put(KAP_B, geometry[me, 5])
    put(TAN_A, geometry[me, 6])
    put(TAN_B, geometry[me, 7])
    put(ICOS_0, icos[0])
    put(ICOS_1, icos[1])
    par[26:32, :] = jnp.zeros((6, LANES), jnp.float32)

    ends = []
    for values, columns in ((west_in[...], (0, 1)), (east_in[...], (LANES - 2, LANES - 1))):
        lane = lax.broadcasted_iota(jnp.int32, values.shape, 1)
        for i in range(2):
            pair = jnp.concatenate([east_speed[i][:, j : j + 1] for j in columns], axis=0)
            values = jnp.where(lane == ROWS + i, pair, values)
        ends.append(values)
    even_spec = lax.rem(lax.axis_index("spec"), 2) == 0
    first[...] = jnp.where(even_spec, ends[0], ends[1])
    second[...] = jnp.where(even_spec, ends[1], ends[0])


def fix_kernel(table, par, first_here, second_here, first_there, second_there, fix, tall):
    even_spec = lax.rem(lax.axis_index("spec"), 2) == 0
    west = jnp.where(even_spec, first_here[...], second_here[...])
    east = jnp.where(even_spec, second_here[...], first_here[...])
    from_west = jnp.where(even_spec, first_there[...], second_there[...])
    from_east = jnp.where(even_spec, second_there[...], first_there[...])
    lane = lax.broadcasted_iota(jnp.int32, (1, WIDE), 1)
    even_row = lax.rem(lane, 2) == 0
    speed = table[0:1] * par[ICOS_0 : ICOS_0 + 1, 0:1] + table[1:2] * par[ICOS_1 : ICOS_1 + 1, 0:1]

    def column(ref, row):
        cells = ref[row : row + 1, :]
        drift = jnp.where(even_row, cells[:, ROWS : ROWS + 1], cells[:, ROWS + 1 : ROWS + 2])
        return cells, drift

    xm2, _ = column(from_west, 0)
    xm1, dm1 = column(from_west, 1)
    x0, d0 = column(west, 0)
    x1, d1 = column(west, 1)
    y2, d2 = column(east, 0)
    y1, dy1 = column(east, 1)
    z0, dz0 = column(from_east, 0)
    z1, _ = column(from_east, 1)
    first = flux(xm2, xm1, x0, x1, speed + 0.5 * (dm1 + d0))
    last = flux(y2, y1, z0, z1, speed + 0.5 * (dy1 + dz0))
    c = speed + 0.5 * (d0 + d1)
    second = jnp.where(c >= 0.0, -c * (1.0 - c * c) * (1.0 / 6.0), 0.0) * (xm1 - y1)
    c = speed + 0.5 * (d2 + dy1)
    before = jnp.where(c >= 0.0, 0.0, -c * (1.0 - c * c) * (1.0 / 6.0)) * (z0 - x0)
    tall[...] = jnp.zeros(tall.shape, jnp.float32)
    for block in range(WIDE // LANES):
        at = block * LANES
        piece = slice(at, at + LANES)
        slot = block % tall.shape[0]
        tall[slot, 0:1, :] = first[:, piece] - second[:, piece]
        tall[slot, 1:2, :] = second[:, piece]
        tall[slot, LANES - 2 : LANES - 1, :] = -before[:, piece]
        tall[slot, LANES - 1 : LANES, :] = before[:, piece] - last[:, piece]
        fix[piece, :] = tall[slot].T


def base_kernel(par, spectra, beyond_first, beyond_last, base_first, base_last, gain_first, gain_last):
    odd = lax.rem(lax.axis_index("band"), 2)
    sea_a, sea_b = wide_row(par, SEA_A), wide_row(par, SEA_B)
    sea_b1, sea_b2 = wide_row(par, SEA_B1), wide_row(par, SEA_B2)
    sea_a1 = wide_row(par, SEA_A1)
    into_a1 = wide_row(par, KAP_A) * sea_a1
    into_a2 = wide_row(par, KAP_A) * wide_row(par, SEA_A2)
    over_a, over_b = wide_row(par, MU_A) * sea_a1, wide_row(par, MU_B) * sea_a1
    cur_a, cur_m, cur_b = wide_row(par, CUR_A), wide_row(par, CUR_M), wide_row(par, CUR_B)
    cx_a, cx_b = wide_row(par, CX_A), wide_row(par, CX_B)
    kap_a, mu_a = wide_row(par, KAP_A), wide_row(par, MU_A)
    mu_b, kap_b = wide_row(par, MU_B), wide_row(par, KAP_B)
    tau = wide_row(par, TAU)
    icos_a, icos_b = wide_row(par, ICOS_A), wide_row(par, ICOS_B)

    def along_east(x, speed_x, current_x, cosine):
        crossing = flux(
            pltpu.roll(x, 2, 1),
            pltpu.roll(x, 1, 1),
            x,
            pltpu.roll(x, LANES - 1, 1),
            speed_x * cosine + current_x,
        )
        return crossing - pltpu.roll(crossing, LANES - 1, 1)

    def one_group(base, gain, beyond, first, g, speeds):
        start = (first + g) * GROUP_ROWS
        far = g * GROUP_ROWS
        north = speeds * tau
        east_a, east_b = speeds * icos_a, speeds * icos_b
        for d in range(HALF):
            row_a = pl.ds(start + 2 * d + odd, 8, stride=ND)
            row_b = pl.ds(start + 2 * d + 1 - odd, 8, stride=ND)
            a = spectra[row_a, :] * sea_a
            b = spectra[row_b, :] * sea_b
            b1 = beyond[pl.ds(far + 2 * d + odd, 8, stride=ND), :] * sea_b1
            b2 = beyond[pl.ds(far + 2 * d + 1 - odd, 8, stride=ND), :] * sea_b2
            c = north * SIN[d] + cur_a
            w = (1.0 / 6.0) - (c * c) * (1.0 / 6.0)
            inward = c >= 0.0
            cw = c * w
            half = 0.5 * c
            flux_a = (half - half * c) * a - cw * jnp.where(inward, a, b - 2.0 * a)
            cm = north * SIN[d] + cur_m
            flux_m = flux(0.0, a, b, b1, cm)
            away = jnp.where(cm >= 0.0, cm * ((cm * cm) * (1.0 / 6.0) - (1.0 / 6.0)), 0.0)
            flux_b = flux(a, b, b1, b2, north * SIN[d] + cur_b)
            to_a = along_east(a, east_a, cx_a, COS[d])
            to_b = along_east(b, east_b, cx_b, COS[d])
            at = pl.multiple_of(g * (HALF * 16) + d * 16, 8)
            base[pl.ds(at, 8), :] = a + to_a + kap_a * flux_a - mu_a * flux_m
            base[pl.ds(at + 8, 8), :] = b + to_b + mu_b * flux_m - kap_b * flux_b
            at = pl.multiple_of(g * (HALF * 24) + d * 24, 8)
            near = half + half * c + jnp.where(inward, 2.0 * cw, -cw)
            gain[pl.ds(at, 8), :] = into_a1 * near - over_a * away
            gain[pl.ds(at + 8, 8), :] = into_a2 * jnp.where(inward, -cw, 0.0)
            gain[pl.ds(at + 16, 8), :] = over_b * away
        return speeds * FREQ_STEP**-GF

    speeds = lax.fori_loop(
        0, FIRST_GROUPS, functools.partial(one_group, base_first, gain_first, beyond_first, 0), group_speed()
    )
    lax.fori_loop(
        0,
        GROUPS - FIRST_GROUPS,
        functools.partial(one_group, base_last, gain_last, beyond_last, FIRST_GROUPS),
        speeds,
    )


def turn(cells, rate):
    k = lax.broadcasted_iota(jnp.int32, (8, LANES), 0)
    first = lax.rem(k, 2) == 0
    cube = rate * rate * rate
    ring = [swap_halves(cells[HALF - 1])] + cells
    ring = ring + [swap_halves(cells[0]), swap_halves(cells[1])]
    steps = [high - low for low, high in zip(ring, ring[1:])]
    bends = [high - low for low, high in zip(steps, steps[1:])]
    fluxes = []
    for d in range(HALF):
        mean = 0.5 * (COS[d] + COS[d + 1])
        low, high = (bends[d + 1], bends[d]) if mean > 0 else (bends[d], bends[d + 1])
        bend = jnp.where(first, low, high)
        both = ring[d + 1] + ring[d + 2]
        weight = rate * (mean / 6.0) - cube * (mean**3 / 6.0)
        fluxes.append(
            (rate * (0.5 * mean)) * (both - (rate * mean) * steps[d + 1]) - weight * bend
        )
    last = swap_halves(fluxes[HALF - 1])
    return [cells[d] - (fluxes[d] - (fluxes[d - 1] if d else last)) for d in range(HALF)]


def finish_groups(first, count, skip, par, base, gain, fix, ahead, turned, total):
    odd = lax.rem(lax.axis_index("band"), 2)
    tan_a, tan_b = wide_row(par, TAN_A), wide_row(par, TAN_B)

    def one_group(g, carry):
        speeds, weight, sum_a, sum_b = carry
        start = (skip + g) * GROUP_ROWS
        fix_start = (first + g) * GROUP_ROWS
        cells_a, cells_b = [], []
        for d in range(HALF):
            n1 = ahead[pl.ds(start + 2 * d + 1 - odd, 8, stride=ND), :]
            n2 = ahead[pl.ds(start + 2 * d + odd, 8, stride=ND), :]
            fix_a = fix[pl.ds(fix_start + 2 * d + odd, 8, stride=ND), :]
            fix_b = fix[pl.ds(fix_start + 2 * d + 1 - odd, 8, stride=ND), :]
            at = pl.multiple_of(g * (HALF * 16) + d * 16, 8)
            by = pl.multiple_of(g * (HALF * 24) + d * 24, 8)
            cells_a.append(
                base[pl.ds(at, 8), :]
                + fix_a
                + gain[pl.ds(by, 8), :] * n1
                + gain[pl.ds(by + 8, 8), :] * n2
            )
            cells_b.append(base[pl.ds(at + 8, 8), :] + fix_b + gain[pl.ds(by + 16, 8), :] * n1)
        square_a = square_b = 0.0
        for d, v in enumerate(turn(cells_a, speeds * tan_a)):
            at = pl.multiple_of(g * (HALF * 16) + d * 16, 8)
            turned[pl.ds(at, 8), :] = v
            square_a = square_a + v * v
        for d, v in enumerate(turn(cells_b, speeds * tan_b)):
            at = pl.multiple_of(g * (HALF * 16) + d * 16 + 8, 8)
            turned[pl.ds(at, 8), :] = v
            square_b = square_b + v * v
        return (
            speeds * FREQ_STEP**-GF,
            weight + GF / NF,
            sum_a + weight * square_a,
            sum_b + weight * square_b,
        )

    speeds = group_speed() * FREQ_STEP ** -(GF * first)
    weight = freq_weight() + GF * first / NF
    carry = (speeds, weight, total[0:8, :], total[8:16, :])
    _, _, total[0:8, :], total[8:16, :] = lax.fori_loop(0, count, one_group, carry)


def finish_either(bands, first, count, par, base, gain, fix, straight, split, turned, total):
    me = lax.axis_index("band")
    middle = jnp.logical_or(me == bands // 2 - 1, me == bands // 2)

    @pl.when(middle)
    def _():
        finish_groups(first, count, 0, par, base, gain, fix, split, turned, total)

    @pl.when(jnp.logical_not(middle))
    def _():
        finish_groups(first, count, first, par, base, gain, fix, straight, turned, total)


def first_kernel(bands, par, base, gain, fix, straight, split, turned, total):
    total[...] = jnp.zeros((16, LANES), jnp.float32)
    finish_either(bands, 0, FIRST_GROUPS, par, base, gain, fix, straight, split, turned, total)


def last_kernel(
    bands, par, base, gain, fix, straight, split, done, before, result, turned, total, out, sems
):
    odd = lax.rem(lax.axis_index("band"), 2)
    later = GROUPS - FIRST_GROUPS
    total[...] = before[...]
    finish_either(bands, FIRST_GROUPS, later, par, base, gain, fix, straight, split, turned, total)
    scale = 2.0 / (NF * ND)
    steep_a = jnp.sum(total[0:8, :], axis=0, keepdims=True) * scale
    steep_b = jnp.sum(total[8:16, :], axis=0, keepdims=True) * scale
    sea_a, sea_b = wide_row(par, SEA_A), wide_row(par, SEA_B)
    w0_a, w0_b = wide_row(par, W0_A), wide_row(par, W0_B)
    w1_a, w1_b = wide_row(par, W1_A), wide_row(par, W1_B)

    def copy_out(g):
        rows = pl.ds(pl.multiple_of(g * GROUP_ROWS, 8), GROUP_ROWS)
        return pltpu.make_async_copy(out.at[rows], result.at[rows], sems.at[g])

    def one_group(first, ref, g, carry):
        coupling, weight = carry
        start = (first + g) * GROUP_ROWS
        gain_a = sea_a / (1.0 + weight * steep_a)
        gain_b = sea_b / (1.0 + weight * steep_b)
        wa0, wa1 = w0_a * coupling, w1_a * coupling
        wb0, wb1 = w0_b * coupling, w1_b * coupling
        for d in range(HALF):
            at = pl.multiple_of(g * (HALF * 16) + d * 16, 8)
            growth_a = jnp.maximum(wa0 * COS[d] + wa1 * SIN[d] + (1.0 - GROWTH), 1.0)
            growth_b = jnp.maximum(wb0 * COS[d] + wb1 * SIN[d] + (1.0 - GROWTH), 1.0)
            out[pl.ds(start + 2 * d + odd, 8, stride=ND), :] = (
                ref[pl.ds(at, 8), :] * gain_a * growth_a
            )
            out[pl.ds(start + 2 * d + 1 - odd, 8, stride=ND), :] = (
                ref[pl.ds(at + 8, 8), :] * gain_b * growth_b
            )
        copy_out(first + g).start()
        return coupling * FREQ_STEP**GF, weight + GF / NF

    k = lax.broadcasted_iota(jnp.int32, (8, LANES), 0)
    coupling = jnp.zeros((8, LANES), jnp.float32)
    for i in range(GF):
        for h in range(2):
            value = GROWTH * WIND_COUPLING * FREQ_STEP**i * (1.0 - 2.0 * h)
            coupling = jnp.where(k == 2 * i + h, value, coupling)
    carry = (coupling, freq_weight())
    carry = lax.fori_loop(0, FIRST_GROUPS, functools.partial(one_group, 0, done), carry)
    lax.fori_loop(0, later, functools.partial(one_group, FIRST_GROUPS, turned), carry)
    for g in range(GROUPS):
        copy_out(g).wait()


def geometry_table(bands):
    total = 2 * bands

    def angle(position):
        return (LAT_SOUTH + (LAT_NORTH - LAT_SOUTH) * position / total) * (math.pi / 180.0)

    table = np.zeros((bands, 8), np.float32)
    for b in range(bands):
        cells = [angle(2 * b + 0.5), angle(2 * b + 1.5)]
        faces = [angle(2 * b), angle(2 * b + 1), angle(2 * b + 2)]
        icos = [1.0 / math.cos(v) for v in cells]
        near, far = (0, 1) if b % 2 == 0 else (1, 0)
        face_a, face_b = (faces[0], faces[2]) if b % 2 == 0 else (faces[2], faces[0])
        table[b] = [
            icos[0],
            icos[1],
            math.cos(face_a) * icos[near],
            math.cos(faces[1]) * icos[near],
            math.cos(faces[1]) * icos[far],
            math.cos(face_b) * icos[far],
            -TURNING * math.tan(cells[near]),
            -TURNING * math.tan(cells[far]),
        ]
    return table


def speed_table():
    table = np.zeros((2, WIDE), np.float32)
    for k in range(NF * ND):
        value = SPEED_TOP * FREQ_STEP ** -(k // ND) * math.cos(2.0 * math.pi * (k % ND) / ND)
        table[0, 2 * k] = value
        table[1, 2 * k + 1] = value
    return table


VMEM = pl.BlockSpec(memory_space=pltpu.VMEM)
SMEM = pl.BlockSpec(memory_space=pltpu.SMEM)
HBM = pl.BlockSpec(memory_space=pltpu.HBM)
ANY = pl.BlockSpec(memory_space=pl.ANY)
PARAMS = pltpu.CompilerParams(vmem_limit_bytes=40 * 1024 * 1024)


def call(kernel, name, operands, specs, shapes, scratch, micros, outs_in=None, flops=0):
    outs = [jax.ShapeDtypeStruct(s, jnp.float32) for s in shapes]
    return pl.pallas_call(
        kernel,
        name=name,
        out_shape=outs,
        in_specs=specs,
        out_specs=[outs_in or VMEM] * len(outs),
        scratch_shapes=scratch,
        compiler_params=PARAMS,
        cost_estimate=pl.CostEstimate(
            flops=flops, bytes_accessed=int(micros * 3.0e6), transcendentals=0
        ),
    )(*operands)


def swapped(pairs):
    return pairs + [(t, s) for s, t in pairs]


def per_device(bands, spec_count, spectra, sea_mask, wind, current):
    comp_count, row_count, col_count = spectra.shape
    cells = spectra.reshape(comp_count * row_count, col_count)
    middle = bands // 2 - 1
    first_rows = FIRST_GROUPS * GROUP_ROWS
    last_rows = ROWS - first_rows

    (own,) = call(
        pack_kernel,
        "pack_forcing",
        tuple(pltpu.with_memory_space_constraint(v, pltpu.HBM) for v in (wind, current, sea_mask)),
        [HBM] * 3,
        [(16, LANES)],
        [
            pltpu.VMEM(wind.shape, jnp.float32),
            pltpu.VMEM(current.shape, jnp.float32),
            pltpu.VMEM(sea_mask.shape, jnp.int32),
            pltpu.SemaphoreType.DMA((3,)),
        ],
        0.3,
    )
    order = [0]

    def gathered(values, bit):
        order.extend([r ^ bit for r in order])
        other = lax.ppermute(values, "band", [(b, b ^ bit) for b in range(bands)])
        return jnp.concatenate([values, other], axis=0)

    forcing = gathered(own, 2)

    def part_of(first, rows, name, when):
        (part,) = call(
            functools.partial(part_kernel, first),
            name,
            (pltpu.with_memory_space_constraint(cells, pltpu.HBM), when),
            [HBM, VMEM],
            [(rows, LANES)],
            [pltpu.SemaphoreType.DMA],
            1.0,
        )
        return part

    part_relayed = part_of(0, first_rows, "part_relayed", own)
    part_relayed, forcing, ends_sea = lax.optimization_barrier((part_relayed, forcing, sea_mask))
    straight = lax.ppermute(
        cells, "band", swapped([(b, b + 1) for b in range(1, bands - 1, 2) if b != middle])
    )
    west, east = call(
        ends_kernel,
        "ends",
        (cells, ends_sea),
        [VMEM] * 2,
        [(2, WIDE), (2, WIDE)],
        [pltpu.VMEM((LANES, LANES), jnp.float32)],
        1.0,
    )
    part_relayed, west, east = lax.optimization_barrier((part_relayed, west, east))
    relay = lax.ppermute(part_relayed, "band", [(middle, bands - 1), (middle + 1, 0)])
    bit = 4
    while bit < bands:
        forcing = gathered(forcing, bit)
        bit *= 2
    part_direct = part_of(first_rows, last_rows, "part_direct", west)
    part_relayed, part_direct, forcing, west, east = lax.optimization_barrier(
        (part_relayed, part_direct, forcing, west, east)
    )
    pairs = [(b, b + 1) for b in range(0, bands, 2)]
    forcing = gathered(forcing, 1)
    beyond = [lax.ppermute(part, "band", swapped(pairs)) for part in (part_relayed, part_direct)]
    part_direct, forcing = lax.optimization_barrier((part_direct, forcing))
    direct = lax.ppermute(
        part_direct, "band", [(middle, middle + 1), (middle + 1, middle)]
    )

    par, first_here, second_here = call(
        functools.partial(table_kernel, bands, tuple(order)),
        "tables",
        (jnp.asarray(geometry_table(bands)), forcing, west, east),
        [SMEM, VMEM, VMEM, VMEM],
        [(PAR_ROWS, LANES), (2, WIDE), (2, WIDE)],
        [pltpu.VMEM((8 * bands, LANES), jnp.float32)],
        0.3,
        flops=4300000000,
    )
    relay, par = lax.optimization_barrier((relay, par))
    relayed = lax.ppermute(relay, "band", [(bands - 1, middle + 1), (0, middle)])
    ring = [(s, (s + 1) % spec_count) for s in range(spec_count)]
    first_there = lax.ppermute(first_here, "spec", swapped(ring[1::2]))
    second_there = lax.ppermute(second_here, "spec", swapped(ring[0::2]))
    base_first, base_last, gain_first, gain_last = call(
        base_kernel,
        "base",
        (par, cells, *beyond),
        [VMEM] * 4,
        [
            (first_rows, LANES),
            (last_rows, LANES),
            (first_rows * 3 // 2, LANES),
            (last_rows * 3 // 2, LANES),
        ],
        [],
        4.0,
    )
    base_first, first_there, second_there = lax.optimization_barrier(
        (base_first, first_there, second_there)
    )
    (fix,) = call(
        fix_kernel,
        "fix",
        (jnp.asarray(speed_table()), par, first_here, second_here, first_there, second_there),
        [VMEM] * 6,
        [(WIDE, LANES)],
        [pltpu.VMEM((4, LANES, LANES), jnp.float32)],
        1.0,
    )
    turned, total = call(
        functools.partial(first_kernel, bands),
        "first_groups",
        (par, base_first, gain_first, fix, straight, relayed),
        [VMEM] * 6,
        [(first_rows, LANES), (16, LANES)],
        [],
        1.0,
    )
    (out,) = call(
        functools.partial(last_kernel, bands),
        "last_groups",
        (par, base_last, gain_last, fix, straight, direct, turned, total),
        [VMEM] * 8,
        [(ROWS, LANES)],
        [
            pltpu.VMEM((last_rows, LANES), jnp.float32),
            pltpu.VMEM((16, LANES), jnp.float32),
            pltpu.VMEM((ROWS, LANES), jnp.float32),
            pltpu.SemaphoreType.DMA((GROUPS,)),
        ],
        2.0,
        outs_in=ANY,
    )
    return out.reshape(comp_count, row_count, col_count)


def solution(mesh):
    placed = (
        P(None, "band", "spec"),
        P("band", "spec"),
        P(None, None, ("spec", "band")),
        P(None, None, ("spec", "band")),
    )
    return jax.shard_map(
        functools.partial(per_device, mesh.shape["band"], mesh.shape["spec"]),
        mesh=mesh,
        in_specs=placed,
        out_specs=P(None, "band", "spec"),
        check_vma=False,
    )
```

```python
import functools
import math

import jax
import jax.numpy as jnp
import numpy as np
from jax import lax
from jax.experimental import pallas as pl
from jax.experimental.pallas import tpu as pltpu
from jax.sharding import PartitionSpec as P

NF = 36
ND = 36
HALF = ND // 2
LAT_SOUTH = 30.0
LAT_NORTH = 55.0
SPEED_TOP = 0.35
FREQ_STEP = 1.1
TURNING = 1.5
GROWTH = 0.05
WIND_COUPLING = 0.04

GF = 4
GROUPS = NF // GF
GROUP_ROWS = GF * ND * 2
FIRST_GROUPS = 4
LANES = 128
ROWS = NF * ND * 2
WIDE = -(-(ROWS + 2) // LANES) * LANES

COS = [math.cos(2.0 * math.pi * d / ND) for d in range(HALF + 1)]
SIN = [math.sin(2.0 * math.pi * d / ND) for d in range(HALF + 1)]

(
    CUR_A,
    CUR_M,
    CUR_B,
    CX_A,
    CX_B,
    W0_A,
    W0_B,
    W1_A,
    W1_B,
    SEA_A,
    SEA_B,
    SEA_A1,
    SEA_A2,
    SEA_B1,
    SEA_B2,
    TAU,
    ICOS_A,
    ICOS_B,
    KAP_A,
    MU_A,
    MU_B,
    KAP_B,
    TAN_A,
    TAN_B,
    ICOS_0,
    ICOS_1,
) = range(26)
PAR_ROWS = 32


def flux(lo2, lo1, hi1, hi2, c):
    forward = c >= 0.0
    source = jnp.where(forward, lo1, hi1)
    upwind = jnp.where(forward, lo2, hi2)
    both = lo1 + hi1
    bend = both - 3.0 * source + upwind
    w = (1.0 / 6.0) - (c * c) * (1.0 / 6.0)
    return c * (0.5 * (both - c * (hi1 - lo1)) - w * bend)


def group_speed():
    k = lax.broadcasted_iota(jnp.int32, (8, LANES), 0)
    speed = jnp.zeros((8, LANES), jnp.float32)
    for i in range(GF):
        for h in range(2):
            value = SPEED_TOP * FREQ_STEP**-i * (1.0 - 2.0 * h)
            speed = jnp.where(k == 2 * i + h, value, speed)
    return speed


def freq_weight():
    k = lax.broadcasted_iota(jnp.int32, (8, LANES), 0)
    weight = jnp.zeros((8, LANES), jnp.float32)
    for i in range(GF):
        weight = jnp.where(lax.div(k, 2) == i, (i + 1.0) / NF, weight)
    return weight


def swap_halves(v):
    k = lax.broadcasted_iota(jnp.int32, (8, LANES), 0)
    return jnp.where(lax.rem(k, 2) == 0, pltpu.roll(v, 7, 0), pltpu.roll(v, 1, 0))


def wide_row(par, index):
    return jnp.broadcast_to(par[index : index + 1, :], (8, LANES))


def pack_kernel(wind, current, sea, out, wind_here, current_here, sea_here, sems):
    rows, strip = wind.shape[1], wind.shape[2]
    copies = [
        pltpu.make_async_copy(wind, wind_here, sems.at[0]),
        pltpu.make_async_copy(current, current_here, sems.at[1]),
        pltpu.make_async_copy(sea, sea_here, sems.at[2]),
    ]
    for copy in copies:
        copy.start()
    empty = jnp.zeros((8, LANES - strip), jnp.float32)
    for copy in copies:
        copy.wait()
    packed = jnp.zeros((8, LANES), jnp.float32)
    piece = 0
    for ref in (current_here, wind_here):
        for axis in range(2):
            for row in range(0, rows, 8):
                wide = jnp.concatenate([ref[axis, row : row + 8, :], empty], axis=1)
                packed = packed + (pltpu.roll(wide, piece * strip, 1) if piece else wide)
                piece += 1
    out[0:8, :] = packed
    out[8:10, :] = sea_here[...].astype(jnp.float32)
    out[10:16, :] = jnp.zeros((6, LANES), jnp.float32)


def split_kernel(source, own, relayed, direct, sems):
    del own
    first = relayed.shape[0]
    parts = [
        pltpu.make_async_copy(source.at[0:first], relayed, sems.at[0]),
        pltpu.make_async_copy(source.at[first:ROWS], direct, sems.at[1]),
    ]
    for part in parts:
        part.start()
    for part in parts:
        part.wait()


def ends_kernel(spectra, sea, west, east, line):
    seas = sea[...].astype(jnp.float32)
    sub = lax.broadcasted_iota(jnp.int32, (LANES, LANES), 0)
    both = jnp.where(
        lax.rem(sub, 2) == 0,
        jnp.broadcast_to(seas[0:1], (LANES, LANES)),
        jnp.broadcast_to(seas[1:2], (LANES, LANES)),
    )
    full = ROWS // LANES
    for block in range(WIDE // LANES):
        at = block * LANES
        if block < full:
            cells = spectra[at : at + LANES, :] * both
        else:
            left = ROWS - at
            line[...] = jnp.zeros((LANES, LANES), jnp.float32)
            line[0:left, :] = spectra[at : at + left, :] * both[0:left]
            cells = line[...]
        turned = cells.T
        west[:, at : at + LANES] = turned[0:2]
        east[:, at : at + LANES] = turned[LANES - 2 : LANES]


def table_kernel(bands, order, geometry, slots, west_in, east_in, par, first, second, line):
    me = lax.axis_index("band")
    is_even = lax.rem(me, 2) == 0
    rows = 2 * bands
    strip = LANES // bands
    block = lax.div(lax.broadcasted_iota(jnp.int32, (8, LANES), 1), strip)
    sources = [jnp.bitwise_xor(me, r) for r in order]
    moved = [
        pltpu.roll(slots[16 * k : 16 * k + 8, :], source * strip, 1)
        for k, source in enumerate(sources)
    ]
    for piece in range(rows // 2):
        row = jnp.zeros((8, LANES), jnp.float32)
        for source, values in zip(sources, moved):
            row = jnp.where(block == lax.rem(source + piece, bands), values, row)
        line[8 * piece : 8 * piece + 8, :] = (
            pltpu.roll(row, LANES - piece * strip, 1) if piece else row
        )

    def mask_of(band):
        found = jnp.zeros((2, LANES), jnp.float32)
        for k, source in enumerate(sources):
            found = jnp.where(source == band, slots[16 * k + 8 : 16 * k + 10, :], found)
        return [found[0:1], found[1:2]]

    seas = mask_of(me - 1) + mask_of(me) + mask_of(me + 1)
    row = 2 * me
    has_south = jnp.where(me > 0, 1.0, 0.0)
    has_north = jnp.where(me < bands - 1, 1.0, 0.0)

    def around(part):
        first = part * rows
        south = line[pl.ds(first + jnp.maximum(row - 1, 0), 1), :] * has_south
        north = line[pl.ds(first + jnp.minimum(row + 2, rows - 1), 1), :] * has_north
        return [south] + [line[pl.ds(first + row + i, 1), :] for i in range(2)] + [north]

    def pick(low, high):
        return jnp.where(is_even, low, high)

    def put(index, value):
        par[index : index + 1, :] = jnp.broadcast_to(value, (1, LANES))

    tau = jnp.where(is_even, 1.0, -1.0)
    north = around(1)
    face = [0.5 * (north[i] + north[i + 1]) for i in range(3)]
    put(CUR_A, tau * pick(face[0], face[2]))
    put(CUR_M, tau * face[1])
    put(CUR_B, tau * pick(face[2], face[0]))
    lane = lax.broadcasted_iota(jnp.int32, (1, LANES), 1)
    inside = jnp.where(lane == 0, 0.0, 1.0)
    east_speed = around(0)[1:3]
    wind_0, wind_1 = around(2)[1:3], around(3)[1:3]
    shifted = [0.5 * inside * (v + pltpu.roll(v, 1, 1)) for v in east_speed]
    put(CX_A, pick(shifted[0], shifted[1]))
    put(CX_B, pick(shifted[1], shifted[0]))
    put(W0_A, pick(wind_0[0], wind_0[1]))
    put(W0_B, pick(wind_0[1], wind_0[0]))
    put(W1_A, pick(wind_1[0], wind_1[1]))
    put(W1_B, pick(wind_1[1], wind_1[0]))
    put(SEA_A, pick(seas[2], seas[3]))
    put(SEA_B, pick(seas[3], seas[2]))
    put(SEA_A1, pick(seas[1], seas[4]))
    put(SEA_A2, pick(seas[0], seas[5]))
    put(SEA_B1, pick(seas[4], seas[1]))
    put(SEA_B2, pick(seas[5], seas[0]))
    put(TAU, tau)
    icos = [geometry[me, 0], geometry[me, 1]]
    put(ICOS_A, inside * pick(icos[0], icos[1]))
    put(ICOS_B, inside * pick(icos[1], icos[0]))
    put(KAP_A, geometry[me, 2])
    put(MU_A, geometry[me, 3])
    put(MU_B, geometry[me, 4])
    put(KAP_B, geometry[me, 5])
    put(TAN_A, geometry[me, 6])
    put(TAN_B, geometry[me, 7])
    put(ICOS_0, icos[0])
    put(ICOS_1, icos[1])
    par[26:32, :] = jnp.zeros((6, LANES), jnp.float32)

    ends = []
    for values, columns in ((west_in[...], (0, 1)), (east_in[...], (LANES - 2, LANES - 1))):
        lane = lax.broadcasted_iota(jnp.int32, values.shape, 1)
        for i in range(2):
            pair = jnp.concatenate([east_speed[i][:, j : j + 1] for j in columns], axis=0)
            values = jnp.where(lane == ROWS + i, pair, values)
        ends.append(values)
    even_spec = lax.rem(lax.axis_index("spec"), 2) == 0
    first[...] = jnp.where(even_spec, ends[1], ends[0])
    second[...] = jnp.where(even_spec, ends[0], ends[1])


def fix_kernel(table, par, first_here, second_here, first_there, second_there, fix, tall):
    even_spec = lax.rem(lax.axis_index("spec"), 2) == 0
    west = jnp.where(even_spec, second_here[...], first_here[...])
    east = jnp.where(even_spec, first_here[...], second_here[...])
    from_west = jnp.where(even_spec, second_there[...], first_there[...])
    from_east = jnp.where(even_spec, first_there[...], second_there[...])
    lane = lax.broadcasted_iota(jnp.int32, (1, WIDE), 1)
    even_row = lax.rem(lane, 2) == 0
    speed = table[0:1] * par[ICOS_0 : ICOS_0 + 1, 0:1] + table[1:2] * par[ICOS_1 : ICOS_1 + 1, 0:1]

    def column(ref, row):
        cells = ref[row : row + 1, :]
        drift = jnp.where(even_row, cells[:, ROWS : ROWS + 1], cells[:, ROWS + 1 : ROWS + 2])
        return cells, drift

    xm2, _ = column(from_west, 0)
    xm1, dm1 = column(from_west, 1)
    x0, d0 = column(west, 0)
    x1, d1 = column(west, 1)
    y2, d2 = column(east, 0)
    y1, dy1 = column(east, 1)
    z0, dz0 = column(from_east, 0)
    z1, _ = column(from_east, 1)
    first = flux(xm2, xm1, x0, x1, speed + 0.5 * (dm1 + d0))
    last = flux(y2, y1, z0, z1, speed + 0.5 * (dy1 + dz0))
    c = speed + 0.5 * (d0 + d1)
    second = jnp.where(c >= 0.0, -c * (1.0 - c * c) * (1.0 / 6.0), 0.0) * (xm1 - y1)
    c = speed + 0.5 * (d2 + dy1)
    before = jnp.where(c >= 0.0, 0.0, -c * (1.0 - c * c) * (1.0 / 6.0)) * (z0 - x0)
    tall[...] = jnp.zeros((LANES, WIDE), jnp.float32)
    tall[0:1, :] = first - second
    tall[1:2, :] = second
    tall[LANES - 2 : LANES - 1, :] = -before
    tall[LANES - 1 : LANES, :] = before - last
    for block in range(WIDE // LANES):
        at = block * LANES
        fix[at : at + LANES, :] = tall[:, at : at + LANES].T


def base_kernel(par, spectra, beyond_first, beyond_last, base_first, base_last, gain_first, gain_last):
    odd = lax.rem(lax.axis_index("band"), 2)
    sea_a, sea_b = wide_row(par, SEA_A), wide_row(par, SEA_B)
    sea_b1, sea_b2 = wide_row(par, SEA_B1), wide_row(par, SEA_B2)
    sea_a1 = wide_row(par, SEA_A1)
    into_a1 = wide_row(par, KAP_A) * sea_a1
    into_a2 = wide_row(par, KAP_A) * wide_row(par, SEA_A2)
    over_a, over_b = wide_row(par, MU_A) * sea_a1, wide_row(par, MU_B) * sea_a1
    cur_a, cur_m, cur_b = wide_row(par, CUR_A), wide_row(par, CUR_M), wide_row(par, CUR_B)
    cx_a, cx_b = wide_row(par, CX_A), wide_row(par, CX_B)
    kap_a, mu_a = wide_row(par, KAP_A), wide_row(par, MU_A)
    mu_b, kap_b = wide_row(par, MU_B), wide_row(par, KAP_B)
    tau = wide_row(par, TAU)
    icos_a, icos_b = wide_row(par, ICOS_A), wide_row(par, ICOS_B)

    def along_east(x, speed_x, current_x, cosine):
        crossing = flux(
            pltpu.roll(x, 2, 1),
            pltpu.roll(x, 1, 1),
            x,
            pltpu.roll(x, LANES - 1, 1),
            speed_x * cosine + current_x,
        )
        return crossing - pltpu.roll(crossing, LANES - 1, 1)

    def one_group(base, gain, beyond, first, g, speeds):
        start = (first + g) * GROUP_ROWS
        far = g * GROUP_ROWS
        north = speeds * tau
        east_a, east_b = speeds * icos_a, speeds * icos_b
        for d in range(HALF):
            row_a = pl.ds(start + 2 * d + odd, 8, stride=ND)
            row_b = pl.ds(start + 2 * d + 1 - odd, 8, stride=ND)
            a = spectra[row_a, :] * sea_a
            b = spectra[row_b, :] * sea_b
            b1 = beyond[pl.ds(far + 2 * d + odd, 8, stride=ND), :] * sea_b1
            b2 = beyond[pl.ds(far + 2 * d + 1 - odd, 8, stride=ND), :] * sea_b2
            c = north * SIN[d] + cur_a
            w = (1.0 / 6.0) - (c * c) * (1.0 / 6.0)
            inward = c >= 0.0
            cw = c * w
            half = 0.5 * c
            flux_a = (half - half * c) * a - cw * jnp.where(inward, a, b - 2.0 * a)
            cm = north * SIN[d] + cur_m
            flux_m = flux(0.0, a, b, b1, cm)
            away = jnp.where(cm >= 0.0, cm * ((cm * cm) * (1.0 / 6.0) - (1.0 / 6.0)), 0.0)
            flux_b = flux(a, b, b1, b2, north * SIN[d] + cur_b)
            to_a = along_east(a, east_a, cx_a, COS[d])
            to_b = along_east(b, east_b, cx_b, COS[d])
            at = pl.multiple_of(g * (HALF * 16) + d * 16, 8)
            base[pl.ds(at, 8), :] = a + to_a + kap_a * flux_a - mu_a * flux_m
            base[pl.ds(at + 8, 8), :] = b + to_b + mu_b * flux_m - kap_b * flux_b
            at = pl.multiple_of(g * (HALF * 24) + d * 24, 8)
            near = half + half * c + jnp.where(inward, 2.0 * cw, -cw)
            gain[pl.ds(at, 8), :] = into_a1 * near - over_a * away
            gain[pl.ds(at + 8, 8), :] = into_a2 * jnp.where(inward, -cw, 0.0)
            gain[pl.ds(at + 16, 8), :] = over_b * away
        return speeds * FREQ_STEP**-GF

    speeds = lax.fori_loop(
        0, FIRST_GROUPS, functools.partial(one_group, base_first, gain_first, beyond_first, 0), group_speed()
    )
    lax.fori_loop(
        0,
        GROUPS - FIRST_GROUPS,
        functools.partial(one_group, base_last, gain_last, beyond_last, FIRST_GROUPS),
        speeds,
    )


def turn(cells, rate):
    k = lax.broadcasted_iota(jnp.int32, (8, LANES), 0)
    first = lax.rem(k, 2) == 0
    cube = rate * rate * rate
    ring = [swap_halves(cells[HALF - 1])] + cells
    ring = ring + [swap_halves(cells[0]), swap_halves(cells[1])]
    steps = [high - low for low, high in zip(ring, ring[1:])]
    bends = [high - low for low, high in zip(steps, steps[1:])]
    fluxes = []
    for d in range(HALF):
        mean = 0.5 * (COS[d] + COS[d + 1])
        low, high = (bends[d + 1], bends[d]) if mean > 0 else (bends[d], bends[d + 1])
        bend = jnp.where(first, low, high)
        both = ring[d + 1] + ring[d + 2]
        weight = rate * (mean / 6.0) - cube * (mean**3 / 6.0)
        fluxes.append(
            (rate * (0.5 * mean)) * (both - (rate * mean) * steps[d + 1]) - weight * bend
        )
    last = swap_halves(fluxes[HALF - 1])
    return [cells[d] - (fluxes[d] - (fluxes[d - 1] if d else last)) for d in range(HALF)]


def finish_groups(first, count, skip, par, base, gain, fix, ahead, turned, total):
    odd = lax.rem(lax.axis_index("band"), 2)
    tan_a, tan_b = wide_row(par, TAN_A), wide_row(par, TAN_B)

    def one_group(g, carry):
        speeds, weight, sum_a, sum_b = carry
        start = (skip + g) * GROUP_ROWS
        fix_start = (first + g) * GROUP_ROWS
        cells_a, cells_b = [], []
        for d in range(HALF):
            n1 = ahead[pl.ds(start + 2 * d + 1 - odd, 8, stride=ND), :]
            n2 = ahead[pl.ds(start + 2 * d + odd, 8, stride=ND), :]
            fix_a = fix[pl.ds(fix_start + 2 * d + odd, 8, stride=ND), :]
            fix_b = fix[pl.ds(fix_start + 2 * d + 1 - odd, 8, stride=ND), :]
            at = pl.multiple_of(g * (HALF * 16) + d * 16, 8)
            by = pl.multiple_of(g * (HALF * 24) + d * 24, 8)
            cells_a.append(
                base[pl.ds(at, 8), :]
                + fix_a
                + gain[pl.ds(by, 8), :] * n1
                + gain[pl.ds(by + 8, 8), :] * n2
            )
            cells_b.append(base[pl.ds(at + 8, 8), :] + fix_b + gain[pl.ds(by + 16, 8), :] * n1)
        square_a = square_b = 0.0
        for d, v in enumerate(turn(cells_a, speeds * tan_a)):
            at = pl.multiple_of(g * (HALF * 16) + d * 16, 8)
            turned[pl.ds(at, 8), :] = v
            square_a = square_a + v * v
        for d, v in enumerate(turn(cells_b, speeds * tan_b)):
            at = pl.multiple_of(g * (HALF * 16) + d * 16 + 8, 8)
            turned[pl.ds(at, 8), :] = v
            square_b = square_b + v * v
        return (
            speeds * FREQ_STEP**-GF,
            weight + GF / NF,
            sum_a + weight * square_a,
            sum_b + weight * square_b,
        )

    speeds = group_speed() * FREQ_STEP ** -(GF * first)
    weight = freq_weight() + GF * first / NF
    carry = (speeds, weight, total[0:8, :], total[8:16, :])
    _, _, total[0:8, :], total[8:16, :] = lax.fori_loop(0, count, one_group, carry)


def finish_either(bands, first, count, par, base, gain, fix, straight, split, turned, total):
    me = lax.axis_index("band")
    middle = jnp.logical_or(me == bands // 2 - 1, me == bands // 2)

    @pl.when(middle)
    def _():
        finish_groups(first, count, 0, par, base, gain, fix, split, turned, total)

    @pl.when(jnp.logical_not(middle))
    def _():
        finish_groups(first, count, first, par, base, gain, fix, straight, turned, total)


def first_kernel(bands, par, base, gain, fix, straight, split, turned, total):
    total[...] = jnp.zeros((16, LANES), jnp.float32)
    finish_either(bands, 0, FIRST_GROUPS, par, base, gain, fix, straight, split, turned, total)


def last_kernel(
    bands, par, base, gain, fix, straight, split, done, before, result, turned, total, out, sems
):
    odd = lax.rem(lax.axis_index("band"), 2)
    later = GROUPS - FIRST_GROUPS
    total[...] = before[...]
    finish_either(bands, FIRST_GROUPS, later, par, base, gain, fix, straight, split, turned, total)
    scale = 2.0 / (NF * ND)
    steep_a = jnp.sum(total[0:8, :], axis=0, keepdims=True) * scale
    steep_b = jnp.sum(total[8:16, :], axis=0, keepdims=True) * scale
    sea_a, sea_b = wide_row(par, SEA_A), wide_row(par, SEA_B)
    w0_a, w0_b = wide_row(par, W0_A), wide_row(par, W0_B)
    w1_a, w1_b = wide_row(par, W1_A), wide_row(par, W1_B)

    def copy_out(g):
        rows = pl.ds(pl.multiple_of(g * GROUP_ROWS, 8), GROUP_ROWS)
        return pltpu.make_async_copy(out.at[rows], result.at[rows], sems.at[g])

    def one_group(first, ref, g, carry):
        coupling, weight = carry
        start = (first + g) * GROUP_ROWS
        gain_a = sea_a / (1.0 + weight * steep_a)
        gain_b = sea_b / (1.0 + weight * steep_b)
        wa0, wa1 = w0_a * coupling, w1_a * coupling
        wb0, wb1 = w0_b * coupling, w1_b * coupling
        for d in range(HALF):
            at = pl.multiple_of(g * (HALF * 16) + d * 16, 8)
            growth_a = jnp.maximum(wa0 * COS[d] + wa1 * SIN[d] + (1.0 - GROWTH), 1.0)
            growth_b = jnp.maximum(wb0 * COS[d] + wb1 * SIN[d] + (1.0 - GROWTH), 1.0)
            out[pl.ds(start + 2 * d + odd, 8, stride=ND), :] = (
                ref[pl.ds(at, 8), :] * gain_a * growth_a
            )
            out[pl.ds(start + 2 * d + 1 - odd, 8, stride=ND), :] = (
                ref[pl.ds(at + 8, 8), :] * gain_b * growth_b
            )
        copy_out(first + g).start()
        return coupling * FREQ_STEP**GF, weight + GF / NF

    k = lax.broadcasted_iota(jnp.int32, (8, LANES), 0)
    coupling = jnp.zeros((8, LANES), jnp.float32)
    for i in range(GF):
        for h in range(2):
            value = GROWTH * WIND_COUPLING * FREQ_STEP**i * (1.0 - 2.0 * h)
            coupling = jnp.where(k == 2 * i + h, value, coupling)
    carry = (coupling, freq_weight())
    carry = lax.fori_loop(0, FIRST_GROUPS, functools.partial(one_group, 0, done), carry)
    lax.fori_loop(0, later, functools.partial(one_group, FIRST_GROUPS, turned), carry)
    for g in range(GROUPS):
        copy_out(g).wait()


def geometry_table(bands):
    total = 2 * bands

    def angle(position):
        return (LAT_SOUTH + (LAT_NORTH - LAT_SOUTH) * position / total) * (math.pi / 180.0)

    table = np.zeros((bands, 8), np.float32)
    for b in range(bands):
        cells = [angle(2 * b + 0.5), angle(2 * b + 1.5)]
        faces = [angle(2 * b), angle(2 * b + 1), angle(2 * b + 2)]
        icos = [1.0 / math.cos(v) for v in cells]
        near, far = (0, 1) if b % 2 == 0 else (1, 0)
        face_a, face_b = (faces[0], faces[2]) if b % 2 == 0 else (faces[2], faces[0])
        table[b] = [
            icos[0],
            icos[1],
            math.cos(face_a) * icos[near],
            math.cos(faces[1]) * icos[near],
            math.cos(faces[1]) * icos[far],
            math.cos(face_b) * icos[far],
            -TURNING * math.tan(cells[near]),
            -TURNING * math.tan(cells[far]),
        ]
    return table


def speed_table():
    table = np.zeros((2, WIDE), np.float32)
    for k in range(NF * ND):
        value = SPEED_TOP * FREQ_STEP ** -(k // ND) * math.cos(2.0 * math.pi * (k % ND) / ND)
        table[0, 2 * k] = value
        table[1, 2 * k + 1] = value
    return table


VMEM = pl.BlockSpec(memory_space=pltpu.VMEM)
SMEM = pl.BlockSpec(memory_space=pltpu.SMEM)
HBM = pl.BlockSpec(memory_space=pltpu.HBM)
ANY = pl.BlockSpec(memory_space=pl.ANY)
PARAMS = pltpu.CompilerParams(vmem_limit_bytes=40 * 1024 * 1024)


def call(kernel, name, operands, specs, shapes, scratch, micros, outs_in=None, flops=0):
    outs = [jax.ShapeDtypeStruct(s, jnp.float32) for s in shapes]
    return pl.pallas_call(
        kernel,
        name=name,
        out_shape=outs,
        in_specs=specs,
        out_specs=[outs_in or VMEM] * len(outs),
        scratch_shapes=scratch,
        compiler_params=PARAMS,
        cost_estimate=pl.CostEstimate(
            flops=flops, bytes_accessed=int(micros * 3.0e6), transcendentals=0
        ),
    )(*operands)


def swapped(pairs):
    return pairs + [(t, s) for s, t in pairs]


def per_device(bands, spec_count, spectra, sea_mask, wind, current):
    comp_count, row_count, col_count = spectra.shape
    cells = spectra.reshape(comp_count * row_count, col_count)
    middle = bands // 2 - 1
    first_rows = FIRST_GROUPS * GROUP_ROWS
    last_rows = ROWS - first_rows

    (own,) = call(
        pack_kernel,
        "pack_forcing",
        tuple(pltpu.with_memory_space_constraint(v, pltpu.HBM) for v in (wind, current, sea_mask)),
        [HBM] * 3,
        [(16, LANES)],
        [
            pltpu.VMEM(wind.shape, jnp.float32),
            pltpu.VMEM(current.shape, jnp.float32),
            pltpu.VMEM(sea_mask.shape, jnp.int32),
            pltpu.SemaphoreType.DMA((3,)),
        ],
        0.3,
    )
    order = [0]

    def gathered(values, bit):
        order.extend([r ^ bit for r in order])
        other = lax.ppermute(values, "band", [(b, b ^ bit) for b in range(bands)])
        return jnp.concatenate([values, other], axis=0)

    forcing = gathered(own, 2)

    part_relayed, part_direct = call(
        split_kernel,
        "split",
        (pltpu.with_memory_space_constraint(cells, pltpu.HBM), own),
        [HBM, VMEM],
        [(first_rows, LANES), (last_rows, LANES)],
        [pltpu.SemaphoreType.DMA((2,))],
        1.0,
    )
    part_relayed, forcing, ends_sea = lax.optimization_barrier((part_relayed, forcing, sea_mask))
    straight = lax.ppermute(
        cells, "band", swapped([(b, b + 1) for b in range(1, bands - 1, 2) if b != middle])
    )
    west, east = call(
        ends_kernel,
        "ends",
        (cells, ends_sea),
        [VMEM] * 2,
        [(2, WIDE), (2, WIDE)],
        [pltpu.VMEM((LANES, LANES), jnp.float32)],
        1.0,
    )
    part_relayed, west, east = lax.optimization_barrier((part_relayed, west, east))
    relay = lax.ppermute(part_relayed, "band", [(middle, bands - 1), (middle + 1, 0)])
    bit = 4
    while bit < bands:
        forcing = gathered(forcing, bit)
        bit *= 2
    part_relayed, part_direct, forcing, west, east = lax.optimization_barrier(
        (part_relayed, part_direct, forcing, west, east)
    )
    pairs = [(b, b + 1) for b in range(0, bands, 2)]
    forcing = gathered(forcing, 1)
    beyond = [lax.ppermute(part, "band", swapped(pairs)) for part in (part_relayed, part_direct)]
    part_direct, forcing = lax.optimization_barrier((part_direct, forcing))
    direct = lax.ppermute(
        part_direct, "band", [(middle, middle + 1), (middle + 1, middle)]
    )

    par, first_here, second_here = call(
        functools.partial(table_kernel, bands, tuple(order)),
        "tables",
        (jnp.asarray(geometry_table(bands)), forcing, west, east),
        [SMEM, VMEM, VMEM, VMEM],
        [(PAR_ROWS, LANES), (2, WIDE), (2, WIDE)],
        [pltpu.VMEM((8 * bands, LANES), jnp.float32)],
        0.3,
        flops=4300000000,
    )
    relay, par = lax.optimization_barrier((relay, par))
    relayed = lax.ppermute(relay, "band", [(bands - 1, middle + 1), (0, middle)])
    ring = [(s, (s + 1) % spec_count) for s in range(spec_count)]
    first_there = lax.ppermute(first_here, "spec", swapped(ring[0::2]))
    second_there = lax.ppermute(second_here, "spec", swapped(ring[1::2]))
    base_first, base_last, gain_first, gain_last = call(
        base_kernel,
        "base",
        (par, cells, *beyond),
        [VMEM] * 4,
        [
            (first_rows, LANES),
            (last_rows, LANES),
            (first_rows * 3 // 2, LANES),
            (last_rows * 3 // 2, LANES),
        ],
        [],
        4.0,
    )
    base_first, first_there, second_there = lax.optimization_barrier(
        (base_first, first_there, second_there)
    )
    (fix,) = call(
        fix_kernel,
        "fix",
        (jnp.asarray(speed_table()), par, first_here, second_here, first_there, second_there),
        [VMEM] * 6,
        [(WIDE, LANES)],
        [pltpu.VMEM((LANES, WIDE), jnp.float32)],
        1.0,
    )
    turned, total = call(
        functools.partial(first_kernel, bands),
        "first_groups",
        (par, base_first, gain_first, fix, straight, relayed),
        [VMEM] * 6,
        [(first_rows, LANES), (16, LANES)],
        [],
        1.0,
    )
    (out,) = call(
        functools.partial(last_kernel, bands),
        "last_groups",
        (par, base_last, gain_last, fix, straight, direct, turned, total),
        [VMEM] * 8,
        [(ROWS, LANES)],
        [
            pltpu.VMEM((last_rows, LANES), jnp.float32),
            pltpu.VMEM((16, LANES), jnp.float32),
            pltpu.VMEM((ROWS, LANES), jnp.float32),
            pltpu.SemaphoreType.DMA((GROUPS,)),
        ],
        2.0,
        outs_in=ANY,
    )
    return out.reshape(comp_count, row_count, col_count)


def solution(mesh):
    placed = (
        P(None, "band", "spec"),
        P("band", "spec"),
        P(None, None, ("spec", "band")),
        P(None, None, ("spec", "band")),
    )
    return jax.shard_map(
        functools.partial(per_device, mesh.shape["band"], mesh.shape["spec"]),
        mesh=mesh,
        in_specs=placed,
        out_specs=P(None, "band", "spec"),
        check_vma=False,
    )
```

```python
import functools
import math

import jax
import jax.numpy as jnp
import numpy as np
from jax import lax
from jax.experimental import pallas as pl
from jax.experimental.pallas import tpu as pltpu
from jax.sharding import PartitionSpec as P

NF = 36
ND = 36
HALF = ND // 2
LAT_SOUTH = 30.0
LAT_NORTH = 55.0
SPEED_TOP = 0.35
FREQ_STEP = 1.1
TURNING = 1.5
GROWTH = 0.05
WIND_COUPLING = 0.04

GF = 4
GROUPS = NF // GF
GROUP_ROWS = GF * ND * 2
FIRST_GROUPS = 4
LANES = 128
ROWS = NF * ND * 2
WIDE = -(-(ROWS + 2) // LANES) * LANES

COS = [math.cos(2.0 * math.pi * d / ND) for d in range(HALF + 1)]
SIN = [math.sin(2.0 * math.pi * d / ND) for d in range(HALF + 1)]

(
    CUR_A,
    CUR_M,
    CUR_B,
    CX_A,
    CX_B,
    W0_A,
    W0_B,
    W1_A,
    W1_B,
    SEA_A,
    SEA_B,
    SEA_A1,
    SEA_A2,
    SEA_B1,
    SEA_B2,
    TAU,
    ICOS_A,
    ICOS_B,
    KAP_A,
    MU_A,
    MU_B,
    KAP_B,
    TAN_A,
    TAN_B,
    ICOS_0,
    ICOS_1,
) = range(26)
PAR_ROWS = 32


def flux(lo2, lo1, hi1, hi2, c):
    forward = c >= 0.0
    source = jnp.where(forward, lo1, hi1)
    upwind = jnp.where(forward, lo2, hi2)
    both = lo1 + hi1
    bend = both - 3.0 * source + upwind
    w = (1.0 / 6.0) - (c * c) * (1.0 / 6.0)
    return c * (0.5 * (both - c * (hi1 - lo1)) - w * bend)


def group_speed():
    k = lax.broadcasted_iota(jnp.int32, (8, LANES), 0)
    speed = jnp.zeros((8, LANES), jnp.float32)
    for i in range(GF):
        for h in range(2):
            value = SPEED_TOP * FREQ_STEP**-i * (1.0 - 2.0 * h)
            speed = jnp.where(k == 2 * i + h, value, speed)
    return speed


def freq_weight():
    k = lax.broadcasted_iota(jnp.int32, (8, LANES), 0)
    weight = jnp.zeros((8, LANES), jnp.float32)
    for i in range(GF):
        weight = jnp.where(lax.div(k, 2) == i, (i + 1.0) / NF, weight)
    return weight


def swap_halves(v):
    k = lax.broadcasted_iota(jnp.int32, (8, LANES), 0)
    return jnp.where(lax.rem(k, 2) == 0, pltpu.roll(v, 7, 0), pltpu.roll(v, 1, 0))


def wide_row(par, index):
    return jnp.broadcast_to(par[index : index + 1, :], (8, LANES))


def pack_kernel(wind, current, sea, out, wind_here, current_here, sea_here, sems):
    rows, strip = wind.shape[1], wind.shape[2]
    copies = [
        pltpu.make_async_copy(wind, wind_here, sems.at[0]),
        pltpu.make_async_copy(current, current_here, sems.at[1]),
        pltpu.make_async_copy(sea, sea_here, sems.at[2]),
    ]
    for copy in copies:
        copy.start()
    empty = jnp.zeros((8, LANES - strip), jnp.float32)
    for copy in copies:
        copy.wait()
    packed = jnp.zeros((8, LANES), jnp.float32)
    piece = 0
    for ref in (current_here, wind_here):
        for axis in range(2):
            for row in range(0, rows, 8):
                wide = jnp.concatenate([ref[axis, row : row + 8, :], empty], axis=1)
                packed = packed + (pltpu.roll(wide, piece * strip, 1) if piece else wide)
                piece += 1
    out[0:8, :] = packed
    out[8:10, :] = sea_here[...].astype(jnp.float32)
    out[10:16, :] = jnp.zeros((6, LANES), jnp.float32)


def split_kernel(source, own, relayed, direct, sems):
    del own
    first = relayed.shape[0]
    parts = [
        pltpu.make_async_copy(source.at[0:first], relayed, sems.at[0]),
        pltpu.make_async_copy(source.at[first:ROWS], direct, sems.at[1]),
    ]
    for part in parts:
        part.start()
    for part in parts:
        part.wait()


def ends_kernel(spectra, sea, west, east, line):
    seas = sea[...].astype(jnp.float32)
    sub = lax.broadcasted_iota(jnp.int32, (LANES, LANES), 0)
    both = jnp.where(
        lax.rem(sub, 2) == 0,
        jnp.broadcast_to(seas[0:1], (LANES, LANES)),
        jnp.broadcast_to(seas[1:2], (LANES, LANES)),
    )
    full = ROWS // LANES
    for block in range(WIDE // LANES):
        at = block * LANES
        if block < full:
            cells = spectra[at : at + LANES, :] * both
        else:
            left = ROWS - at
            line[...] = jnp.zeros((LANES, LANES), jnp.float32)
            line[0:left, :] = spectra[at : at + left, :] * both[0:left]
            cells = line[...]
        turned = cells.T
        west[:, at : at + LANES] = turned[0:2]
        east[:, at : at + LANES] = turned[LANES - 2 : LANES]


def table_kernel(bands, order, geometry, slots, west_in, east_in, par, first, second, line):
    me = lax.axis_index("band")
    is_even = lax.rem(me, 2) == 0
    rows = 2 * bands
    strip = LANES // bands
    block = lax.div(lax.broadcasted_iota(jnp.int32, (8, LANES), 1), strip)
    sources = [jnp.bitwise_xor(me, r) for r in order]
    moved = [
        pltpu.roll(slots[16 * k : 16 * k + 8, :], source * strip, 1)
        for k, source in enumerate(sources)
    ]
    for piece in range(rows // 2):
        row = jnp.zeros((8, LANES), jnp.float32)
        for source, values in zip(sources, moved):
            row = jnp.where(block == lax.rem(source + piece, bands), values, row)
        line[8 * piece : 8 * piece + 8, :] = (
            pltpu.roll(row, LANES - piece * strip, 1) if piece else row
        )

    def mask_of(band):
        found = jnp.zeros((2, LANES), jnp.float32)
        for k, source in enumerate(sources):
            found = jnp.where(source == band, slots[16 * k + 8 : 16 * k + 10, :], found)
        return [found[0:1], found[1:2]]

    seas = mask_of(me - 1) + mask_of(me) + mask_of(me + 1)
    row = 2 * me
    has_south = jnp.where(me > 0, 1.0, 0.0)
    has_north = jnp.where(me < bands - 1, 1.0, 0.0)

    def around(part):
        first = part * rows
        south = line[pl.ds(first + jnp.maximum(row - 1, 0), 1), :] * has_south
        north = line[pl.ds(first + jnp.minimum(row + 2, rows - 1), 1), :] * has_north
        return [south] + [line[pl.ds(first + row + i, 1), :] for i in range(2)] + [north]

    def pick(low, high):
        return jnp.where(is_even, low, high)

    def put(index, value):
        par[index : index + 1, :] = jnp.broadcast_to(value, (1, LANES))

    tau = jnp.where(is_even, 1.0, -1.0)
    north = around(1)
    face = [0.5 * (north[i] + north[i + 1]) for i in range(3)]
    put(CUR_A, tau * pick(face[0], face[2]))
    put(CUR_M, tau * face[1])
    put(CUR_B, tau * pick(face[2], face[0]))
    lane = lax.broadcasted_iota(jnp.int32, (1, LANES), 1)
    inside = jnp.where(lane == 0, 0.0, 1.0)
    east_speed = around(0)[1:3]
    wind_0, wind_1 = around(2)[1:3], around(3)[1:3]
    shifted = [0.5 * inside * (v + pltpu.roll(v, 1, 1)) for v in east_speed]
    put(CX_A, pick(shifted[0], shifted[1]))
    put(CX_B, pick(shifted[1], shifted[0]))
    put(W0_A, pick(wind_0[0], wind_0[1]))
    put(W0_B, pick(wind_0[1], wind_0[0]))
    put(W1_A, pick(wind_1[0], wind_1[1]))
    put(W1_B, pick(wind_1[1], wind_1[0]))
    put(SEA_A, pick(seas[2], seas[3]))
    put(SEA_B, pick(seas[3], seas[2]))
    put(SEA_A1, pick(seas[1], seas[4]))
    put(SEA_A2, pick(seas[0], seas[5]))
    put(SEA_B1, pick(seas[4], seas[1]))
    put(SEA_B2, pick(seas[5], seas[0]))
    put(TAU, tau)
    icos = [geometry[me, 0], geometry[me, 1]]
    put(ICOS_A, inside * pick(icos[0], icos[1]))
    put(ICOS_B, inside * pick(icos[1], icos[0]))
    put(KAP_A, geometry[me, 2])
    put(MU_A, geometry[me, 3])
    put(MU_B, geometry[me, 4])
    put(KAP_B, geometry[me, 5])
    put(TAN_A, geometry[me, 6])
    put(TAN_B, geometry[me, 7])
    put(ICOS_0, icos[0])
    put(ICOS_1, icos[1])
    par[26:32, :] = jnp.zeros((6, LANES), jnp.float32)

    ends = []
    for values, columns in ((west_in[...], (0, 1)), (east_in[...], (LANES - 2, LANES - 1))):
        lane = lax.broadcasted_iota(jnp.int32, values.shape, 1)
        for i in range(2):
            pair = jnp.concatenate([east_speed[i][:, j : j + 1] for j in columns], axis=0)
            values = jnp.where(lane == ROWS + i, pair, values)
        ends.append(values)
    even_spec = lax.rem(lax.axis_index("spec"), 2) == 0
    first[...] = jnp.where(even_spec, ends[0], ends[1])
    second[...] = jnp.where(even_spec, ends[1], ends[0])


def fix_kernel(table, par, first_here, second_here, first_there, second_there, fix, tall):
    even_spec = lax.rem(lax.axis_index("spec"), 2) == 0
    west = jnp.where(even_spec, first_here[...], second_here[...])
    east = jnp.where(even_spec, second_here[...], first_here[...])
    from_west = jnp.where(even_spec, first_there[...], second_there[...])
    from_east = jnp.where(even_spec, second_there[...], first_there[...])
    lane = lax.broadcasted_iota(jnp.int32, (1, WIDE), 1)
    even_row = lax.rem(lane, 2) == 0
    speed = table[0:1] * par[ICOS_0 : ICOS_0 + 1, 0:1] + table[1:2] * par[ICOS_1 : ICOS_1 + 1, 0:1]

    def column(ref, row):
        cells = ref[row : row + 1, :]
        drift = jnp.where(even_row, cells[:, ROWS : ROWS + 1], cells[:, ROWS + 1 : ROWS + 2])
        return cells, drift

    xm2, _ = column(from_west, 0)
    xm1, dm1 = column(from_west, 1)
    x0, d0 = column(west, 0)
    x1, d1 = column(west, 1)
    y2, d2 = column(east, 0)
    y1, dy1 = column(east, 1)
    z0, dz0 = column(from_east, 0)
    z1, _ = column(from_east, 1)
    first = flux(xm2, xm1, x0, x1, speed + 0.5 * (dm1 + d0))
    last = flux(y2, y1, z0, z1, speed + 0.5 * (dy1 + dz0))
    c = speed + 0.5 * (d0 + d1)
    second = jnp.where(c >= 0.0, -c * (1.0 - c * c) * (1.0 / 6.0), 0.0) * (xm1 - y1)
    c = speed + 0.5 * (d2 + dy1)
    before = jnp.where(c >= 0.0, 0.0, -c * (1.0 - c * c) * (1.0 / 6.0)) * (z0 - x0)
    tall[...] = jnp.zeros((LANES, WIDE), jnp.float32)
    tall[0:1, :] = first - second
    tall[1:2, :] = second
    tall[LANES - 2 : LANES - 1, :] = -before
    tall[LANES - 1 : LANES, :] = before - last
    for block in range(WIDE // LANES):
        at = block * LANES
        fix[at : at + LANES, :] = tall[:, at : at + LANES].T


def base_kernel(par, spectra, beyond_first, beyond_last, base_first, base_last, gain_first, gain_last):
    odd = lax.rem(lax.axis_index("band"), 2)
    sea_a, sea_b = wide_row(par, SEA_A), wide_row(par, SEA_B)
    sea_b1, sea_b2 = wide_row(par, SEA_B1), wide_row(par, SEA_B2)
    sea_a1 = wide_row(par, SEA_A1)
    into_a1 = wide_row(par, KAP_A) * sea_a1
    into_a2 = wide_row(par, KAP_A) * wide_row(par, SEA_A2)
    over_a, over_b = wide_row(par, MU_A) * sea_a1, wide_row(par, MU_B) * sea_a1
    cur_a, cur_m, cur_b = wide_row(par, CUR_A), wide_row(par, CUR_M), wide_row(par, CUR_B)
    cx_a, cx_b = wide_row(par, CX_A), wide_row(par, CX_B)
    kap_a, mu_a = wide_row(par, KAP_A), wide_row(par, MU_A)
    mu_b, kap_b = wide_row(par, MU_B), wide_row(par, KAP_B)
    tau = wide_row(par, TAU)
    icos_a, icos_b = wide_row(par, ICOS_A), wide_row(par, ICOS_B)

    def along_east(x, speed_x, current_x, cosine):
        crossing = flux(
            pltpu.roll(x, 2, 1),
            pltpu.roll(x, 1, 1),
            x,
            pltpu.roll(x, LANES - 1, 1),
            speed_x * cosine + current_x,
        )
        return crossing - pltpu.roll(crossing, LANES - 1, 1)

    def one_group(base, gain, beyond, first, g, speeds):
        start = (first + g) * GROUP_ROWS
        far = g * GROUP_ROWS
        north = speeds * tau
        east_a, east_b = speeds * icos_a, speeds * icos_b
        for d in range(HALF):
            row_a = pl.ds(start + 2 * d + odd, 8, stride=ND)
            row_b = pl.ds(start + 2 * d + 1 - odd, 8, stride=ND)
            a = spectra[row_a, :] * sea_a
            b = spectra[row_b, :] * sea_b
            b1 = beyond[pl.ds(far + 2 * d + odd, 8, stride=ND), :] * sea_b1
            b2 = beyond[pl.ds(far + 2 * d + 1 - odd, 8, stride=ND), :] * sea_b2
            c = north * SIN[d] + cur_a
            w = (1.0 / 6.0) - (c * c) * (1.0 / 6.0)
            inward = c >= 0.0
            cw = c * w
            half = 0.5 * c
            flux_a = (half - half * c) * a - cw * jnp.where(inward, a, b - 2.0 * a)
            cm = north * SIN[d] + cur_m
            flux_m = flux(0.0, a, b, b1, cm)
            away = jnp.where(cm >= 0.0, cm * ((cm * cm) * (1.0 / 6.0) - (1.0 / 6.0)), 0.0)
            flux_b = flux(a, b, b1, b2, north * SIN[d] + cur_b)
            to_a = along_east(a, east_a, cx_a, COS[d])
            to_b = along_east(b, east_b, cx_b, COS[d])
            at = pl.multiple_of(g * (HALF * 16) + d * 16, 8)
            base[pl.ds(at, 8), :] = a + to_a + kap_a * flux_a - mu_a * flux_m
            base[pl.ds(at + 8, 8), :] = b + to_b + mu_b * flux_m - kap_b * flux_b
            at = pl.multiple_of(g * (HALF * 24) + d * 24, 8)
            near = half + half * c + jnp.where(inward, 2.0 * cw, -cw)
            gain[pl.ds(at, 8), :] = into_a1 * near - over_a * away
            gain[pl.ds(at + 8, 8), :] = into_a2 * jnp.where(inward, -cw, 0.0)
            gain[pl.ds(at + 16, 8), :] = over_b * away
        return speeds * FREQ_STEP**-GF

    speeds = lax.fori_loop(
        0, FIRST_GROUPS, functools.partial(one_group, base_first, gain_first, beyond_first, 0), group_speed()
    )
    lax.fori_loop(
        0,
        GROUPS - FIRST_GROUPS,
        functools.partial(one_group, base_last, gain_last, beyond_last, FIRST_GROUPS),
        speeds,
    )


def turn(cells, rate):
    k = lax.broadcasted_iota(jnp.int32, (8, LANES), 0)
    first = lax.rem(k, 2) == 0
    cube = rate * rate * rate
    ring = [swap_halves(cells[HALF - 1])] + cells
    ring = ring + [swap_halves(cells[0]), swap_halves(cells[1])]
    steps = [high - low for low, high in zip(ring, ring[1:])]
    bends = [high - low for low, high in zip(steps, steps[1:])]
    fluxes = []
    for d in range(HALF):
        mean = 0.5 * (COS[d] + COS[d + 1])
        low, high = (bends[d + 1], bends[d]) if mean > 0 else (bends[d], bends[d + 1])
        bend = jnp.where(first, low, high)
        both = ring[d + 1] + ring[d + 2]
        weight = rate * (mean / 6.0) - cube * (mean**3 / 6.0)
        fluxes.append(
            (rate * (0.5 * mean)) * (both - (rate * mean) * steps[d + 1]) - weight * bend
        )
    last = swap_halves(fluxes[HALF - 1])
    return [cells[d] - (fluxes[d] - (fluxes[d - 1] if d else last)) for d in range(HALF)]


def finish_groups(first, count, skip, par, base, gain, fix, ahead, turned, total):
    odd = lax.rem(lax.axis_index("band"), 2)
    tan_a, tan_b = wide_row(par, TAN_A), wide_row(par, TAN_B)

    def one_group(g, carry):
        speeds, weight, sum_a, sum_b = carry
        start = (skip + g) * GROUP_ROWS
        fix_start = (first + g) * GROUP_ROWS
        cells_a, cells_b = [], []
        for d in range(HALF):
            n1 = ahead[pl.ds(start + 2 * d + 1 - odd, 8, stride=ND), :]
            n2 = ahead[pl.ds(start + 2 * d + odd, 8, stride=ND), :]
            fix_a = fix[pl.ds(fix_start + 2 * d + odd, 8, stride=ND), :]
            fix_b = fix[pl.ds(fix_start + 2 * d + 1 - odd, 8, stride=ND), :]
            at = pl.multiple_of(g * (HALF * 16) + d * 16, 8)
            by = pl.multiple_of(g * (HALF * 24) + d * 24, 8)
            cells_a.append(
                base[pl.ds(at, 8), :]
                + fix_a
                + gain[pl.ds(by, 8), :] * n1
                + gain[pl.ds(by + 8, 8), :] * n2
            )
            cells_b.append(base[pl.ds(at + 8, 8), :] + fix_b + gain[pl.ds(by + 16, 8), :] * n1)
        square_a = square_b = 0.0
        for d, v in enumerate(turn(cells_a, speeds * tan_a)):
            at = pl.multiple_of(g * (HALF * 16) + d * 16, 8)
            turned[pl.ds(at, 8), :] = v
            square_a = square_a + v * v
        for d, v in enumerate(turn(cells_b, speeds * tan_b)):
            at = pl.multiple_of(g * (HALF * 16) + d * 16 + 8, 8)
            turned[pl.ds(at, 8), :] = v
            square_b = square_b + v * v
        return (
            speeds * FREQ_STEP**-GF,
            weight + GF / NF,
            sum_a + weight * square_a,
            sum_b + weight * square_b,
        )

    speeds = group_speed() * FREQ_STEP ** -(GF * first)
    weight = freq_weight() + GF * first / NF
    carry = (speeds, weight, total[0:8, :], total[8:16, :])
    _, _, total[0:8, :], total[8:16, :] = lax.fori_loop(0, count, one_group, carry)


def finish_either(bands, first, count, par, base, gain, fix, straight, split, turned, total):
    me = lax.axis_index("band")
    middle = jnp.logical_or(me == bands // 2 - 1, me == bands // 2)

    @pl.when(middle)
    def _():
        finish_groups(first, count, 0, par, base, gain, fix, split, turned, total)

    @pl.when(jnp.logical_not(middle))
    def _():
        finish_groups(first, count, first, par, base, gain, fix, straight, turned, total)


def first_kernel(bands, par, base, gain, fix, straight, split, turned, total):
    total[...] = jnp.zeros((16, LANES), jnp.float32)
    finish_either(bands, 0, FIRST_GROUPS, par, base, gain, fix, straight, split, turned, total)


def last_kernel(
    bands, par, base, gain, fix, straight, split, done, before, result, turned, total, out, sems
):
    odd = lax.rem(lax.axis_index("band"), 2)
    later = GROUPS - FIRST_GROUPS
    total[...] = before[...]
    finish_either(bands, FIRST_GROUPS, later, par, base, gain, fix, straight, split, turned, total)
    scale = 2.0 / (NF * ND)
    steep_a = jnp.sum(total[0:8, :], axis=0, keepdims=True) * scale
    steep_b = jnp.sum(total[8:16, :], axis=0, keepdims=True) * scale
    sea_a, sea_b = wide_row(par, SEA_A), wide_row(par, SEA_B)
    w0_a, w0_b = wide_row(par, W0_A), wide_row(par, W0_B)
    w1_a, w1_b = wide_row(par, W1_A), wide_row(par, W1_B)

    def copy_out(g):
        rows = pl.ds(pl.multiple_of(g * GROUP_ROWS, 8), GROUP_ROWS)
        return pltpu.make_async_copy(out.at[rows], result.at[rows], sems.at[g])

    def one_group(first, ref, g, carry):
        coupling, weight = carry
        start = (first + g) * GROUP_ROWS
        gain_a = sea_a / (1.0 + weight * steep_a)
        gain_b = sea_b / (1.0 + weight * steep_b)
        wa0, wa1 = w0_a * coupling, w1_a * coupling
        wb0, wb1 = w0_b * coupling, w1_b * coupling
        for d in range(HALF):
            at = pl.multiple_of(g * (HALF * 16) + d * 16, 8)
            growth_a = jnp.maximum(wa0 * COS[d] + wa1 * SIN[d] + (1.0 - GROWTH), 1.0)
            growth_b = jnp.maximum(wb0 * COS[d] + wb1 * SIN[d] + (1.0 - GROWTH), 1.0)
            out[pl.ds(start + 2 * d + odd, 8, stride=ND), :] = (
                ref[pl.ds(at, 8), :] * gain_a * growth_a
            )
            out[pl.ds(start + 2 * d + 1 - odd, 8, stride=ND), :] = (
                ref[pl.ds(at + 8, 8), :] * gain_b * growth_b
            )
        copy_out(first + g).start()
        return coupling * FREQ_STEP**GF, weight + GF / NF

    k = lax.broadcasted_iota(jnp.int32, (8, LANES), 0)
    coupling = jnp.zeros((8, LANES), jnp.float32)
    for i in range(GF):
        for h in range(2):
            value = GROWTH * WIND_COUPLING * FREQ_STEP**i * (1.0 - 2.0 * h)
            coupling = jnp.where(k == 2 * i + h, value, coupling)
    carry = (coupling, freq_weight())
    carry = lax.fori_loop(0, FIRST_GROUPS, functools.partial(one_group, 0, done), carry)
    lax.fori_loop(0, later, functools.partial(one_group, FIRST_GROUPS, turned), carry)
    for g in range(GROUPS):
        copy_out(g).wait()


def geometry_table(bands):
    total = 2 * bands

    def angle(position):
        return (LAT_SOUTH + (LAT_NORTH - LAT_SOUTH) * position / total) * (math.pi / 180.0)

    table = np.zeros((bands, 8), np.float32)
    for b in range(bands):
        cells = [angle(2 * b + 0.5), angle(2 * b + 1.5)]
        faces = [angle(2 * b), angle(2 * b + 1), angle(2 * b + 2)]
        icos = [1.0 / math.cos(v) for v in cells]
        near, far = (0, 1) if b % 2 == 0 else (1, 0)
        face_a, face_b = (faces[0], faces[2]) if b % 2 == 0 else (faces[2], faces[0])
        table[b] = [
            icos[0],
            icos[1],
            math.cos(face_a) * icos[near],
            math.cos(faces[1]) * icos[near],
            math.cos(faces[1]) * icos[far],
            math.cos(face_b) * icos[far],
            -TURNING * math.tan(cells[near]),
            -TURNING * math.tan(cells[far]),
        ]
    return table


def speed_table():
    table = np.zeros((2, WIDE), np.float32)
    for k in range(NF * ND):
        value = SPEED_TOP * FREQ_STEP ** -(k // ND) * math.cos(2.0 * math.pi * (k % ND) / ND)
        table[0, 2 * k] = value
        table[1, 2 * k + 1] = value
    return table


VMEM = pl.BlockSpec(memory_space=pltpu.VMEM)
SMEM = pl.BlockSpec(memory_space=pltpu.SMEM)
HBM = pl.BlockSpec(memory_space=pltpu.HBM)
ANY = pl.BlockSpec(memory_space=pl.ANY)
PARAMS = pltpu.CompilerParams(vmem_limit_bytes=40 * 1024 * 1024)


def call(kernel, name, operands, specs, shapes, scratch, micros, outs_in=None, flops=0):
    outs = [jax.ShapeDtypeStruct(s, jnp.float32) for s in shapes]
    return pl.pallas_call(
        kernel,
        name=name,
        out_shape=outs,
        in_specs=specs,
        out_specs=[outs_in or VMEM] * len(outs),
        scratch_shapes=scratch,
        compiler_params=PARAMS,
        cost_estimate=pl.CostEstimate(
            flops=flops, bytes_accessed=int(micros * 3.0e6), transcendentals=0
        ),
    )(*operands)


def swapped(pairs):
    return pairs + [(t, s) for s, t in pairs]


def per_device(bands, spec_count, spectra, sea_mask, wind, current):
    comp_count, row_count, col_count = spectra.shape
    cells = spectra.reshape(comp_count * row_count, col_count)
    middle = bands // 2 - 1
    first_rows = FIRST_GROUPS * GROUP_ROWS
    last_rows = ROWS - first_rows

    (own,) = call(
        pack_kernel,
        "pack_forcing",
        tuple(pltpu.with_memory_space_constraint(v, pltpu.HBM) for v in (wind, current, sea_mask)),
        [HBM] * 3,
        [(16, LANES)],
        [
            pltpu.VMEM(wind.shape, jnp.float32),
            pltpu.VMEM(current.shape, jnp.float32),
            pltpu.VMEM(sea_mask.shape, jnp.int32),
            pltpu.SemaphoreType.DMA((3,)),
        ],
        0.3,
    )
    order = [0]

    def gathered(values, bit):
        order.extend([r ^ bit for r in order])
        other = lax.ppermute(values, "band", [(b, b ^ bit) for b in range(bands)])
        return jnp.concatenate([values, other], axis=0)

    forcing = gathered(own, 2)

    part_relayed, part_direct = call(
        split_kernel,
        "split",
        (pltpu.with_memory_space_constraint(cells, pltpu.HBM), own),
        [HBM, VMEM],
        [(first_rows, LANES), (last_rows, LANES)],
        [pltpu.SemaphoreType.DMA((2,))],
        1.0,
    )
    part_relayed, forcing, ends_sea = lax.optimization_barrier((part_relayed, forcing, sea_mask))
    straight = lax.ppermute(
        cells, "band", swapped([(b, b + 1) for b in range(1, bands - 1, 2) if b != middle])
    )
    west, east = call(
        ends_kernel,
        "ends",
        (cells, ends_sea),
        [VMEM] * 2,
        [(2, WIDE), (2, WIDE)],
        [pltpu.VMEM((LANES, LANES), jnp.float32)],
        1.0,
    )
    part_relayed, west, east = lax.optimization_barrier((part_relayed, west, east))
    relay = lax.ppermute(part_relayed, "band", [(middle, bands - 1), (middle + 1, 0)])
    bit = 4
    while bit < bands:
        forcing = gathered(forcing, bit)
        bit *= 2
    part_relayed, part_direct, forcing, west, east = lax.optimization_barrier(
        (part_relayed, part_direct, forcing, west, east)
    )
    pairs = [(b, b + 1) for b in range(0, bands, 2)]
    forcing = gathered(forcing, 1)
    beyond = [lax.ppermute(part, "band", swapped(pairs)) for part in (part_relayed, part_direct)]
    direct = lax.ppermute(
        part_direct, "band", [(middle, middle + 1), (middle + 1, middle)]
    )

    par, first_here, second_here = call(
        functools.partial(table_kernel, bands, tuple(order)),
        "tables",
        (jnp.asarray(geometry_table(bands)), forcing, west, east),
        [SMEM, VMEM, VMEM, VMEM],
        [(PAR_ROWS, LANES), (2, WIDE), (2, WIDE)],
        [pltpu.VMEM((8 * bands, LANES), jnp.float32)],
        0.3,
        flops=4300000000,
    )
    relay, par = lax.optimization_barrier((relay, par))
    relayed = lax.ppermute(relay, "band", [(bands - 1, middle + 1), (0, middle)])
    ring = [(s, (s + 1) % spec_count) for s in range(spec_count)]
    first_there = lax.ppermute(first_here, "spec", swapped(ring[1::2]))
    second_there = lax.ppermute(second_here, "spec", swapped(ring[0::2]))
    base_first, base_last, gain_first, gain_last = call(
        base_kernel,
        "base",
        (par, cells, *beyond),
        [VMEM] * 4,
        [
            (first_rows, LANES),
            (last_rows, LANES),
            (first_rows * 3 // 2, LANES),
            (last_rows * 3 // 2, LANES),
        ],
        [],
        4.0,
    )
    base_first, first_there, second_there = lax.optimization_barrier(
        (base_first, first_there, second_there)
    )
    (fix,) = call(
        fix_kernel,
        "fix",
        (jnp.asarray(speed_table()), par, first_here, second_here, first_there, second_there),
        [VMEM] * 6,
        [(WIDE, LANES)],
        [pltpu.VMEM((LANES, WIDE), jnp.float32)],
        1.0,
    )
    turned, total = call(
        functools.partial(first_kernel, bands),
        "first_groups",
        (par, base_first, gain_first, fix, straight, relayed),
        [VMEM] * 6,
        [(first_rows, LANES), (16, LANES)],
        [],
        1.0,
    )
    (out,) = call(
        functools.partial(last_kernel, bands),
        "last_groups",
        (par, base_last, gain_last, fix, straight, direct, turned, total),
        [VMEM] * 8,
        [(ROWS, LANES)],
        [
            pltpu.VMEM((last_rows, LANES), jnp.float32),
            pltpu.VMEM((16, LANES), jnp.float32),
            pltpu.VMEM((ROWS, LANES), jnp.float32),
            pltpu.SemaphoreType.DMA((GROUPS,)),
        ],
        2.0,
        outs_in=ANY,
    )
    return out.reshape(comp_count, row_count, col_count)


def solution(mesh):
    placed = (
        P(None, "band", "spec"),
        P("band", "spec"),
        P(None, None, ("spec", "band")),
        P(None, None, ("spec", "band")),
    )
    return jax.shard_map(
        functools.partial(per_device, mesh.shape["band"], mesh.shape["spec"]),
        mesh=mesh,
        in_specs=placed,
        out_specs=P(None, "band", "spec"),
        check_vma=False,
    )
```
